32 devices in a mesh: gx: 4 (over x, core), gy: 8 (over z, y).
Axes of the slice: x: 2, y: 2, z: 4, core: 2. Of those that a mesh axis runs over, the one named last changes fastest.
Arguments:
- plate_motion: bfloat16 [8, 16, 128, 2, 128], P('gx', 'gy'), may hold values from -6 to 6
- adjoint_load: bfloat16 [8, 16, 128, 2, 128], P('gx', 'gy'), may hold values from -6 to 6
- excitation: bfloat16 [8, 16, 128, 2, 128], P('gx', 'gy'), may hold values from -6 to 6
- coupling: bfloat16 [8, 16, 5, 2, 128, 128], P('gx', 'gy'), may hold values from -0.25 to 0.25
- joints: int32 [8, 16, 4], P('gx', 'gy'), may hold values 0 or 1
- hydro: bfloat16 [2, 1024, 1024], P(None, 'gx', 'gy'), may hold values from -0.1875 to 0.1875
- panel_map: bfloat16 [1024, 2, 2, 128], P(('gx', 'gy')), may hold values from -0.25 to 0.25
Outputs:
- residual: float32 [8, 16, 128, 2, 128], P('gx', 'gy')
- multiplier: float32 [8, 16, 128, 2, 128], P('gx', 'gy')
- sensitivity: float32 [8, 16], P('gx', 'gy')
The draws below stay inside these ranges and needn't reach their ends.
All inputs are finite; a program needn't handle non-finite values. No bound on the sum of `joints` on one device may be relied on, other than what follows from the above.
Results may differ from the reference program's by a relative error of at most 0.0031.
Values may be sent and summed in bfloat16 or wider, within the bound.
No kernel may reach another device: no remote copies, remote signals or barrier semaphores. Data moves between devices by JAX's collectives and lax.ppermute only.
A program may use at most 64 MiB of HBM per device.

```python
import math
import jax
import jax.numpy as jnp
from jax import lax

NDOF = 128
BX = 2
BY = 2
NH = 128
PD = 32
GBX = 8
GBY = 16
NP = 1024
N_GX = 4
N_GY = 8
DEVICES = 32


def with_ends(entries, rng, least, high):
    longest = entries.shape.index(max(entries.shape))
    spots = []
    for shift in (0, 1):
        where = [jax.random.randint(jax.random.fold_in(rng, axis), (), 0, length) for axis, length in enumerate(entries.shape)]
        where[longest] = (where[longest] + shift) % entries.shape[longest]
        spots.append(tuple(where))
    return entries.at[spots[0]].set(least).at[spots[1]].set(high)


def levels(key, extent, shards, least, top_value):
    loudness = 1.0
    for axis_at, parts in shards:
        draws = jax.random.uniform(jax.random.fold_in(jax.random.fold_in(key, 6), axis_at), (parts,), jnp.float32, least / len(shards), top_value / len(shards))
        loudness = loudness * jnp.repeat(jnp.exp(draws), extent[axis_at] // parts).reshape((-1,) + (1,) * (len(extent) - 1 - axis_at))
    return loudness


def normal_values(rng, extent, deviation, most, split=(), kind=jnp.bfloat16):
    loudness = levels(rng, extent, split, -0.22, 0.18) if split else 1.0
    values = jax.random.normal(rng, extent, jnp.float32) * deviation * loudness
    return jnp.minimum(jnp.maximum(values, -most), most).astype(kind)


def setup_inputs(seed: int = 0) -> dict:
    splits = jax.random.split(jax.random.key(seed), 8)
    return {
        "plate_motion": normal_values(splits[0], (GBX, GBY, NH, 2, NDOF), 1.0, 6.0, ((0, 4), (1, 8))),
        "adjoint_load": normal_values(splits[1], (GBX, GBY, NH, 2, NDOF), 1.0, 6.0, ((0, 4), (1, 8))),
        "excitation": normal_values(splits[2], (GBX, GBY, NH, 2, NDOF), 1.0, 6.0, ((0, 4), (1, 8))),
        "coupling": normal_values(splits[3], (GBX, GBY, 5, 2, NDOF, NDOF), (5 * NDOF) ** -0.5, 0.25, ((0, 4), (1, 8))),
        "joints": with_ends((jax.random.randint(splits[4], (GBX, GBY, 4), 0, 4) < 3).astype(jnp.int32), jax.random.fold_in(splits[4], 1), 0, 1),
        "hydro": normal_values(splits[5], (2, NP, NP), NP ** -0.5, 0.1875, ((1, 4), (2, 8))),
        "panel_map": normal_values(splits[6], (NP, BX, BY, NDOF), (BX * BY * NDOF) ** -0.5, 0.25, ((0, 32),)),
    }


def complex_apply(form, coupling, vector):
    real_c = coupling[..., 0, :, :].astype(jnp.float32)
    imag_c = coupling[..., 1, :, :].astype(jnp.float32)
    real_v = vector[..., 0, :].astype(jnp.float32)
    imag_v = vector[..., 1, :].astype(jnp.float32)
    first = jnp.einsum(form, real_c, real_v) - jnp.einsum(form, imag_c, imag_v)
    second = jnp.einsum(form, real_c, imag_v) + jnp.einsum(form, imag_c, real_v)
    return jnp.stack([first, second], axis=-2)

def adjoint_apply(form, coupling, vector):
    real_c = coupling[..., 0, :, :].astype(jnp.float32)
    imag_c = coupling[..., 1, :, :].astype(jnp.float32)
    real_v = vector[..., 0, :].astype(jnp.float32)
    imag_v = vector[..., 1, :].astype(jnp.float32)
    first = jnp.einsum(form, real_c, real_v) + jnp.einsum(form, imag_c, imag_v)
    second = jnp.einsum(form, real_c, imag_v) - jnp.einsum(form, imag_c, real_v)
    return jnp.stack([first, second], axis=-2)

def neighbour(field, off_x, off_y):
    widths = ((1, 1), (1, 1)) + ((0, 0),) * (field.ndim - 2)
    padded = jnp.pad(field, widths)
    return padded[1 + off_x:1 + off_x + GBX, 1 + off_y:1 + off_y + GBY]

def to_tiles(field):
    rest = field.shape[2:]
    shaped = field.reshape((N_GX, BX, N_GY, BY) + rest).swapaxes(1, 2)
    return shaped.reshape((DEVICES, BX, BY) + rest)

def from_tiles(field):
    rest = field.shape[3:]
    shaped = field.reshape((N_GX, N_GY, BX, BY) + rest).swapaxes(1, 2)
    return shaped.reshape((GBX, GBY) + rest)

def reference(plate_motion, adjoint_load, excitation, coupling, joints, hydro, panel_map):
    offsets = ((-1, 0), (1, 0), (0, -1), (0, 1))
    links = joints.astype(jnp.float32)
    own = complex_apply('xyij,xyhj->xyhi', coupling[:, :, 0], plate_motion)
    structural = own
    for direction in range(4):
        moved = neighbour(plate_motion, offsets[direction][0], offsets[direction][1])
        term = complex_apply('xyij,xyhj->xyhi', coupling[:, :, direction + 1], moved)
        structural = structural + links[:, :, direction, None, None, None] * term
    adjoint_part = adjoint_apply('xyji,xyhj->xyhi', coupling[:, :, 0], adjoint_load)
    for direction in range(4):
        term = adjoint_apply('xyji,xyhj->xyhi', coupling[:, :, direction + 1], adjoint_load)
        term = links[:, :, direction, None, None, None] * term
        adjoint_part = adjoint_part + neighbour(term, -offsets[direction][0], -offsets[direction][1])
    lift = math.sqrt(BX * BY * NDOF / PD)
    map_tiles = panel_map.reshape(DEVICES, PD, BX, BY, NDOF).astype(jnp.float32)
    motion_panels = jnp.einsum('dnxyk,dxyhck->cdnh', map_tiles, to_tiles(plate_motion).astype(jnp.float32))
    motion_panels = motion_panels.astype(jnp.bfloat16).reshape(2, NP, NH)
    load_panels = jnp.einsum('dnxyk,dxyhck->cdnh', map_tiles, to_tiles(adjoint_load).astype(jnp.float32))
    load_panels = load_panels.astype(jnp.bfloat16).reshape(2, NP, NH)
    column_order = motion_panels.reshape(2, N_GX, N_GY, PD, NH).swapaxes(1, 2).reshape(2, NP, NH)
    band = N_GY * PD

    def band_matrix(index):
        return lax.dynamic_slice_in_dim(hydro, index * band, band, 1)

    def band_forward(index):
        masked = band_matrix(index)
        first = jnp.dot(masked[0], column_order[0], preferred_element_type=jnp.float32) - jnp.dot(masked[1], column_order[1], preferred_element_type=jnp.float32)
        second = jnp.dot(masked[0], column_order[1], preferred_element_type=jnp.float32) + jnp.dot(masked[1], column_order[0], preferred_element_type=jnp.float32)
        return jnp.stack([first, second])
    indices = jnp.arange(N_GX).astype(jnp.int32)
    pressure = lax.map(band_forward, indices).transpose(1, 0, 2, 3).reshape(2, NP, NH).astype(jnp.bfloat16)

    def band_adjoint(carry, index):
        masked = band_matrix(index)
        loads = lax.dynamic_slice_in_dim(load_panels, index * band, band, 1)
        first = jnp.dot(masked[0].T, loads[0], preferred_element_type=jnp.float32) + jnp.dot(masked[1].T, loads[1], preferred_element_type=jnp.float32)
        second = jnp.dot(masked[0].T, loads[1], preferred_element_type=jnp.float32) - jnp.dot(masked[1].T, loads[0], preferred_element_type=jnp.float32)
        return (carry + jnp.stack([first, second]), None)
    reaction, unused = lax.scan(band_adjoint, jnp.zeros((2, NP, NH), jnp.float32), indices)
    reaction = reaction.reshape(2, N_GY, N_GX, PD, NH).swapaxes(1, 2).reshape(2, NP, NH).astype(jnp.bfloat16)
    pressure_force = jnp.einsum('dnxyk,cdnh->dxyhck', map_tiles, pressure.reshape(2, DEVICES, PD, NH).astype(jnp.float32))
    reaction_force = jnp.einsum('dnxyk,cdnh->dxyhck', map_tiles, reaction.reshape(2, DEVICES, PD, NH).astype(jnp.float32))
    residual = structural + lift * from_tiles(pressure_force) - excitation.astype(jnp.float32)
    multiplier = adjoint_part + lift * from_tiles(reaction_force)
    sensitivity = lax.optimization_barrier(jnp.sum(multiplier * own, axis=(2, 3, 4))) / math.sqrt(NH * NDOF)
    return (residual, multiplier, sensitivity)
```

```python
import functools
import math

import jax
import jax.numpy as jnp
from jax import lax
from jax.experimental import pallas as pl
from jax.experimental.pallas import tpu as pltpu
from jax.sharding import PartitionSpec as P


F32 = jnp.float32
BF16 = jnp.bfloat16
OFFSETS = ((-1, 0), (1, 0), (0, -1), (0, 1))
WHOLE = pl.BlockSpec(memory_space=pltpu.VMEM)
SCALARS = pl.BlockSpec(memory_space=pltpu.SMEM)
FAR = pl.BlockSpec(memory_space=pltpu.HBM)


def dot(a, b, over):
    return lax.dot_general(a, b, ((over[:1], over[1:]), ((), ())), preferred_element_type=F32)


def times_i(field, axis):
    size = field.shape[axis]
    after = pltpu.roll(field, size - 1, axis)
    before = pltpu.roll(field, 1, axis)
    place = lax.broadcasted_iota(jnp.int32, field.shape, axis)
    return jnp.where(lax.rem(place, 2) == 0, -after, before)


def forward_parts(coupling, motion):
    return dot(motion, coupling.reshape(-1, coupling.shape[-1]), (1, 1))


def adjoint_parts(coupling, load):
    return dot(load, jnp.concatenate([coupling[0], coupling[1]], axis=1), (1, 0))


def joined(parts, sign):
    half = parts.shape[1] // 2
    turned = times_i(parts[:, half:], 0)
    return parts[:, :half] + turned if sign > 0 else parts[:, :half] - turned


def map_of_blocks(map_ref, blocks):
    rows = map_ref.shape[0]
    panels = rows // blocks
    row = lax.broadcasted_iota(jnp.int32, (panels, rows), 0)
    column = lax.broadcasted_iota(jnp.int32, (panels, rows), 1)
    whole = map_ref[...]
    out = []
    for b in range(blocks):
        pick = (column == row * blocks + b).astype(F32).astype(BF16)
        out.append(dot(pick, whole, (1, 0)).astype(BF16))
    return out


def target(i, step, n):
    if step == 0:
        return i
    if step == 1:
        return i ^ 1
    if step == 2:
        return (((i + 1) ^ 1) + n - 1) % n
    return (i + step - 1) % n


def source(i, step, n):
    return target(i, step, n) if step < 3 else (i + n + 1 - step) % n


def exchange(x, step):
    n = lax.axis_size("gx")
    return lax.ppermute(x, "gx", [(i, target(i, step, n)) for i in range(n)])


def panels_kernel(motion_far, load_far, map_far, motion_out, load_out, motion, load, maps, panels, arrive, leave):
    blocks = motion.shape[0]
    moves = [
        pltpu.make_async_copy(map_far, maps, arrive.at[0]),
        pltpu.make_async_copy(load_far, load, arrive.at[1]),
        pltpu.make_async_copy(motion_far, motion, arrive.at[2]),
    ]
    for move in moves:
        move.start()
    moves[0].wait()
    split = map_of_blocks(maps, blocks)
    moves[1].wait()
    panels[...] = sum(dot(split[b], load[b], (1, 1)) for b in range(blocks)).astype(BF16)
    outs = [pltpu.make_async_copy(panels, load_out.at[j], leave.at[j]) for j in range(load_out.shape[0])]
    for out in outs:
        out.start()
    moves[2].wait()
    motion_out[...] = sum(dot(split[b], motion[b], (1, 1)) for b in range(blocks)).astype(BF16)
    for out in outs:
        out.wait()


def edges(rows, cols, me):
    even = 1 - me % 2
    sides = []
    for d in (even, 1 - even):
        sides.append([(d * (rows - 1), y, d) for y in range(cols)])
    for d in (2, 3):
        sides.append([(x, (d - 2) * (cols - 1), d) for x in range(rows)])
    return sides


def edges_kernel(rows, cols, spot, joints, panels, motion_far, load_far, coupling_far, *refs):
    outs, (load, coupling, terms, arrive, pass_by, leave) = refs[:4], refs[4:]
    wide = load.shape[1]
    sides = edges(rows, cols, spot[0])
    spots = [(o, k) + place for o, side in enumerate(sides) for k, place in enumerate(side)]
    fetch = [pltpu.make_async_copy(load_far, load, arrive.at[len(spots)])]
    for i, (o, k, x, y, d) in enumerate(spots):
        fetch.append(pltpu.make_async_copy(coupling_far.at[x * cols + y, d + 1], coupling.at[i], arrive.at[i]))
    for move in fetch:
        move.start()
    direct = []
    for i, (o, k, x, y, d) in enumerate(spots):
        there = outs[o].at[pl.ds(k * wide, wide)]
        direct.append(pltpu.make_async_copy(motion_far.at[x * cols + y], there, pass_by.at[i]))
    size = panels.shape[0]
    for o in range(2):
        for h in range(wide // load.shape[2]):
            i = len(direct)
            there = outs[o].at[pl.ds(2 * len(sides[o]) * wide + h * size, size)]
            here = panels.at[:, pl.ds(h * load.shape[2], load.shape[2])]
            direct.append(pltpu.make_async_copy(here, there, pass_by.at[i]))
    for move in direct:
        move.start()
    fetch[0].wait()
    final = []
    for i, (o, k, x, y, d) in enumerate(spots):
        fetch[i + 1].wait()
        link = joints[x, y, d].astype(F32)
        term = joined(adjoint_parts(coupling[i], load[x * cols + y]), -1)
        terms[i] = (link * term).astype(BF16)
        there = outs[o].at[pl.ds((len(sides[o]) + k) * wide, wide)]
        final.append(pltpu.make_async_copy(terms.at[i], there, leave.at[i]))
        final[-1].start()
    for move in direct + final:
        move.wait()


def hydro_kernel(n_gx, spot, hydro_ref, loads_ref, *refs):
    pieces, (pressure_out, *reaction_outs, gathered, pressures, reacted, leave) = refs[:n_gx], refs[n_gx:]
    me = spot[0]
    panels, wide = pieces[0].shape
    for step in range(n_gx):
        start = pl.multiple_of(source(me, step, n_gx) * panels, panels)
        if step in (1, 2):
            narrow = pieces[step].shape[1]
            top = pieces[step].shape[0] - panels * wide // narrow
            for h in range(wide // narrow):
                part = pieces[step][pl.ds(top + h * panels, panels), :]
                gathered[pl.ds(start, panels), pl.ds(h * narrow, narrow)] = part
        else:
            gathered[pl.ds(start, panels), :] = pieces[step][...]
    hydro = hydro_ref[...]
    size, depth = hydro.shape[1:]
    both = dot(hydro.reshape(2 * size, depth), gathered[...], (1, 0))
    pressure = both[:size] + times_i(both[size:], 1)
    pressures[...] = pressure.astype(BF16).reshape(pressures.shape)
    out = pltpu.make_async_copy(pressures, pressure_out, leave)
    out.start()
    loads = loads_ref[...].reshape(size, -1)
    real = dot(hydro[0], loads, (0, 0))
    imag = dot(hydro[1], loads, (0, 0))
    reacted[...] = real - times_i(imag, 1)
    for step in range(n_gx):
        start = pl.multiple_of(target(me, step, n_gx) * panels, panels)
        reaction_outs[step][...] = reacted[pl.ds(start, panels), :]
    out.wait()


def local_kernel(rows, cols, n_gx, spot, joints, motion, load, excitation, coupling, *refs):
    first, second, before, after, residual_out, multiplier_out, own_out = refs
    wide = motion.shape[1]
    me = spot[0]
    even = me % 2 == 0
    valid = [(me > 0).astype(F32), (me < n_gx - 1).astype(F32), 1.0, 1.0]

    def received(d, k, kind):
        count = cols if d < 2 else rows
        here = pl.ds((kind * count + k) * wide, wide)
        if d >= 2:
            return (before if d == 2 else after)[here, :]
        return jnp.where(even, (second if d == 0 else first)[here, :], (first if d == 0 else second)[here, :])

    for x in range(rows):
        for y in range(cols):
            b = x * cols + y
            own = joined(forward_parts(coupling[b, 0], motion[b]), 1)
            own_out[b] = own
            parts = None
            adjoint = adjoint_parts(coupling[b, 0], load[b])
            extra = None
            for d in range(4):
                nx, ny = x + OFFSETS[d][0], y + OFFSETS[d][1]
                link = joints[x, y, d].astype(F32)
                if 0 <= nx < rows and 0 <= ny < cols:
                    n = nx * cols + ny
                    beside = motion[n]
                    back = joints[nx, ny, d ^ 1].astype(F32)
                    adjoint = adjoint + back * adjoint_parts(coupling[n, (d ^ 1) + 1], load[n])
                else:
                    k = y if d < 2 else x
                    beside = received(d, k, 0)
                    link = link * valid[d]
                    term = received(d, k, 1).astype(F32) * valid[d]
                    extra = term if extra is None else extra + term
                part = link * forward_parts(coupling[b, d + 1], beside)
                parts = part if parts is None else parts + part
            residual_out[b] = own + joined(parts, 1) - excitation[b].astype(F32)
            multiplier = joined(adjoint, -1)
            multiplier_out[b] = multiplier if extra is None else multiplier + extra


def final_kernel(rows, cols, lift, map_ref, residual, multiplier, own, pressures, *refs):
    reactions, (residual_out, multiplier_out, sensitivity_out) = refs[:-3], refs[-3:]
    blocks = rows * cols
    maps = map_of_blocks(map_ref, blocks)
    pressure = jnp.sum(pressures[...].astype(F32), axis=0).astype(BF16)
    reaction = sum(r[...].astype(F32) for r in reactions).astype(BF16)
    scale = 1.0 / math.sqrt(own.shape[1] // 2 * own.shape[2])
    for x in range(rows):
        for y in range(cols):
            b = x * cols + y
            residual_out[b] = residual[b] + lift * dot(pressure, maps[b], (0, 0))
            full = multiplier[b] + lift * dot(reaction, maps[b], (0, 0))
            multiplier_out[b] = full
            sensitivity_out[x, y] = jnp.sum(full * own[b]) * scale


def cost(flops, bytes_accessed):
    return pl.CostEstimate(flops=int(flops), bytes_accessed=int(bytes_accessed), transcendentals=0)


def shaped(dtype, *shape):
    return jax.ShapeDtypeStruct(shape, dtype)


PARAMS = pltpu.CompilerParams(vmem_limit_bytes=40 * 1024 * 1024)
DMA = pltpu.SemaphoreType.DMA


def on_device(plate_motion, adjoint_load, excitation, coupling, joints, hydro, panel_map):
    rows, cols, cases, _, unknowns = plate_motion.shape
    panels = panel_map.shape[0]
    blocks, wide = rows * cols, 2 * cases
    n_gx, n_gy = lax.axis_size("gx"), lax.axis_size("gy")
    spot = lax.axis_index("gx").reshape(1)
    motion = plate_motion.reshape(blocks, wide, unknowns)
    load = adjoint_load.reshape(blocks, wide, unknowns)
    force = excitation.reshape(blocks, wide, unknowns)
    coupling = coupling.reshape(blocks, 5, 2, unknowns, unknowns)
    panel_map = panel_map.reshape(panels * blocks, unknowns)
    lift = math.sqrt(blocks * unknowns / panels)
    block_flops = 2 * wide * unknowns * unknowns * 2
    field = (blocks, wide, unknowns)

    motion_panels, load_copies = pl.pallas_call(
        panels_kernel,
        name="panels",
        out_shape=[shaped(BF16, panels, wide), shaped(BF16, n_gy, panels, wide)],
        in_specs=[FAR] * 3,
        out_specs=[WHOLE, FAR],
        scratch_shapes=[
            pltpu.VMEM(field, BF16),
            pltpu.VMEM(field, BF16),
            pltpu.VMEM(panel_map.shape, BF16),
            pltpu.VMEM((panels, wide), BF16),
            DMA((3,)),
            DMA((n_gy,)),
        ],
        compiler_params=PARAMS,
        cost_estimate=cost(4 * blocks * wide * unknowns * panels, 4 * blocks * wide * unknowns),
    )(motion, load, panel_map)
    loads = lax.all_to_all(load_copies, "gy", 0, 0, tiled=True)

    counts = [cols, cols, rows, rows]
    extra = panels * wide // unknowns
    lengths = [2 * c * wide + (extra if o < 2 else 0) for o, c in enumerate(counts)]
    payloads = pl.pallas_call(
        functools.partial(edges_kernel, rows, cols),
        name="edges",
        out_shape=[shaped(BF16, length, unknowns) for length in lengths],
        in_specs=[SCALARS, SCALARS, WHOLE] + [FAR] * 3,
        out_specs=[FAR] * 4,
        scratch_shapes=[
            pltpu.VMEM(field, BF16),
            pltpu.VMEM((sum(counts), 2, unknowns, unknowns), BF16),
            pltpu.VMEM((sum(counts), wide, unknowns), BF16),
            DMA((sum(counts) + 1,)),
            DMA((sum(counts) + 2 * (wide // unknowns),)),
            DMA((sum(counts),)),
        ],
        compiler_params=PARAMS,
        cost_estimate=cost(sum(counts) * block_flops, 4 * blocks * wide * unknowns + 20 * blocks * unknowns**2),
    )(spot, joints, motion_panels, motion, load, coupling)
    first, second = exchange(payloads[0], 1), exchange(payloads[1], 2)
    pieces = [motion_panels, first, second] + [exchange(motion_panels, step) for step in range(3, n_gx)]
    before = lax.ppermute(payloads[3], "gy", [(i, i + 1) for i in range(n_gy - 1)])
    after = lax.ppermute(payloads[2], "gy", [(i + 1, i) for i in range(n_gy - 1)])

    pressure_parts, *reaction_parts = pl.pallas_call(
        functools.partial(hydro_kernel, n_gx),
        name="hydro",
        out_shape=[shaped(BF16, n_gy, panels, wide)] + [shaped(F32, panels, wide)] * n_gx,
        in_specs=[SCALARS] + [WHOLE] * (2 + n_gx),
        out_specs=[FAR] + [WHOLE] * n_gx,
        scratch_shapes=[
            pltpu.VMEM((n_gx * panels, wide), BF16),
            pltpu.VMEM((n_gy, panels, wide), BF16),
            pltpu.VMEM((n_gx * panels, wide), F32),
            DMA,
        ],
        compiler_params=PARAMS,
        cost_estimate=cost(4 * hydro.size * wide, 2 * hydro.size),
    )(spot, hydro, loads, *pieces)
    pressures = lax.all_to_all(pressure_parts, "gy", 0, 0, tiled=True)
    reactions = [reaction_parts[0]] + [exchange(reaction_parts[step], step) for step in range(1, n_gx)]

    residual, multiplier, own = pl.pallas_call(
        functools.partial(local_kernel, rows, cols, n_gx),
        name="local",
        out_shape=[shaped(F32, *field)] * 3,
        in_specs=[SCALARS] * 2 + [WHOLE] * 8,
        out_specs=[WHOLE] * 3,
        compiler_params=PARAMS,
        cost_estimate=cost(10 * blocks * block_flops, 20 * blocks * unknowns**2 + 20 * blocks * wide * unknowns),
    )(spot, joints, motion, load, force, coupling, first, second, before, after)

    residual, multiplier, sensitivity = pl.pallas_call(
        functools.partial(final_kernel, rows, cols, lift),
        name="final",
        out_shape=[shaped(F32, *field), shaped(F32, *field), shaped(F32, rows, cols)],
        in_specs=[WHOLE] * (5 + n_gx),
        out_specs=[WHOLE, WHOLE, SCALARS],
        compiler_params=PARAMS,
        cost_estimate=cost(4 * blocks * wide * unknowns * panels, 20 * blocks * wide * unknowns),
    )(panel_map, residual, multiplier, own, pressures, *reactions)
    shape = plate_motion.shape
    return residual.reshape(shape), multiplier.reshape(shape), sensitivity


def solution(mesh):
    field = P("gx", "gy", None, None, None)
    placed = (
        field,
        field,
        field,
        P("gx", "gy", None, None, None, None),
        P("gx", "gy", None),
        P(None, "gx", "gy"),
        P(("gx", "gy"), None, None, None),
    )
    return jax.shard_map(on_device, mesh=mesh, in_specs=placed, out_specs=(field, field, P("gx", "gy")), check_vma=False)
```

```python
import functools
import math

import jax
import jax.numpy as jnp
from jax import lax
from jax.experimental import pallas as pl
from jax.experimental.pallas import tpu as pltpu
from jax.sharding import PartitionSpec as P


F32 = jnp.float32
BF16 = jnp.bfloat16
OFFSETS = ((-1, 0), (1, 0), (0, -1), (0, 1))
WHOLE = pl.BlockSpec(memory_space=pltpu.VMEM)
SCALARS = pl.BlockSpec(memory_space=pltpu.SMEM)
FAR = pl.BlockSpec(memory_space=pltpu.HBM)


def dot(a, b, over):
    return lax.dot_general(a, b, ((over[:1], over[1:]), ((), ())), preferred_element_type=F32)


def times_i(field, axis):
    size = field.shape[axis]
    after = pltpu.roll(field, size - 1, axis)
    before = pltpu.roll(field, 1, axis)
    place = lax.broadcasted_iota(jnp.int32, field.shape, axis)
    return jnp.where(lax.rem(place, 2) == 0, -after, before)


def forward_parts(coupling, motion):
    return dot(motion, coupling.reshape(-1, coupling.shape[-1]), (1, 1))


def adjoint_parts(coupling, load):
    return dot(load, jnp.concatenate([coupling[0], coupling[1]], axis=1), (1, 0))


def joined(parts, sign):
    half = parts.shape[1] // 2
    turned = times_i(parts[:, half:], 0)
    return parts[:, :half] + turned if sign > 0 else parts[:, :half] - turned


def map_of_blocks(map_ref, blocks):
    rows = map_ref.shape[0]
    panels = rows // blocks
    row = lax.broadcasted_iota(jnp.int32, (panels, rows), 0)
    column = lax.broadcasted_iota(jnp.int32, (panels, rows), 1)
    whole = map_ref[...]
    out = []
    for b in range(blocks):
        pick = (column == row * blocks + b).astype(F32).astype(BF16)
        out.append(dot(pick, whole, (1, 0)).astype(BF16))
    return out


def target(i, step, n):
    if step == 0:
        return i
    if step == 1:
        return i ^ 1
    if step == 2:
        return (((i + 1) ^ 1) + n - 1) % n
    return (i + step - 1) % n


def source(i, step, n):
    return target(i, step, n) if step < 3 else (i + n + 1 - step) % n


def exchange(x, step):
    n = lax.axis_size("gx")
    return lax.ppermute(x, "gx", [(i, target(i, step, n)) for i in range(n)])


def edges(rows, cols, me):
    even = 1 - me % 2
    sides = []
    for d in (even, 1 - even):
        sides.append([(d * (rows - 1), y, d) for y in range(cols)])
    for d in (2, 3):
        sides.append([(x, (d - 2) * (cols - 1), d) for x in range(rows)])
    return sides


def send_kernel(rows, cols, spot, joints, motion_far, load_far, coupling_far, map_far, *refs):
    load_out, motion_out, outs, refs = refs[0], refs[1], refs[2:6], refs[6:]
    motion, load, coupling, maps, motion_panels, load_panels, terms, arrive, pass_by, leave = refs
    blocks, wide, unknowns = motion.shape
    sides = edges(rows, cols, spot[0])
    spots = [(o, k) + place for o, side in enumerate(sides) for k, place in enumerate(side)]
    fetch = [
        pltpu.make_async_copy(map_far, maps, arrive.at[0]),
        pltpu.make_async_copy(load_far, load, arrive.at[1]),
        pltpu.make_async_copy(motion_far, motion, arrive.at[2]),
    ]
    for i, (o, k, x, y, d) in enumerate(spots):
        fetch.append(pltpu.make_async_copy(coupling_far.at[x * cols + y, d + 1], coupling.at[i], arrive.at[i + 3]))
    for move in fetch:
        move.start()
    fetch[0].wait()
    split = map_of_blocks(maps, blocks)
    fetch[1].wait()
    load_panels[...] = sum(dot(split[b], load[b], (1, 1)) for b in range(blocks)).astype(BF16)
    sent = [pltpu.make_async_copy(load_panels, load_out.at[j], leave.at[j]) for j in range(load_out.shape[0])]
    for move in sent:
        move.start()
    fetch[2].wait()
    for i, (o, k, x, y, d) in enumerate(spots):
        there = outs[o].at[pl.ds(k * wide, wide)]
        move = pltpu.make_async_copy(motion.at[x * cols + y], there, pass_by.at[i])
        move.start()
        sent.append(move)
    motion_panels[...] = sum(dot(split[b], motion[b], (1, 1)) for b in range(blocks)).astype(BF16)
    size, i = motion_panels.shape[0], len(spots)
    move = pltpu.make_async_copy(motion_panels, motion_out, pass_by.at[i])
    move.start()
    sent.append(move)
    for o in range(2):
        for h in range(wide // unknowns):
            i += 1
            there = outs[o].at[pl.ds(2 * len(sides[o]) * wide + h * size, size)]
            move = pltpu.make_async_copy(motion_panels.at[:, pl.ds(h * unknowns, unknowns)], there, pass_by.at[i])
            move.start()
            sent.append(move)
    for i, (o, k, x, y, d) in enumerate(spots):
        fetch[i + 3].wait()
        link = joints[x, y, d].astype(F32)
        term = joined(adjoint_parts(coupling[i], load[x * cols + y]), -1)
        terms[i] = (link * term).astype(BF16)
        there = outs[o].at[pl.ds((len(sides[o]) + k) * wide, wide)]
        move = pltpu.make_async_copy(terms.at[i], there, leave.at[load_out.shape[0] + i])
        move.start()
        sent.append(move)
    for move in sent:
        move.wait()


def hydro_kernel(n_gx, spot, hydro_ref, loads_ref, *refs):
    pieces, (pressure_out, *reaction_outs, gathered, pressures, reacted, leave) = refs[:n_gx], refs[n_gx:]
    outs = [pltpu.make_async_copy(pressures, pressure_out, leave.at[0])]
    me = spot[0]
    panels, wide = pieces[0].shape
    for step in range(n_gx):
        start = pl.multiple_of(source(me, step, n_gx) * panels, panels)
        if step in (1, 2):
            narrow = pieces[step].shape[1]
            top = pieces[step].shape[0] - panels * wide // narrow
            for h in range(wide // narrow):
                part = pieces[step][pl.ds(top + h * panels, panels), :]
                gathered[pl.ds(start, panels), pl.ds(h * narrow, narrow)] = part
        else:
            gathered[pl.ds(start, panels), :] = pieces[step][...]
    hydro = hydro_ref[...]
    size, depth = hydro.shape[1:]
    both = dot(hydro.reshape(2 * size, depth), gathered[...], (1, 0))
    pressure = both[:size] + times_i(both[size:], 1)
    pressures[...] = pressure.astype(BF16).reshape(pressures.shape)
    outs[0].start()
    loads = loads_ref[...].reshape(size, -1)
    real = dot(hydro[0], loads, (0, 0))
    imag = dot(hydro[1], loads, (0, 0))
    reacted[...] = real - times_i(imag, 1)
    for step in range(n_gx):
        start = pl.multiple_of(target(me, step, n_gx) * panels, panels)
        outs.append(pltpu.make_async_copy(reacted.at[pl.ds(start, panels)], reaction_outs[step], leave.at[step + 1]))
        outs[-1].start()
    for out in outs:
        out.wait()


def local_kernel(rows, cols, n_gx, spot, joints, motion, load, excitation, coupling, *refs):
    first, second, before, after, residual_out, multiplier_out, own_out = refs
    wide = motion.shape[1]
    me = spot[0]
    even = me % 2 == 0
    valid = [(me > 0).astype(F32), (me < n_gx - 1).astype(F32), 1.0, 1.0]

    def received(d, k, kind):
        count = cols if d < 2 else rows
        here = pl.ds((kind * count + k) * wide, wide)
        if d >= 2:
            return (before if d == 2 else after)[here, :]
        return jnp.where(even, (second if d == 0 else first)[here, :], (first if d == 0 else second)[here, :])

    for x in range(rows):
        for y in range(cols):
            b = x * cols + y
            own = joined(forward_parts(coupling[b, 0], motion[b]), 1)
            own_out[b] = own
            parts = None
            adjoint = adjoint_parts(coupling[b, 0], load[b])
            extra = None
            for d in range(4):
                nx, ny = x + OFFSETS[d][0], y + OFFSETS[d][1]
                link = joints[x, y, d].astype(F32)
                if 0 <= nx < rows and 0 <= ny < cols:
                    n = nx * cols + ny
                    beside = motion[n]
                    back = joints[nx, ny, d ^ 1].astype(F32)
                    adjoint = adjoint + back * adjoint_parts(coupling[n, (d ^ 1) + 1], load[n])
                else:
                    k = y if d < 2 else x
                    beside = received(d, k, 0)
                    link = link * valid[d]
                    term = received(d, k, 1).astype(F32) * valid[d]
                    extra = term if extra is None else extra + term
                part = link * forward_parts(coupling[b, d + 1], beside)
                parts = part if parts is None else parts + part
            residual_out[b] = own + joined(parts, 1) - excitation[b].astype(F32)
            multiplier = joined(adjoint, -1)
            multiplier_out[b] = multiplier if extra is None else multiplier + extra


def final_kernel(rows, cols, lift, map_ref, residual, multiplier, own, pressures, *refs):
    reactions, (residual_out, multiplier_out, sensitivity_out) = refs[:-3], refs[-3:]
    blocks = rows * cols
    maps = map_of_blocks(map_ref, blocks)
    pressure = jnp.sum(pressures[...].astype(F32), axis=0).astype(BF16)
    reaction = sum(r[...].astype(F32) for r in reactions).astype(BF16)
    scale = 1.0 / math.sqrt(own.shape[1] // 2 * own.shape[2])
    for x in range(rows):
        for y in range(cols):
            b = x * cols + y
            residual_out[b] = residual[b] + lift * dot(pressure, maps[b], (0, 0))
            full = multiplier[b] + lift * dot(reaction, maps[b], (0, 0))
            multiplier_out[b] = full
            sensitivity_out[x, y] = jnp.sum(full * own[b]) * scale


def cost(flops, bytes_accessed):
    return pl.CostEstimate(flops=int(flops), bytes_accessed=int(bytes_accessed), transcendentals=0)


def shaped(dtype, *shape):
    return jax.ShapeDtypeStruct(shape, dtype)


def params(mebibytes):
    return pltpu.CompilerParams(vmem_limit_bytes=mebibytes * 1024 * 1024)


DMA = pltpu.SemaphoreType.DMA


def on_device(plate_motion, adjoint_load, excitation, coupling, joints, hydro, panel_map):
    rows, cols, cases, _, unknowns = plate_motion.shape
    panels = panel_map.shape[0]
    blocks, wide = rows * cols, 2 * cases
    n_gx, n_gy = lax.axis_size("gx"), lax.axis_size("gy")
    spot = lax.axis_index("gx").reshape(1)
    motion = plate_motion.reshape(blocks, wide, unknowns)
    load = adjoint_load.reshape(blocks, wide, unknowns)
    force = excitation.reshape(blocks, wide, unknowns)
    coupling = coupling.reshape(blocks, 5, 2, unknowns, unknowns)
    panel_map = panel_map.reshape(panels * blocks, unknowns)
    lift = math.sqrt(blocks * unknowns / panels)
    block_flops = 2 * wide * unknowns * unknowns * 2
    field = (blocks, wide, unknowns)

    counts = [cols, cols, rows, rows]
    extra = panels * wide // unknowns
    lengths = [2 * c * wide + (extra if o < 2 else 0) for o, c in enumerate(counts)]
    load_copies, motion_panels, *payloads = pl.pallas_call(
        functools.partial(send_kernel, rows, cols),
        name="send",
        out_shape=[shaped(BF16, n_gy, panels, wide), shaped(BF16, panels, wide)]
        + [shaped(BF16, length, unknowns) for length in lengths],
        in_specs=[SCALARS, SCALARS] + [FAR] * 4,
        out_specs=[FAR] * 6,
        scratch_shapes=[
            pltpu.VMEM(field, BF16),
            pltpu.VMEM(field, BF16),
            pltpu.VMEM((sum(counts), 2, unknowns, unknowns), BF16),
            pltpu.VMEM(panel_map.shape, BF16),
            pltpu.VMEM((panels, wide), BF16),
            pltpu.VMEM((panels, wide), BF16),
            pltpu.VMEM((sum(counts), wide, unknowns), BF16),
            DMA((sum(counts) + 3,)),
            DMA((sum(counts) + 1 + 2 * (wide // unknowns),)),
            DMA((n_gy + sum(counts),)),
        ],
        compiler_params=params(60),
        cost_estimate=cost(sum(counts) * block_flops, 4 * blocks * wide * unknowns + 20 * blocks * unknowns**2),
    )(spot, joints, motion, load, coupling, panel_map)
    loads = lax.all_to_all(load_copies, "gy", 0, 0, tiled=True)
    first, second = exchange(payloads[0], 1), exchange(payloads[1], 2)
    pieces = [motion_panels, first, second] + [exchange(motion_panels, step) for step in range(3, n_gx)]
    before = lax.ppermute(payloads[3], "gy", [(i, i + 1) for i in range(n_gy - 1)])
    after = lax.ppermute(payloads[2], "gy", [(i + 1, i) for i in range(n_gy - 1)])

    pressure_parts, *reaction_parts = pl.pallas_call(
        functools.partial(hydro_kernel, n_gx),
        name="hydro",
        out_shape=[shaped(BF16, n_gy, panels, wide)] + [shaped(F32, panels, wide)] * n_gx,
        in_specs=[SCALARS] + [WHOLE] * (2 + n_gx),
        out_specs=[FAR] * (1 + n_gx),
        scratch_shapes=[
            pltpu.VMEM((n_gx * panels, wide), BF16),
            pltpu.VMEM((n_gy, panels, wide), BF16),
            pltpu.VMEM((n_gx * panels, wide), F32),
            DMA((n_gx + 1,)),
        ],
        compiler_params=params(16),
        cost_estimate=cost(4 * hydro.size * wide, 2 * hydro.size),
    )(spot, hydro, loads, *pieces)
    pressures = lax.all_to_all(pressure_parts, "gy", 0, 0, tiled=True)
    reactions = [reaction_parts[0]] + [exchange(reaction_parts[step], step) for step in range(1, n_gx)]

    residual, multiplier, own = pl.pallas_call(
        functools.partial(local_kernel, rows, cols, n_gx),
        name="local",
        out_shape=[shaped(F32, *field)] * 3,
        in_specs=[SCALARS] * 2 + [WHOLE] * 8,
        out_specs=[WHOLE] * 3,
        compiler_params=params(16),
        cost_estimate=cost(10 * blocks * block_flops, 20 * blocks * unknowns**2 + 20 * blocks * wide * unknowns),
    )(spot, joints, motion, load, force, coupling, first, second, before, after)

    residual, multiplier, sensitivity = pl.pallas_call(
        functools.partial(final_kernel, rows, cols, lift),
        name="final",
        out_shape=[shaped(F32, *field), shaped(F32, *field), shaped(F32, rows, cols)],
        in_specs=[WHOLE] * (5 + n_gx),
        out_specs=[WHOLE, WHOLE, SCALARS],
        compiler_params=params(16),
        cost_estimate=cost(4 * blocks * wide * unknowns * panels, 20 * blocks * wide * unknowns),
    )(panel_map, residual, multiplier, own, pressures, *reactions)
    shape = plate_motion.shape
    return residual.reshape(shape), multiplier.reshape(shape), sensitivity


def solution(mesh):
    field = P("gx", "gy", None, None, None)
    placed = (
        field,
        field,
        field,
        P("gx", "gy", None, None, None, None),
        P("gx", "gy", None),
        P(None, "gx", "gy"),
        P(("gx", "gy"), None, None, None),
    )
    return jax.shard_map(on_device, mesh=mesh, in_specs=placed, out_specs=(field, field, P("gx", "gy")), check_vma=False)
```

```python
import functools
import math

import jax
import jax.numpy as jnp
from jax import lax
from jax.experimental import pallas as pl
from jax.experimental.pallas import tpu as pltpu
from jax.sharding import PartitionSpec as P


F32 = jnp.float32
BF16 = jnp.bfloat16
OFFSETS = ((-1, 0), (1, 0), (0, -1), (0, 1))
WHOLE = pl.BlockSpec(memory_space=pltpu.VMEM)
SCALARS = pl.BlockSpec(memory_space=pltpu.SMEM)
FAR = pl.BlockSpec(memory_space=pltpu.HBM)


def dot(a, b, over):
    return lax.dot_general(a, b, ((over[:1], over[1:]), ((), ())), preferred_element_type=F32)


def times_i(field, axis):
    size = field.shape[axis]
    after = pltpu.roll(field, size - 1, axis)
    before = pltpu.roll(field, 1, axis)
    place = lax.broadcasted_iota(jnp.int32, field.shape, axis)
    return jnp.where(lax.rem(place, 2) == 0, -after, before)


def forward_parts(coupling, motion):
    return dot(motion, coupling.reshape(-1, coupling.shape[-1]), (1, 1))


def adjoint_parts(coupling, load):
    return dot(load, jnp.concatenate([coupling[0], coupling[1]], axis=1), (1, 0))


def joined(parts, sign):
    half = parts.shape[1] // 2
    turned = times_i(parts[:, half:], 0)
    return parts[:, :half] + turned if sign > 0 else parts[:, :half] - turned


def map_of_blocks(map_ref, blocks):
    rows = map_ref.shape[0]
    panels = rows // blocks
    row = lax.broadcasted_iota(jnp.int32, (panels, rows), 0)
    column = lax.broadcasted_iota(jnp.int32, (panels, rows), 1)
    whole = map_ref[...]
    out = []
    for b in range(blocks):
        pick = (column == row * blocks + b).astype(F32).astype(BF16)
        out.append(dot(pick, whole, (1, 0)).astype(BF16))
    return out


def target(i, step, n):
    if step == 0:
        return i
    if step == 1:
        return i ^ 1
    if step == 2:
        return (((i + 1) ^ 1) + n - 1) % n
    return (i + step - 1) % n


def source(i, step, n):
    return target(i, step, n) if step < 3 else (i + n + 1 - step) % n


def exchange(x, step, axis="gx", wrap=True):
    n = lax.axis_size(axis)
    pairs = [(i, target(i, step, n)) for i in range(n)]
    return lax.ppermute(x, axis, [(i, j) for i, j in pairs if wrap or abs(i - j) < n - 1 or n == 2])


def near(x):
    return pltpu.with_memory_space_constraint(x, pltpu.VMEM)


def far(x):
    return pltpu.with_memory_space_constraint(x, pltpu.HBM)


def edges(rows, cols, spot):
    sides = []
    for axis in range(2):
        even = 1 - spot[axis] % 2
        for up in (even, 1 - even):
            if axis == 0:
                sides.append([(up * (rows - 1), y, up) for y in range(cols)])
            else:
                sides.append([(x, up * (cols - 1), 2 + up) for x in range(rows)])
    return sides


def send_kernel(rows, cols, spot, joints, motion_far, load_far, coupling_far, map_far, *refs):
    load_out, motion_out, outs, refs = refs[0], refs[1], refs[2:6], refs[6:]
    motion, load, coupling, maps, load_panels, arrive, leave = refs
    blocks, wide, unknowns = motion.shape
    sides = edges(rows, cols, spot)
    spots = [(o, k) + place for o, side in enumerate(sides) for k, place in enumerate(side)]
    fetch = [
        pltpu.make_async_copy(map_far, maps, arrive.at[0]),
        pltpu.make_async_copy(load_far, load, arrive.at[1]),
        pltpu.make_async_copy(motion_far, motion, arrive.at[2]),
    ]
    for i, (o, k, x, y, d) in enumerate(spots):
        fetch.append(pltpu.make_async_copy(coupling_far.at[x * cols + y, d + 1], coupling.at[i], arrive.at[i + 3]))
    for move in fetch:
        move.start()
    fetch[0].wait()
    split = map_of_blocks(maps, blocks)
    fetch[1].wait()
    load_panels[...] = sum(dot(split[b], load[b], (1, 1)) for b in range(blocks)).astype(BF16)
    sent = [pltpu.make_async_copy(load_panels, load_out.at[j], leave.at[j]) for j in range(load_out.shape[0])]
    for move in sent:
        move.start()
    fetch[2].wait()
    panels = sum(dot(split[b], motion[b], (1, 1)) for b in range(blocks)).astype(BF16)
    motion_out[...] = panels
    for o in range(2):
        for h in range(wide // unknowns):
            top = 2 * len(sides[o]) * wide + h * panels.shape[0]
            outs[o][pl.ds(top, panels.shape[0]), :] = panels[:, h * unknowns : (h + 1) * unknowns]
    for i, (o, k, x, y, d) in enumerate(spots):
        outs[o][pl.ds(k * wide, wide), :] = motion[x * cols + y]
        fetch[i + 3].wait()
        link = joints[x, y, d].astype(F32)
        term = joined(adjoint_parts(coupling[i], load[x * cols + y]), -1)
        outs[o][pl.ds((len(sides[o]) + k) * wide, wide), :] = (link * term).astype(BF16)
    for move in sent:
        move.wait()


def hydro_kernel(n_gx, spot, hydro_ref, loads_ref, *refs):
    pieces, (pressure_out, *reaction_outs, gathered, pressures, reacted, leave) = refs[:n_gx], refs[n_gx:]
    outs = [pltpu.make_async_copy(pressures, pressure_out, leave)]
    me = spot[0]
    panels, wide = pieces[0].shape
    for step in range(n_gx):
        start = pl.multiple_of(source(me, step, n_gx) * panels, panels)
        if step in (1, 2):
            narrow = pieces[step].shape[1]
            top = pieces[step].shape[0] - panels * wide // narrow
            for h in range(wide // narrow):
                part = pieces[step][pl.ds(top + h * panels, panels), :]
                gathered[pl.ds(start, panels), pl.ds(h * narrow, narrow)] = part
        else:
            gathered[pl.ds(start, panels), :] = pieces[step][...]
    hydro = hydro_ref[...]
    size, depth = hydro.shape[1:]
    both = dot(hydro.reshape(2 * size, depth), gathered[...], (1, 0))
    pressure = both[:size] + times_i(both[size:], 1)
    pressures[...] = pressure.astype(BF16).reshape(pressures.shape)
    outs[0].start()
    loads = loads_ref[...].reshape(size, -1)
    real = dot(hydro[0], loads, (0, 0))
    imag = dot(hydro[1], loads, (0, 0))
    reacted[...] = real - times_i(imag, 1)
    for step in range(n_gx):
        start = pl.multiple_of(target(me, step, n_gx) * panels, panels)
        reaction_outs[step][...] = reacted[pl.ds(start, panels), :]
    outs[0].wait()


def local_kernel(rows, cols, sizes, spot, joints, motion_far, load_far, excitation_far, coupling_far, *refs):
    received_refs, (residual_out, multiplier_out, own_out), refs = refs[:4], refs[4:7], refs[7:]
    motion, load, excitation, coupling, arrive = refs
    moves = [
        pltpu.make_async_copy(motion_far, motion, arrive.at[0]),
        pltpu.make_async_copy(load_far, load, arrive.at[1]),
        pltpu.make_async_copy(coupling_far, coupling, arrive.at[2]),
        pltpu.make_async_copy(excitation_far, excitation, arrive.at[3]),
    ]
    for move in moves:
        move.start()
    wide = motion.shape[1]
    even = [spot[axis] % 2 == 0 for axis in range(2)]
    valid = []
    for axis in range(2):
        valid += [(spot[axis] > 0).astype(F32), (spot[axis] < sizes[axis] - 1).astype(F32)]

    def received(d, k, kind):
        count = cols if d < 2 else rows
        here = pl.ds((kind * count + k) * wide, wide)
        first, second = received_refs[d // 2 * 2], received_refs[d // 2 * 2 + 1]
        if d % 2:
            first, second = second, first
        return jnp.where(even[d // 2], second[here, :], first[here, :])

    for move in moves:
        move.wait()
    for x in range(rows):
        for y in range(cols):
            b = x * cols + y
            own = joined(forward_parts(coupling[b, 0], motion[b]), 1)
            own_out[b] = own
            parts = None
            adjoint = adjoint_parts(coupling[b, 0], load[b])
            extra = None
            for d in range(4):
                nx, ny = x + OFFSETS[d][0], y + OFFSETS[d][1]
                link = joints[x, y, d].astype(F32)
                if 0 <= nx < rows and 0 <= ny < cols:
                    n = nx * cols + ny
                    beside = motion[n]
                    back = joints[nx, ny, d ^ 1].astype(F32)
                    adjoint = adjoint + back * adjoint_parts(coupling[n, (d ^ 1) + 1], load[n])
                else:
                    k = y if d < 2 else x
                    beside = received(d, k, 0)
                    link = link * valid[d]
                    term = received(d, k, 1).astype(F32) * valid[d]
                    extra = term if extra is None else extra + term
                part = link * forward_parts(coupling[b, d + 1], beside)
                parts = part if parts is None else parts + part
            residual_out[b] = own + joined(parts, 1) - excitation[b].astype(F32)
            multiplier = joined(adjoint, -1)
            multiplier_out[b] = multiplier if extra is None else multiplier + extra


def final_kernel(rows, cols, lift, map_ref, residual, multiplier, own, pressures, *refs):
    reactions, (residual_out, multiplier_out, sensitivity_out, full, leave) = refs[:-5], refs[-5:]
    blocks = rows * cols
    maps = map_of_blocks(map_ref, blocks)
    pressure = jnp.sum(pressures[...].astype(F32), axis=0).astype(BF16)
    reaction = sum(r[...].astype(F32) for r in reactions).astype(BF16)
    scale = 1.0 / math.sqrt(own.shape[1] // 2 * own.shape[2])
    sent = []
    for b in range(blocks):
        full[0, b] = residual[b] + lift * dot(pressure, maps[b], (0, 0))
        sent.append(pltpu.make_async_copy(full.at[0, b], residual_out.at[b], leave.at[0, b]))
        sent[-1].start()
    for b in range(blocks):
        value = multiplier[b] + lift * dot(reaction, maps[b], (0, 0))
        full[1, b] = value
        sent.append(pltpu.make_async_copy(full.at[1, b], multiplier_out.at[b], leave.at[1, b]))
        sent[-1].start()
        sensitivity_out[b // cols, b % cols] = jnp.sum(value * own[b]) * scale
    for move in sent:
        move.wait()


def cost(flops, bytes_accessed):
    return pl.CostEstimate(flops=int(flops), bytes_accessed=int(bytes_accessed), transcendentals=0)


def shaped(dtype, *shape):
    return jax.ShapeDtypeStruct(shape, dtype)


def params(mebibytes):
    return pltpu.CompilerParams(vmem_limit_bytes=mebibytes * 1024 * 1024)


DMA = pltpu.SemaphoreType.DMA


def on_device(plate_motion, adjoint_load, excitation, coupling, joints, hydro, panel_map):
    rows, cols, cases, _, unknowns = plate_motion.shape
    panels = panel_map.shape[0]
    blocks, wide = rows * cols, 2 * cases
    n_gx, n_gy = lax.axis_size("gx"), lax.axis_size("gy")
    spot = jnp.stack([lax.axis_index("gx"), lax.axis_index("gy")])
    motion = plate_motion.reshape(blocks, wide, unknowns)
    load = adjoint_load.reshape(blocks, wide, unknowns)
    force = excitation.reshape(blocks, wide, unknowns)
    coupling = coupling.reshape(blocks, 5, 2, unknowns, unknowns)
    panel_map = panel_map.reshape(panels * blocks, unknowns)
    lift = math.sqrt(blocks * unknowns / panels)
    block_flops = 2 * wide * unknowns * unknowns * 2
    field = (blocks, wide, unknowns)

    counts = [cols, cols, rows, rows]
    extra = panels * wide // unknowns
    lengths = [2 * c * wide + (extra if o < 2 else 0) for o, c in enumerate(counts)]
    load_copies, motion_panels, *payloads = pl.pallas_call(
        functools.partial(send_kernel, rows, cols),
        name="send",
        out_shape=[pltpu.HBM((n_gy, panels, wide), BF16), pltpu.VMEM((panels, wide), BF16)]
        + [pltpu.VMEM((length, unknowns), BF16) for length in lengths],
        in_specs=[SCALARS, SCALARS] + [FAR] * 4,
        out_specs=[FAR] + [WHOLE] * 5,
        scratch_shapes=[
            pltpu.VMEM(field, BF16),
            pltpu.VMEM(field, BF16),
            pltpu.VMEM((sum(counts), 2, unknowns, unknowns), BF16),
            pltpu.VMEM(panel_map.shape, BF16),
            pltpu.VMEM((panels, wide), BF16),
            DMA((sum(counts) + 3,)),
            DMA((n_gy,)),
        ],
        compiler_params=params(16),
        cost_estimate=cost(sum(counts) * block_flops, 4 * blocks * wide * unknowns + 20 * blocks * unknowns**2),
    )(spot, joints, far(motion), far(load), far(coupling), far(panel_map))
    loads = lax.all_to_all(load_copies, "gy", 0, 0, tiled=True)
    further = [exchange(motion_panels, step) for step in range(3, n_gx)]
    (*payloads, further) = lax.optimization_barrier((*payloads, further))
    first, second = exchange(payloads[0], 1), exchange(payloads[1], 2)
    third, fourth = exchange(payloads[2], 1, "gy"), exchange(payloads[3], 2, "gy", wrap=False)
    pieces = [motion_panels, first, second] + further

    pressure_parts, *reaction_parts = pl.pallas_call(
        functools.partial(hydro_kernel, n_gx),
        name="hydro",
        out_shape=[pltpu.HBM((n_gy, panels, wide), BF16)] + [pltpu.VMEM((panels, wide), F32)] * n_gx,
        in_specs=[SCALARS] + [WHOLE] * (2 + n_gx),
        out_specs=[FAR] + [WHOLE] * n_gx,
        scratch_shapes=[
            pltpu.VMEM((n_gx * panels, wide), BF16),
            pltpu.VMEM((n_gy, panels, wide), BF16),
            pltpu.VMEM((n_gx * panels, wide), F32),
            DMA,
        ],
        compiler_params=params(16),
        cost_estimate=cost(4 * hydro.size * wide, 2 * hydro.size),
    )(spot, hydro, loads, *pieces)
    pressures = lax.all_to_all(pressure_parts, "gy", 0, 0, tiled=True)
    reactions = [reaction_parts[0]] + [exchange(reaction_parts[step], step) for step in range(1, n_gx)]

    residual, multiplier, own = pl.pallas_call(
        functools.partial(local_kernel, rows, cols, (n_gx, n_gy)),
        name="local",
        out_shape=[pltpu.VMEM(field, F32)] * 3,
        in_specs=[SCALARS] * 2 + [FAR] * 4 + [WHOLE] * 4,
        out_specs=[WHOLE] * 3,
        scratch_shapes=[pltpu.VMEM(field, BF16)] * 3 + [pltpu.VMEM(coupling.shape, BF16), DMA((4,))],
        compiler_params=params(16),
        cost_estimate=cost(10 * blocks * block_flops, 20 * blocks * unknowns**2 + 20 * blocks * wide * unknowns),
    )(spot, joints, far(motion), far(load), far(force), far(coupling), first, second, third, fourth)

    residual, multiplier, sensitivity = pl.pallas_call(
        functools.partial(final_kernel, rows, cols, lift),
        name="final",
        out_shape=[pltpu.HBM(field, F32), pltpu.HBM(field, F32), shaped(F32, rows, cols)],
        in_specs=[WHOLE] * (5 + n_gx),
        out_specs=[FAR, FAR, SCALARS],
        scratch_shapes=[pltpu.VMEM((2,) + field, F32), DMA((2, blocks))],
        compiler_params=params(16),
        cost_estimate=cost(4 * blocks * wide * unknowns * panels, 20 * blocks * wide * unknowns),
    )(panel_map, residual, multiplier, own, pressures, *reactions)
    shape = plate_motion.shape
    return residual.reshape(shape), multiplier.reshape(shape), sensitivity


def solution(mesh):
    field = P("gx", "gy", None, None, None)
    placed = (
        field,
        field,
        field,
        P("gx", "gy", None, None, None, None),
        P("gx", "gy", None),
        P(None, "gx", "gy"),
        P(("gx", "gy"), None, None, None),
    )
    return jax.shard_map(on_device, mesh=mesh, in_specs=placed, out_specs=(field, field, P("gx", "gy")), check_vma=False)
```

```python
import functools
import math

import jax
import jax.numpy as jnp
from jax import lax
from jax.experimental import pallas as pl
from jax.experimental.pallas import tpu as pltpu
from jax.sharding import PartitionSpec as P


F32 = jnp.float32
BF16 = jnp.bfloat16
OFFSETS = ((-1, 0), (1, 0), (0, -1), (0, 1))
WHOLE = pl.BlockSpec(memory_space=pltpu.VMEM)
SCALARS = pl.BlockSpec(memory_space=pltpu.SMEM)
FAR = pl.BlockSpec(memory_space=pltpu.HBM)


def dot(a, b, over):
    return lax.dot_general(a, b, ((over[:1], over[1:]), ((), ())), preferred_element_type=F32)


def times_i(field, axis):
    shape = field.shape
    if axis == 0:
        field, axis = field.reshape(-1, 8, shape[1]), 1
    size = field.shape[axis]
    after = pltpu.roll(field, size - 1, axis)
    before = pltpu.roll(field, 1, axis)
    place = lax.broadcasted_iota(jnp.int32, field.shape, axis)
    return jnp.where(lax.rem(place, 2) == 0, -after, before).reshape(shape)


def forward_parts(coupling, motion):
    return dot(motion, coupling.reshape(-1, coupling.shape[-1]), (1, 1))


def adjoint_parts(coupling, load):
    return dot(load, jnp.concatenate([coupling[0], coupling[1]], axis=1), (1, 0))


def joined(parts, sign):
    half = parts.shape[1] // 2
    turned = times_i(parts[:, half:], 0)
    return parts[:, :half] + turned if sign > 0 else parts[:, :half] - turned


def map_of_blocks(map_ref, blocks):
    rows = map_ref.shape[0]
    panels = rows // blocks
    row = lax.broadcasted_iota(jnp.int32, (panels, rows), 0)
    column = lax.broadcasted_iota(jnp.int32, (panels, rows), 1)
    whole = map_ref[...]
    out = []
    for b in range(blocks):
        pick = (column == row * blocks + b).astype(F32).astype(BF16)
        out.append(dot(pick, whole, (1, 0)).astype(BF16))
    return out


def target(i, step, n):
    if step == 0:
        return i
    if step == 1:
        return i ^ 1
    if step == 2:
        return (((i + 1) ^ 1) + n - 1) % n
    return (i + step - 1) % n


def source(i, step, n):
    return target(i, step, n) if step < 3 else (i + n + 1 - step) % n


def exchange(x, step, axis="gx", wrap=True):
    n = lax.axis_size(axis)
    pairs = [(i, target(i, step, n)) for i in range(n)]
    return lax.ppermute(x, axis, [(i, j) for i, j in pairs if wrap or abs(i - j) < n - 1 or n == 2])


def near(x):
    return pltpu.with_memory_space_constraint(x, pltpu.VMEM)


def far(x):
    return pltpu.with_memory_space_constraint(x, pltpu.HBM)


def edges(rows, cols, spot):
    sides = []
    for axis in range(2):
        even = 1 - spot[axis] % 2
        for up in (even, 1 - even):
            if axis == 0:
                sides.append([(up * (rows - 1), y, up) for y in range(cols)])
            else:
                sides.append([(x, up * (cols - 1), 2 + up) for x in range(rows)])
    return sides


def fetch_edges(which, sides, cols, coupling_far, coupling, arrive, first):
    moves = []
    for o in which:
        for x, y, d in sides[o]:
            i = len(moves)
            moves.append(pltpu.make_async_copy(coupling_far.at[x * cols + y, d + 1], coupling.at[i], arrive.at[first + i]))
            moves[-1].start()
    return moves


def fill_edges(which, sides, cols, joints, motion, load, coupling, moves, outs):
    wide = motion.shape[1]
    i = 0
    for o, out in zip(which, outs):
        for k, (x, y, d) in enumerate(sides[o]):
            out[pl.ds(k * wide, wide), :] = motion[x * cols + y]
            moves[i].wait()
            link = joints[x, y, d].astype(F32)
            term = joined(adjoint_parts(coupling[i], load[x * cols + y]), -1)
            out[pl.ds((len(sides[o]) + k) * wide, wide), :] = (link * term).astype(BF16)
            i += 1


def panels_kernel(rows, cols, which, spot, joints, motion_far, load_far, coupling_far, map_far, *refs):
    motion_out, load_out, outs, refs = refs[0], refs[1], refs[2 : 2 + len(which)], refs[2 + len(which) :]
    motion, load, coupling, maps, arrive = refs
    moves = [
        pltpu.make_async_copy(map_far, maps, arrive.at[0]),
        pltpu.make_async_copy(motion_far, motion, arrive.at[1]),
        pltpu.make_async_copy(load_far, load, arrive.at[2]),
    ]
    for move in moves:
        move.start()
    sides = edges(rows, cols, spot)
    more = fetch_edges(which, sides, cols, coupling_far, coupling, arrive, 3)
    blocks = motion.shape[0]
    moves[0].wait()
    split = map_of_blocks(maps, blocks)
    for move, field, out in ((moves[1], motion, motion_out), (moves[2], load, load_out)):
        move.wait()
        out[...] = sum(dot(split[b], field[b], (1, 1)) for b in range(blocks)).astype(BF16)
    fill_edges(which, sides, cols, joints, motion, load, coupling, more, outs)


def edges_kernel(rows, cols, which, spot, joints, motion_far, load_far, coupling_far, *refs):
    outs, (motion, load, coupling, arrive) = refs[: len(which)], refs[len(which) :]
    moves = [
        pltpu.make_async_copy(load_far, load, arrive.at[0]),
        pltpu.make_async_copy(motion_far, motion, arrive.at[1]),
    ]
    for move in moves:
        move.start()
    sides = edges(rows, cols, spot)
    more = fetch_edges(which, sides, cols, coupling_far, coupling, arrive, 2)
    for move in moves:
        move.wait()
    fill_edges(which, sides, cols, joints, motion, load, coupling, more, outs)


def pressure_kernel(n_gx, spot, hydro_ref, load_panels, *refs):
    pieces, (out_far, gathered, out, leave) = refs[:n_gx], refs[n_gx:]
    me = spot[0]
    panels, wide = load_panels.shape
    for step in range(n_gx):
        start = pl.multiple_of(source(me, step, n_gx) * panels, panels)
        gathered[pl.ds(start, panels), :] = pieces[step][...]
    hydro = hydro_ref[...]
    size, depth = hydro.shape[1:]
    both = dot(hydro.reshape(2 * size, depth), gathered[...], (1, 0))
    pressure = both[:size] + times_i(both[size:], 1)
    out[:, :panels, :] = pressure.astype(BF16).reshape(-1, panels, wide)
    out[:, panels:, :] = jnp.broadcast_to(load_panels[...], (out.shape[0], panels, wide))
    move = pltpu.make_async_copy(out, out_far, leave)
    move.start()
    move.wait()


def reaction_kernel(n_gx, spot, hydro_ref, arrived, *refs):
    outs, (reacted,) = refs[:n_gx], refs[n_gx:]
    me = spot[0]
    panels = outs[0].shape[0]
    hydro = hydro_ref[...]
    loads = arrived[:, panels:, :].reshape(hydro.shape[1], -1)
    real = dot(hydro[0], loads, (0, 0))
    imag = dot(hydro[1], loads, (0, 0))
    reacted[...] = real - times_i(imag, 1)
    for step in range(n_gx):
        start = pl.multiple_of(target(me, step, n_gx) * panels, panels)
        outs[step][...] = reacted[pl.ds(start, panels), :]


def local_kernel(rows, cols, sizes, spot, joints, motion_far, load_far, excitation_far, coupling_far, *refs):
    received_refs, (residual_out, multiplier_out, own_out), refs = refs[:4], refs[4:7], refs[7:]
    motion, load, excitation, coupling, arrive = refs
    moves = [
        pltpu.make_async_copy(motion_far, motion, arrive.at[0]),
        pltpu.make_async_copy(load_far, load, arrive.at[1]),
        pltpu.make_async_copy(coupling_far, coupling, arrive.at[2]),
        pltpu.make_async_copy(excitation_far, excitation, arrive.at[3]),
    ]
    for move in moves:
        move.start()
    wide = motion.shape[1]
    even = [spot[axis] % 2 == 0 for axis in range(2)]
    valid = []
    for axis in range(2):
        valid += [(spot[axis] > 0).astype(F32), (spot[axis] < sizes[axis] - 1).astype(F32)]

    def received(d, k, kind):
        count = cols if d < 2 else rows
        here = pl.ds((kind * count + k) * wide, wide)
        first, second = received_refs[d // 2 * 2], received_refs[d // 2 * 2 + 1]
        if d % 2:
            first, second = second, first
        return jnp.where(even[d // 2], second[here, :], first[here, :])

    for move in moves:
        move.wait()
    for x in range(rows):
        for y in range(cols):
            b = x * cols + y
            own = joined(forward_parts(coupling[b, 0], motion[b]), 1)
            own_out[b] = own
            parts = None
            adjoint = adjoint_parts(coupling[b, 0], load[b])
            extra = None
            for d in range(4):
                nx, ny = x + OFFSETS[d][0], y + OFFSETS[d][1]
                link = joints[x, y, d].astype(F32)
                if 0 <= nx < rows and 0 <= ny < cols:
                    n = nx * cols + ny
                    beside = motion[n]
                    back = joints[nx, ny, d ^ 1].astype(F32)
                    adjoint = adjoint + back * adjoint_parts(coupling[n, (d ^ 1) + 1], load[n])
                else:
                    k = y if d < 2 else x
                    beside = received(d, k, 0)
                    link = link * valid[d]
                    term = received(d, k, 1).astype(F32) * valid[d]
                    extra = term if extra is None else extra + term
                part = link * forward_parts(coupling[b, d + 1], beside)
                parts = part if parts is None else parts + part
            residual_out[b] = own + joined(parts, 1) - excitation[b].astype(F32)
            multiplier = joined(adjoint, -1)
            multiplier_out[b] = multiplier if extra is None else multiplier + extra


def final_kernel(rows, cols, lift, map_ref, residual, multiplier, own, pressures, *refs):
    reactions, (residual_out, multiplier_out, sensitivity_out, full, leave) = refs[:-5], refs[-5:]
    blocks = rows * cols
    maps = map_of_blocks(map_ref, blocks)
    panels = reactions[0].shape[0]
    pressure = jnp.sum(pressures[:, :panels, :].astype(F32), axis=0).astype(BF16)
    reaction = sum(r[...].astype(F32) for r in reactions).astype(BF16)
    scale = 1.0 / math.sqrt(own.shape[1] // 2 * own.shape[2])
    sent = []
    for b in range(blocks):
        full[0, b] = residual[b] + lift * dot(pressure, maps[b], (0, 0))
        sent.append(pltpu.make_async_copy(full.at[0, b], residual_out.at[b], leave.at[0, b]))
        sent[-1].start()
    for b in range(blocks):
        value = multiplier[b] + lift * dot(reaction, maps[b], (0, 0))
        full[1, b] = value
        sent.append(pltpu.make_async_copy(full.at[1, b], multiplier_out.at[b], leave.at[1, b]))
        sent[-1].start()
        sensitivity_out[b // cols, b % cols] = jnp.sum(value * own[b]) * scale
    for move in sent:
        move.wait()


def cost(flops, bytes_accessed):
    return pl.CostEstimate(flops=int(flops), bytes_accessed=int(bytes_accessed), transcendentals=0)


def shaped(dtype, *shape):
    return jax.ShapeDtypeStruct(shape, dtype)


def params(mebibytes):
    return pltpu.CompilerParams(vmem_limit_bytes=mebibytes * 1024 * 1024)


DMA = pltpu.SemaphoreType.DMA


def on_device(plate_motion, adjoint_load, excitation, coupling, joints, hydro, panel_map):
    rows, cols, cases, _, unknowns = plate_motion.shape
    panels = panel_map.shape[0]
    blocks, wide = rows * cols, 2 * cases
    n_gx, n_gy = lax.axis_size("gx"), lax.axis_size("gy")
    spot = jnp.stack([lax.axis_index("gx"), lax.axis_index("gy")])
    motion = plate_motion.reshape(blocks, wide, unknowns)
    load = adjoint_load.reshape(blocks, wide, unknowns)
    force = excitation.reshape(blocks, wide, unknowns)
    coupling = coupling.reshape(blocks, 5, 2, unknowns, unknowns)
    panel_map = panel_map.reshape(panels * blocks, unknowns)
    lift = math.sqrt(blocks * unknowns / panels)
    block_flops = 2 * wide * unknowns * unknowns * 2
    field = (blocks, wide, unknowns)

    counts = [cols, cols, rows, rows]
    early, late = (2,), (0, 1, 3)
    motion_panels, load_panels, *payloads = pl.pallas_call(
        functools.partial(panels_kernel, rows, cols, early),
        name="panels",
        out_shape=[pltpu.VMEM((panels, wide), BF16)] * 2
        + [pltpu.VMEM((2 * counts[o] * wide, unknowns), BF16) for o in early],
        in_specs=[SCALARS, SCALARS] + [FAR] * 4,
        out_specs=[WHOLE] * (2 + len(early)),
        scratch_shapes=[
            pltpu.VMEM(field, BF16),
            pltpu.VMEM(field, BF16),
            pltpu.VMEM((sum(counts[o] for o in early), 2, unknowns, unknowns), BF16),
            pltpu.VMEM(panel_map.shape, BF16),
            DMA((3 + sum(counts[o] for o in early),)),
        ],
        compiler_params=params(16),
        cost_estimate=cost(4 * blocks * wide * unknowns * panels, 4 * blocks * wide * unknowns),
    )(spot, far(joints), far(motion), far(load), far(coupling), far(panel_map))
    pieces = [motion_panels] + [exchange(motion_panels, step) for step in range(1, n_gx)]
    third = exchange(payloads[0], 1, "gy")

    payloads = pl.pallas_call(
        functools.partial(edges_kernel, rows, cols, late),
        name="edges",
        out_shape=[pltpu.VMEM((2 * counts[o] * wide, unknowns), BF16) for o in late],
        in_specs=[SCALARS, SCALARS] + [FAR] * 3,
        out_specs=[WHOLE] * len(late),
        scratch_shapes=[
            pltpu.VMEM(field, BF16),
            pltpu.VMEM(field, BF16),
            pltpu.VMEM((sum(counts[o] for o in late), 2, unknowns, unknowns), BF16),
            DMA((2 + sum(counts[o] for o in late),)),
        ],
        compiler_params=params(16),
        cost_estimate=cost(sum(counts) * block_flops, 4 * blocks * wide * unknowns + 20 * blocks * unknowns**2),
    )(spot, far(joints), far(motion), far(load), far(coupling))
    (*payloads, load_panels) = lax.optimization_barrier((*payloads, load_panels))
    first, second = exchange(payloads[0], 1), exchange(payloads[1], 2, wrap=False)
    fourth = exchange(payloads[2], 2, "gy", wrap=False)

    parts = pl.pallas_call(
        functools.partial(pressure_kernel, n_gx),
        name="pressure",
        out_shape=pltpu.HBM((n_gy, 2 * panels, wide), BF16),
        in_specs=[SCALARS] + [WHOLE] * (2 + n_gx),
        out_specs=FAR,
        scratch_shapes=[pltpu.VMEM((n_gx * panels, wide), BF16), pltpu.VMEM((n_gy, 2 * panels, wide), BF16), DMA],
        compiler_params=params(16),
        cost_estimate=cost(2 * hydro.size * wide, 2 * hydro.size),
    )(spot, hydro, load_panels, *pieces)
    parts, third = lax.optimization_barrier((parts, third))
    arrived = lax.all_to_all(parts, "gy", 0, 0, tiled=True)

    reaction_parts = pl.pallas_call(
        functools.partial(reaction_kernel, n_gx),
        name="reaction",
        out_shape=[pltpu.VMEM((panels, wide), F32)] * n_gx,
        in_specs=[SCALARS] + [WHOLE] * 2,
        out_specs=[WHOLE] * n_gx,
        scratch_shapes=[pltpu.VMEM((n_gx * panels, wide), F32)],
        compiler_params=params(16),
        cost_estimate=cost(2 * hydro.size * wide, 2 * hydro.size),
    )(spot, hydro, arrived)
    reactions = [reaction_parts[0]] + [exchange(reaction_parts[step], step) for step in range(1, n_gx)]

    residual, multiplier, own = pl.pallas_call(
        functools.partial(local_kernel, rows, cols, (n_gx, n_gy)),
        name="local",
        out_shape=[pltpu.VMEM(field, F32)] * 3,
        in_specs=[SCALARS] * 2 + [FAR] * 4 + [WHOLE] * 4,
        out_specs=[WHOLE] * 3,
        scratch_shapes=[pltpu.VMEM(field, BF16)] * 3 + [pltpu.VMEM(coupling.shape, BF16), DMA((4,))],
        compiler_params=params(16),
        cost_estimate=cost(10 * blocks * block_flops, 20 * blocks * unknowns**2 + 20 * blocks * wide * unknowns),
    )(spot, far(joints), far(motion), far(load), far(force), far(coupling), first, second, third, fourth)

    residual, multiplier, sensitivity = pl.pallas_call(
        functools.partial(final_kernel, rows, cols, lift),
        name="final",
        out_shape=[pltpu.HBM(field, F32), pltpu.HBM(field, F32), shaped(F32, rows, cols)],
        in_specs=[WHOLE] * (5 + n_gx),
        out_specs=[FAR, FAR, SCALARS],
        scratch_shapes=[pltpu.VMEM((2,) + field, F32), DMA((2, blocks))],
        compiler_params=params(16),
        cost_estimate=cost(4 * blocks * wide * unknowns * panels, 20 * blocks * wide * unknowns),
    )(panel_map, residual, multiplier, own, arrived, *reactions)
    shape = plate_motion.shape
    return residual.reshape(shape), multiplier.reshape(shape), sensitivity


def solution(mesh):
    field = P("gx", "gy", None, None, None)
    placed = (
        field,
        field,
        field,
        P("gx", "gy", None, None, None, None),
        P("gx", "gy", None),
        P(None, "gx", "gy"),
        P(("gx", "gy"), None, None, None),
    )
    return jax.shard_map(on_device, mesh=mesh, in_specs=placed, out_specs=(field, field, P("gx", "gy")), check_vma=False)
```

```python
import functools
import math

import jax
import jax.numpy as jnp
from jax import lax
from jax.experimental import pallas as pl
from jax.experimental.pallas import tpu as pltpu
from jax.sharding import PartitionSpec as P


F32 = jnp.float32
BF16 = jnp.bfloat16
OFFSETS = ((-1, 0), (1, 0), (0, -1), (0, 1))
WHOLE = pl.BlockSpec(memory_space=pltpu.VMEM)
SCALARS = pl.BlockSpec(memory_space=pltpu.SMEM)
FAR = pl.BlockSpec(memory_space=pltpu.HBM)


def dot(a, b, over):
    return lax.dot_general(a, b, ((over[:1], over[1:]), ((), ())), preferred_element_type=F32)


def times_i(field, axis):
    shape = field.shape
    if axis == 0:
        field, axis = field.reshape(-1, 8, shape[1]), 1
        place = lax.broadcasted_iota(jnp.int32, (1, 8, shape[1]), 1)
    else:
        place = lax.broadcasted_iota(jnp.int32, (1, shape[1]), 1)
    size = field.shape[axis]
    after = pltpu.roll(field, size - 1, axis)
    before = pltpu.roll(field, 1, axis)
    return jnp.where((place & 1) == 0, -after, before).reshape(shape)


def forward_parts(coupling, motion):
    return dot(motion, coupling.reshape(-1, coupling.shape[-1]), (1, 1))


def adjoint_parts(coupling, load):
    return dot(load, jnp.concatenate([coupling[0], coupling[1]], axis=1), (1, 0))


def beside_turned(field, sign):
    turned = times_i(field.astype(F32), 0)
    return jnp.concatenate([field, (turned if sign > 0 else -turned).astype(BF16)], axis=1)


def forward_product(coupling, both):
    return dot(both, jnp.concatenate([coupling[0], coupling[1]], axis=1), (1, 1))


def adjoint_product(coupling, both):
    return dot(both, coupling.reshape(-1, coupling.shape[-1]), (1, 0))


def joined(parts, sign):
    half = parts.shape[1] // 2
    turned = times_i(parts[:, half:], 0)
    return parts[:, :half] + turned if sign > 0 else parts[:, :half] - turned


def map_of_blocks(map_ref, blocks):
    rows = map_ref.shape[0]
    panels = rows // blocks
    row = lax.broadcasted_iota(jnp.int32, (panels, rows), 0)
    column = lax.broadcasted_iota(jnp.int32, (panels, rows), 1)
    whole = map_ref[...]
    out = []
    for b in range(blocks):
        pick = (column == row * blocks + b).astype(F32).astype(BF16)
        out.append(dot(pick, whole, (1, 0)).astype(BF16))
    return out


def target(i, step, n):
    if step == 0:
        return i
    if step == 1:
        return i ^ 1
    if step == 2:
        return (((i + 1) ^ 1) + n - 1) % n
    return (i + step - 1) % n


def source(i, step, n):
    return target(i, step, n) if step < 3 else (i + n + 1 - step) % n


def exchange(x, step):
    n = lax.axis_size("gx")
    return lax.ppermute(x, "gx", [(i, target(i, step, n)) for i in range(n)])


def exchange_sides(x, axis, step):
    sizes = lax.axis_size("gx"), lax.axis_size("gy")
    pairs = []
    for x_at in range(sizes[0]):
        for y_at in range(sizes[1]):
            there = [x_at, y_at]
            other = target(there[axis], step, sizes[axis])
            if axis == 0 or abs(other - there[axis]) == 1:
                there[axis] = other
            else:
                there[0] ^= 1
            pairs.append((x_at * sizes[1] + y_at, there[0] * sizes[1] + there[1]))
    return lax.ppermute(x, ("gx", "gy"), pairs)


def far(x):
    return pltpu.with_memory_space_constraint(x, pltpu.HBM)


def edges(rows, cols, spot):
    sides = []
    for axis in range(2):
        even = 1 - spot[axis] % 2
        for up in (even, 1 - even):
            if axis == 0:
                sides.append([(up * (rows - 1), y, up) for y in range(cols)])
            else:
                sides.append([(x, up * (cols - 1), 2 + up) for x in range(rows)])
    return sides


def fetch_edges(which, sides, cols, coupling_far, coupling, arrive, first):
    moves = []
    for o in which:
        for x, y, d in sides[o]:
            i = len(moves)
            moves.append(pltpu.make_async_copy(coupling_far.at[x * cols + y, d + 1], coupling.at[i], arrive.at[first + i]))
            moves[-1].start()
    return moves


def panels_kernel(rows, cols, early, late, spot, joints, motion_far, load_far, coupling_far, map_far, *refs):
    motion_out, outs, refs = refs[0], refs[1 : 1 + len(early)], refs[1 + len(early) :]
    motion, load, maps, near_coupling, coupling, arrive = refs
    moves = [
        pltpu.make_async_copy(map_far, maps, arrive.at[0]),
        pltpu.make_async_copy(motion_far, motion, arrive.at[1]),
        pltpu.make_async_copy(load_far, load, arrive.at[2]),
    ]
    for move in moves:
        move.start()
    sides = edges(rows, cols, spot)
    more = fetch_edges(early, sides, cols, coupling_far, coupling, arrive, 3)
    later = fetch_edges(late, sides, cols, coupling_far, near_coupling, arrive, 3 + len(more))
    blocks, wide = motion.shape[:2]
    moves[0].wait()
    split = map_of_blocks(maps, blocks)
    moves[1].wait()
    motion_out[...] = sum(dot(split[b], motion[b], (1, 1)) for b in range(blocks)).astype(BF16)
    moves[2].wait()
    i = 0
    for o, out in zip(early, outs):
        for k, (x, y, d) in enumerate(sides[o]):
            out[pl.ds(k * wide, wide), :] = motion[x * cols + y]
            more[i].wait()
            link = joints[x, y, d].astype(F32)
            term = joined(adjoint_parts(coupling[i], load[x * cols + y]), -1)
            out[pl.ds((len(sides[o]) + k) * wide, wide), :] = (link * term).astype(BF16)
            i += 1
    for move in later:
        move.wait()


def edges_kernel(rows, cols, late, spot, joints, motion, load, maps, coupling, *refs):
    load_out, outs, (both,) = refs[0], refs[1 : 1 + len(late)], refs[1 + len(late) :]
    blocks, wide = motion.shape[:2]
    sides = edges(rows, cols, spot)
    split = map_of_blocks(maps, blocks)
    load_out[...] = sum(dot(split[b], load[b], (1, 1)) for b in range(blocks)).astype(BF16)
    for b in range(blocks):
        both[b] = beside_turned(load[b], -1)
    i = 0
    for o, out in zip(late, outs):
        for k, (x, y, d) in enumerate(sides[o]):
            out[pl.ds(k * wide, wide), :] = motion[x * cols + y]
            matrix = coupling[i] * joints[x, y, d].astype(BF16)
            term = adjoint_product(matrix, both[x * cols + y])
            out[pl.ds((len(sides[o]) + k) * wide, wide), :] = term.astype(BF16)
            i += 1


def pressure_kernel(n_gx, spot, hydro_ref, load_panels, *refs):
    pieces, (out_far, gathered, out, leave) = refs[:n_gx], refs[n_gx:]
    me = spot[0]
    panels, wide = load_panels.shape
    for step in range(n_gx):
        start = pl.multiple_of(source(me, step, n_gx) * panels, panels)
        gathered[0, pl.ds(start, panels), :] = pieces[step][...]
        gathered[1, pl.ds(start, panels), :] = times_i(pieces[step][...].astype(F32), 1).astype(BF16)
    fields = gathered[...].reshape(-1, wide)
    tiles = out.shape[0]
    moves = []
    for i in range(2):
        here = pl.ds(i * tiles // 2, tiles // 2)
        rows = pl.ds(i * tiles // 2 * panels, tiles // 2 * panels)
        hydro = jnp.concatenate([hydro_ref[0, rows, :], hydro_ref[1, rows, :]], axis=1)
        out[here, :panels, :] = dot(hydro, fields, (1, 0)).astype(BF16).reshape(-1, panels, wide)
        out[here, panels:, :] = jnp.broadcast_to(load_panels[...], (tiles // 2, panels, wide))
        moves.append(pltpu.make_async_copy(out.at[here], out_far.at[here], leave.at[i]))
        moves[-1].start()
    for move in moves:
        move.wait()


def reaction_kernel(n_gx, spot, hydro_ref, arrived, *refs):
    outs, (reacted,) = refs[:n_gx], refs[n_gx:]
    me = spot[0]
    panels = outs[0].shape[0]
    hydro = hydro_ref[...]
    loads = arrived[:, panels:, :].reshape(hydro.shape[1], -1)
    real = dot(hydro[0], loads, (0, 0))
    imag = dot(hydro[1], loads, (0, 0))
    reacted[...] = real - times_i(imag, 1)
    for step in range(n_gx):
        start = pl.multiple_of(target(me, step, n_gx) * panels, panels)
        outs[step][...] = reacted[pl.ds(start, panels), :]


def add_side(side, joints, valid, received, couplings, residual, multiplier):
    wide = residual.shape[1]
    for k, (b, x, y, d) in enumerate(side):
        matrix = couplings(k, b, d) * (joints[x, y, d].astype(F32) * valid).astype(BF16)
        motion = received[pl.ds(k * wide, wide), :]
        residual[b] += joined(forward_parts(matrix, motion), 1)
        terms = received[pl.ds((len(side) + k) * wide, wide), :]
        multiplier[b] += valid * terms.astype(F32)


def placed(cols, sides):
    return [[(x * cols + y, x, y, d) for x, y, d in side] for side in sides]


def beyond(spot, sizes, o):
    n, me = sizes[o // 2], spot[o // 2]
    other = target(me, 1 + o % 2, n)
    return (abs(me - other) <= 1).astype(F32) if n > 2 else F32(1 - o % 2)


def interior_kernel(rows, cols, sizes, early, late, spot, joints, motion_far, load_far, excitation_far, *refs):
    coupling_far, received, refs = refs[0], refs[1 : 1 + len(early)], refs[1 + len(early) :]
    residual_out, multiplier_out, own_far, outer, motion, load, excitation, coupling, own, arrive, leave = refs
    blocks = rows * cols
    moves = [
        pltpu.make_async_copy(motion_far, motion, arrive.at[0]),
        pltpu.make_async_copy(load_far, load, arrive.at[1]),
    ]
    for b in range(blocks):
        moves.append(pltpu.make_async_copy(coupling_far.at[b], coupling.at[b], arrive.at[2 + b]))
    moves.append(pltpu.make_async_copy(excitation_far, excitation, arrive.at[2 + blocks]))
    for move in moves:
        move.start()
    sides = edges(rows, cols, spot)
    later = fetch_edges(late, sides, cols, coupling_far, outer, arrive, 3 + blocks)
    moves[0].wait()
    moving = [beside_turned(motion[b], 1) for b in range(blocks)]
    moves[1].wait()
    loads = [beside_turned(load[b], -1) for b in range(blocks)]
    sent = []
    for b in range(blocks):
        moves[2 + b].wait()
        own[b] = forward_product(coupling[b, 0], moving[b])
        sent.append(pltpu.make_async_copy(own.at[b], own_far.at[b], leave.at[b]))
        sent[-1].start()
    moves[2 + blocks].wait()
    for x in range(rows):
        for y in range(cols):
            b = x * cols + y
            forward, adjoint = [], [(loads[b], coupling[b, 0])]
            for d in range(4):
                nx, ny = x + OFFSETS[d][0], y + OFFSETS[d][1]
                if 0 <= nx < rows and 0 <= ny < cols:
                    n = nx * cols + ny
                    forward.append((moving[n], coupling[b, d + 1] * joints[x, y, d].astype(BF16)))
                    adjoint.append((loads[n], coupling[n, (d ^ 1) + 1] * joints[nx, ny, d ^ 1].astype(BF16)))
            residual = own[b] - excitation[b].astype(F32)
            if forward:
                fields = jnp.concatenate([f for f, _ in forward], axis=1)
                matrix = jnp.concatenate([c[part] for _, c in forward for part in range(2)], axis=1)
                residual = residual + dot(fields, matrix, (1, 1))
            residual_out[b] = residual
            fields = jnp.concatenate([f for f, _ in adjoint], axis=1)
            matrix = jnp.concatenate([c[part] for _, c in adjoint for part in range(2)], axis=0)
            multiplier_out[b] = dot(fields, matrix, (1, 0))
    for o, ref in zip(early, received):
        side = placed(cols, sides)[o]
        add_side(side, joints, beyond(spot, sizes, o), ref, lambda k, b, d: coupling[b, d + 1], residual_out, multiplier_out)
    for move in sent + later:
        move.wait()


def boundary_kernel(rows, cols, sizes, lift, late, spot, joints, map_ref, coupling, residual, multiplier, arrived, *refs):
    received, (residual_out, multiplier_out, full, leave) = refs[: len(late)], refs[len(late) :]
    blocks, unknowns = rows * cols, residual.shape[2]
    panels = map_ref.shape[0] // blocks
    maps = jnp.concatenate(map_of_blocks(map_ref, blocks), axis=1)
    pressure = jnp.sum(arrived[:, :panels, :].astype(F32), axis=0).astype(BF16)
    forces = lift * dot(pressure, maps, (0, 0))
    for b in range(blocks):
        full[b] = residual[b] + forces[:, b * unknowns : (b + 1) * unknowns]
        multiplier_out[b] = multiplier[b]
    sides, first = placed(cols, edges(rows, cols, spot)), 0
    for o, ref in zip(late, received):
        at = first
        add_side(sides[o], joints, beyond(spot, sizes, o), ref, lambda k, b, d: coupling[at + k], full, multiplier_out)
        first += len(sides[o])
    move = pltpu.make_async_copy(full, residual_out, leave)
    move.start()
    move.wait()


def final_kernel(rows, cols, lift, map_ref, multiplier, own, *refs):
    reactions, (multiplier_out, sensitivity_out, full, leave) = refs[:-4], refs[-4:]
    blocks = rows * cols
    unknowns = own.shape[2]
    maps = jnp.concatenate(map_of_blocks(map_ref, blocks), axis=1)
    reaction = sum(r[...].astype(F32) for r in reactions).astype(BF16)
    scale = 1.0 / math.sqrt(own.shape[1] // 2 * unknowns)
    forces = lift * dot(reaction, maps, (0, 0))
    sent, sums = [], []
    for b in range(blocks):
        value = multiplier[b] + forces[:, b * unknowns : (b + 1) * unknowns]
        full[b] = value
        sent.append(pltpu.make_async_copy(full.at[b], multiplier_out.at[b], leave.at[b]))
        sent[-1].start()
        sums.append(jnp.sum((value * own[b]).reshape(-1, 8, unknowns), axis=0))
    for b in range(blocks):
        sensitivity_out[b // cols, b % cols] = jnp.sum(sums[b]) * scale
    for move in sent:
        move.wait()


def cost(flops, bytes_accessed):
    return pl.CostEstimate(flops=int(flops), bytes_accessed=int(bytes_accessed), transcendentals=0)


def shaped(dtype, *shape):
    return jax.ShapeDtypeStruct(shape, dtype)


def params(mebibytes):
    return pltpu.CompilerParams(vmem_limit_bytes=mebibytes * 1024 * 1024)


DMA = pltpu.SemaphoreType.DMA


def on_device(plate_motion, adjoint_load, excitation, coupling, joints, hydro, panel_map):
    rows, cols, cases, _, unknowns = plate_motion.shape
    panels = panel_map.shape[0]
    blocks, wide = rows * cols, 2 * cases
    n_gx, n_gy = lax.axis_size("gx"), lax.axis_size("gy")
    spot = jnp.stack([lax.axis_index("gx"), lax.axis_index("gy")])
    motion = plate_motion.reshape(blocks, wide, unknowns)
    load = adjoint_load.reshape(blocks, wide, unknowns)
    force = excitation.reshape(blocks, wide, unknowns)
    coupling = coupling.reshape(blocks, 5, 2, unknowns, unknowns)
    panel_map = panel_map.reshape(panels * blocks, unknowns)
    lift = math.sqrt(blocks * unknowns / panels)
    block_flops = 2 * wide * unknowns * unknowns * 2
    field = (blocks, wide, unknowns)

    counts = [cols, cols, rows, rows]
    early, late = (3,), (0, 1, 2)
    few, many = sum(counts[o] for o in early), sum(counts[o] for o in late)
    pair = (2, unknowns, unknowns)
    motion_panels, *payloads, near_motion, near_load, near_map, near_coupling = pl.pallas_call(
        functools.partial(panels_kernel, rows, cols, early, late),
        name="panels",
        out_shape=[pltpu.VMEM((panels, wide), BF16)]
        + [pltpu.VMEM((2 * counts[o] * wide, unknowns), BF16) for o in early]
        + [pltpu.VMEM(field, BF16)] * 2
        + [pltpu.VMEM(panel_map.shape, BF16), pltpu.VMEM((many,) + pair, BF16)],
        in_specs=[SCALARS, SCALARS] + [FAR] * 4,
        out_specs=[WHOLE] * (5 + len(early)),
        scratch_shapes=[pltpu.VMEM((few,) + pair, BF16), DMA((3 + few + many,))],
        compiler_params=params(16),
        cost_estimate=cost(4 * blocks * wide * unknowns * panels, 4 * blocks * wide * unknowns),
    )(spot, far(joints), far(motion), far(load), far(coupling), far(panel_map))
    pieces = [motion_panels] + [exchange(motion_panels, step) for step in range(1, n_gx)]
    fourth = exchange_sides(payloads[0], 1, 2)

    load_panels, *payloads = pl.pallas_call(
        functools.partial(edges_kernel, rows, cols, late),
        name="edges",
        out_shape=[pltpu.VMEM((panels, wide), BF16)]
        + [pltpu.VMEM((2 * counts[o] * wide, unknowns), BF16) for o in late],
        in_specs=[SCALARS, SCALARS] + [WHOLE] * 4,
        out_specs=[WHOLE] * (1 + len(late)),
        scratch_shapes=[pltpu.VMEM((blocks, wide, 2 * unknowns), BF16)],
        compiler_params=params(16),
        cost_estimate=cost(many * block_flops, 4 * blocks * wide * unknowns + 12 * blocks * unknowns**2),
    )(spot, far(joints), near_motion, near_load, near_map, near_coupling)
    (*payloads, load_panels) = lax.optimization_barrier((*payloads, load_panels))
    first, second = exchange_sides(payloads[0], 0, 1), exchange_sides(payloads[1], 0, 2)
    third = exchange_sides(payloads[2], 1, 1)

    parts = pl.pallas_call(
        functools.partial(pressure_kernel, n_gx),
        name="pressure",
        out_shape=pltpu.HBM((n_gy, 2 * panels, wide), BF16),
        in_specs=[SCALARS] + [WHOLE] * (2 + n_gx),
        out_specs=FAR,
        scratch_shapes=[pltpu.VMEM((2, n_gx * panels, wide), BF16), pltpu.VMEM((n_gy, 2 * panels, wide), BF16), DMA((2,))],
        compiler_params=params(16),
        cost_estimate=cost(2 * hydro.size * wide, 2 * hydro.size),
    )(spot, hydro, load_panels, *pieces)
    parts, fourth = lax.optimization_barrier((parts, fourth))
    arrived = lax.all_to_all(parts, "gy", 0, 0, tiled=True)

    residual, multiplier, own, outer = pl.pallas_call(
        functools.partial(interior_kernel, rows, cols, (n_gx, n_gy), early, late),
        name="interior",
        out_shape=[pltpu.VMEM(field, F32)] * 2
        + [pltpu.HBM(field, F32), pltpu.VMEM((many,) + pair, BF16)],
        in_specs=[SCALARS] * 2 + [FAR] * 4 + [WHOLE] * len(early),
        out_specs=[WHOLE] * 2 + [FAR, WHOLE],
        scratch_shapes=[pltpu.VMEM(field, BF16)] * 3
        + [pltpu.VMEM(coupling.shape, BF16), pltpu.VMEM(field, F32), DMA((3 + blocks + many,)), DMA((blocks,))],
        compiler_params=params(16),
        cost_estimate=cost(6 * blocks * block_flops, 20 * blocks * unknowns**2 + 18 * blocks * wide * unknowns),
    )(spot, far(joints), far(motion), far(load), far(force), far(coupling), fourth)
    arrived, residual, multiplier, own, outer = lax.optimization_barrier((arrived, residual, multiplier, own, outer))

    reaction_parts = pl.pallas_call(
        functools.partial(reaction_kernel, n_gx),
        name="reaction",
        out_shape=[pltpu.VMEM((panels, wide), F32)] * n_gx,
        in_specs=[SCALARS] + [WHOLE] * 2,
        out_specs=[WHOLE] * n_gx,
        scratch_shapes=[pltpu.VMEM((n_gx * panels, wide), F32)],
        compiler_params=params(16),
        cost_estimate=cost(2 * hydro.size * wide, 2 * hydro.size),
    )(spot, hydro, arrived)
    reactions = [reaction_parts[0]] + [exchange(reaction_parts[step], step) for step in range(1, n_gx)]

    residual, multiplier = pl.pallas_call(
        functools.partial(boundary_kernel, rows, cols, (n_gx, n_gy), lift, late),
        name="boundary",
        out_shape=[pltpu.HBM(field, F32), pltpu.VMEM(field, F32)],
        in_specs=[SCALARS] * 2 + [WHOLE] * (5 + len(late)),
        out_specs=[FAR, WHOLE],
        scratch_shapes=[pltpu.VMEM(field, F32), DMA],
        compiler_params=params(16),
        cost_estimate=cost(4 * blocks * block_flops, 10 * blocks * unknowns**2 + 18 * blocks * wide * unknowns),
    )(spot, far(joints), panel_map, outer, residual, multiplier, arrived, first, second, third)

    multiplier, sensitivity = pl.pallas_call(
        functools.partial(final_kernel, rows, cols, lift),
        name="final",
        out_shape=[pltpu.HBM(field, F32), shaped(F32, rows, cols)],
        in_specs=[WHOLE] * (3 + n_gx),
        out_specs=[FAR, SCALARS],
        scratch_shapes=[pltpu.VMEM(field, F32), DMA((blocks,))],
        compiler_params=params(16),
        cost_estimate=cost(4 * blocks * wide * unknowns * panels, 20 * blocks * wide * unknowns),
    )(panel_map, multiplier, own, *reactions)
    shape = plate_motion.shape
    return residual.reshape(shape), multiplier.reshape(shape), sensitivity


def solution(mesh):
    field = P("gx", "gy", None, None, None)
    placed = (
        field,
        field,
        field,
        P("gx", "gy", None, None, None, None),
        P("gx", "gy", None),
        P(None, "gx", "gy"),
        P(("gx", "gy"), None, None, None),
    )
    return jax.shard_map(on_device, mesh=mesh, in_specs=placed, out_specs=(field, field, P("gx", "gy")), check_vma=False)
```

```python
import functools
import math

import jax
import jax.numpy as jnp
from jax import lax
from jax.experimental import pallas as pl
from jax.experimental.pallas import tpu as pltpu
from jax.sharding import PartitionSpec as P


F32 = jnp.float32
BF16 = jnp.bfloat16
OFFSETS = ((-1, 0), (1, 0), (0, -1), (0, 1))
WHOLE = pl.BlockSpec(memory_space=pltpu.VMEM)
FAR = pl.BlockSpec(memory_space=pltpu.HBM)


def dot(a, b, over):
    return lax.dot_general(a, b, ((over[:1], over[1:]), ((), ())), preferred_element_type=F32)


def times_i(field, axis):
    shape = field.shape
    if axis == 0:
        field, axis = field.reshape(-1, 8, shape[1]), 1
        place = lax.broadcasted_iota(jnp.int32, (1, 8, shape[1]), 1)
    else:
        place = lax.broadcasted_iota(jnp.int32, (1, shape[1]), 1)
    size = field.shape[axis]
    after = pltpu.roll(field, size - 1, axis)
    before = pltpu.roll(field, 1, axis)
    return jnp.where((place & 1) == 0, -after, before).reshape(shape)


def forward_parts(coupling, motion):
    return dot(motion, coupling.reshape(-1, coupling.shape[-1]), (1, 1))


def adjoint_parts(coupling, load):
    return dot(load, jnp.concatenate([coupling[0], coupling[1]], axis=1), (1, 0))


def beside_turned(field, sign):
    turned = times_i(field.astype(F32), 0)
    return jnp.concatenate([field, (turned if sign > 0 else -turned).astype(BF16)], axis=1)


def forward_product(coupling, both):
    return dot(both, jnp.concatenate([coupling[0], coupling[1]], axis=1), (1, 1))


def adjoint_product(coupling, both):
    return dot(both, coupling.reshape(-1, coupling.shape[-1]), (1, 0))


def joined(parts, sign):
    half = parts.shape[1] // 2
    turned = times_i(parts[:, half:], 0)
    return parts[:, :half] + turned if sign > 0 else parts[:, :half] - turned


def map_of_blocks(map_ref, blocks):
    rows = map_ref.shape[0]
    panels = rows // blocks
    row = lax.broadcasted_iota(jnp.int32, (panels, rows), 0)
    column = lax.broadcasted_iota(jnp.int32, (panels, rows), 1)
    whole = map_ref[...]
    out = []
    for b in range(blocks):
        pick = (column == row * blocks + b).astype(F32).astype(BF16)
        out.append(dot(pick, whole, (1, 0)).astype(BF16))
    return out


def target(i, step, n):
    if step == 0:
        return i
    if step == 1:
        return i ^ 1
    if step == 2:
        return (((i + 1) ^ 1) + n - 1) % n
    return (i + step - 1) % n


def source(i, step, n):
    return target(i, step, n) if step < 3 else (i + n + 1 - step) % n


def exchange(x, step):
    n = lax.axis_size("gx")
    return lax.ppermute(x, "gx", [(i, target(i, step, n)) for i in range(n)])


def exchange_sides(x, axis, step):
    sizes = lax.axis_size("gx"), lax.axis_size("gy")
    pairs = []
    for x_at in range(sizes[0]):
        for y_at in range(sizes[1]):
            there = [x_at, y_at]
            other = target(there[axis], step, sizes[axis])
            if axis == 0 or abs(other - there[axis]) == 1:
                there[axis] = other
            else:
                there[0] ^= 1
            pairs.append((x_at * sizes[1] + y_at, there[0] * sizes[1] + there[1]))
    return lax.ppermute(x, ("gx", "gy"), pairs)


def far(x):
    return pltpu.with_memory_space_constraint(x, pltpu.HBM)


def edges(rows, cols, spot):
    sides = []
    for axis in range(2):
        even = 1 - spot[axis] % 2
        for up in (even, 1 - even):
            if axis == 0:
                sides.append([(up * (rows - 1), y, up) for y in range(cols)])
            else:
                sides.append([(x, up * (cols - 1), 2 + up) for x in range(rows)])
    return sides


def here_on_mesh():
    return lax.axis_index("gx"), lax.axis_index("gy")


def fetch_edges(which, sides, cols, coupling_far, coupling, arrive, first):
    moves = []
    for o in which:
        for x, y, d in sides[o]:
            i = len(moves)
            moves.append(pltpu.make_async_copy(coupling_far.at[x * cols + y, d + 1], coupling.at[i], arrive.at[first + i]))
            moves[-1].start()
    return moves


def panels_kernel(rows, cols, early, late, joints_far, motion_far, load_far, coupling_far, map_far, *refs):
    motion_out, outs, refs = refs[0], refs[1 : 1 + len(early)], refs[1 + len(early) :]
    motion, load, maps, near_coupling, coupling, joints, arrive = refs
    moves = [
        pltpu.make_async_copy(map_far, maps, arrive.at[0]),
        pltpu.make_async_copy(motion_far, motion, arrive.at[1]),
        pltpu.make_async_copy(load_far, load, arrive.at[2]),
        pltpu.make_async_copy(joints_far, joints, arrive.at[3]),
    ]
    for move in moves:
        move.start()
    sides = edges(rows, cols, here_on_mesh())
    more = fetch_edges(early, sides, cols, coupling_far, coupling, arrive, 4)
    later = fetch_edges(late, sides, cols, coupling_far, near_coupling, arrive, 4 + len(more))
    blocks, wide = motion.shape[:2]
    moves[0].wait()
    split = map_of_blocks(maps, blocks)
    moves[1].wait()
    motion_out[...] = sum(dot(split[b], motion[b], (1, 1)) for b in range(blocks)).astype(BF16)
    moves[2].wait()
    moves[3].wait()
    i = 0
    for o, out in zip(early, outs):
        for k, (x, y, d) in enumerate(sides[o]):
            out[pl.ds(k * wide, wide), :] = motion[x * cols + y]
            more[i].wait()
            matrix = coupling[i] * joints[x, y, d].astype(BF16)
            term = joined(adjoint_parts(matrix, load[x * cols + y]), -1)
            out[pl.ds((len(sides[o]) + k) * wide, wide), :] = term.astype(BF16)
            i += 1
    i = 0
    for o in late:
        for x, y, d in sides[o]:
            later[i].wait()
            near_coupling[i] = near_coupling[i] * joints[x, y, d].astype(BF16)
            i += 1


def edges_kernel(rows, cols, late, motion, load, maps, coupling, *refs):
    load_out, outs, (both,) = refs[0], refs[1 : 1 + len(late)], refs[1 + len(late) :]
    blocks, wide = motion.shape[:2]
    sides = edges(rows, cols, here_on_mesh())
    split = map_of_blocks(maps, blocks)
    load_out[...] = sum(dot(split[b], load[b], (1, 1)) for b in range(blocks)).astype(BF16)
    for b in range(blocks):
        both[b] = beside_turned(load[b], -1)
    i = 0
    for o, out in zip(late, outs):
        for k, (x, y, d) in enumerate(sides[o]):
            out[pl.ds(k * wide, wide), :] = motion[x * cols + y]
            term = adjoint_product(coupling[i], both[x * cols + y])
            out[pl.ds((len(sides[o]) + k) * wide, wide), :] = term.astype(BF16)
            i += 1


def pressure_kernel(n_gx, hydro_ref, load_panels, *refs):
    pieces, (out_far, gathered, out, leave) = refs[:n_gx], refs[n_gx:]
    me = lax.axis_index("gx")
    panels, wide = load_panels.shape
    for step in range(n_gx):
        start = pl.multiple_of(source(me, step, n_gx) * panels, panels)
        gathered[0, pl.ds(start, panels), :] = pieces[step][...]
        gathered[1, pl.ds(start, panels), :] = times_i(pieces[step][...].astype(F32), 1).astype(BF16)
    fields = gathered[...].reshape(-1, wide)
    tiles = out.shape[0]
    moves = []
    for i in range(2):
        here = pl.ds(i * tiles // 2, tiles // 2)
        rows = pl.ds(i * tiles // 2 * panels, tiles // 2 * panels)
        hydro = jnp.concatenate([hydro_ref[0, rows, :], hydro_ref[1, rows, :]], axis=1)
        out[here, :panels, :] = dot(hydro, fields, (1, 0)).astype(BF16).reshape(-1, panels, wide)
        out[here, panels:, :] = jnp.broadcast_to(load_panels[...], (tiles // 2, panels, wide))
        moves.append(pltpu.make_async_copy(out.at[here], out_far.at[here], leave.at[i]))
        moves[-1].start()
    for move in moves:
        move.wait()


def reaction_kernel(n_gx, hydro_ref, arrived, *refs):
    outs, (reacted,) = refs[:n_gx], refs[n_gx:]
    me = lax.axis_index("gx")
    panels = outs[0].shape[0]
    hydro = hydro_ref[...]
    loads = arrived[:, panels:, :].reshape(hydro.shape[1], -1)
    real = dot(hydro[0], loads, (0, 0))
    imag = dot(hydro[1], loads, (0, 0))
    reacted[...] = real - times_i(imag, 1)
    for step in range(n_gx):
        start = pl.multiple_of(target(me, step, n_gx) * panels, panels)
        outs[step][...] = reacted[pl.ds(start, panels), :]


def add_side(side, valid, received, couplings, residual, multiplier):
    wide = residual.shape[1]
    for k, (b, x, y, d) in enumerate(side):
        motion = received[pl.ds(k * wide, wide), :]
        residual[b] += joined(forward_parts(couplings(k, x, y, d), motion), 1)
        terms = received[pl.ds((len(side) + k) * wide, wide), :]
        multiplier[b] += valid * terms.astype(F32)


def placed(cols, sides):
    return [[(x * cols + y, x, y, d) for x, y, d in side] for side in sides]


def beyond(spot, sizes, o):
    n, me = sizes[o // 2], spot[o // 2]
    other = target(me, 1 + o % 2, n)
    return (abs(me - other) <= 1).astype(F32) if n > 2 else F32(1 - o % 2)


def interior_kernel(rows, cols, sizes, early, late, joints_far, motion_far, load_far, excitation_far, *refs):
    coupling_far, received, refs = refs[0], refs[1 : 1 + len(early)], refs[1 + len(early) :]
    residual_out, multiplier_out, own_far, outer, motion, load, excitation, coupling, own, joints, arrive, leave = refs
    blocks, spot = rows * cols, here_on_mesh()
    moves = [
        pltpu.make_async_copy(motion_far, motion, arrive.at[0]),
        pltpu.make_async_copy(load_far, load, arrive.at[1]),
    ]
    for b in range(blocks):
        moves.append(pltpu.make_async_copy(coupling_far.at[b], coupling.at[b], arrive.at[2 + b]))
    moves.append(pltpu.make_async_copy(excitation_far, excitation, arrive.at[2 + blocks]))
    moves.append(pltpu.make_async_copy(joints_far, joints, arrive.at[3 + blocks]))
    for move in moves:
        move.start()
    sides = edges(rows, cols, spot)
    later = fetch_edges(late, sides, cols, coupling_far, outer, arrive, 4 + blocks)
    moves[0].wait()
    moving = [beside_turned(motion[b], 1) for b in range(blocks)]
    moves[1].wait()
    loads = [beside_turned(load[b], -1) for b in range(blocks)]
    sent = []
    for b in range(blocks):
        moves[2 + b].wait()
        own[b] = forward_product(coupling[b, 0], moving[b])
        sent.append(pltpu.make_async_copy(own.at[b], own_far.at[b], leave.at[b]))
        sent[-1].start()
    moves[2 + blocks].wait()
    moves[3 + blocks].wait()
    for x in range(rows):
        for y in range(cols):
            b = x * cols + y
            forward, adjoint = [], [(loads[b], coupling[b, 0])]
            for d in range(4):
                nx, ny = x + OFFSETS[d][0], y + OFFSETS[d][1]
                if 0 <= nx < rows and 0 <= ny < cols:
                    n = nx * cols + ny
                    forward.append((moving[n], coupling[b, d + 1] * joints[x, y, d].astype(BF16)))
                    adjoint.append((loads[n], coupling[n, (d ^ 1) + 1] * joints[nx, ny, d ^ 1].astype(BF16)))
            residual = own[b] - excitation[b].astype(F32)
            if forward:
                fields = jnp.concatenate([f for f, _ in forward], axis=1)
                matrix = jnp.concatenate([c[part] for _, c in forward for part in range(2)], axis=1)
                residual = residual + dot(fields, matrix, (1, 1))
            residual_out[b] = residual
            fields = jnp.concatenate([f for f, _ in adjoint], axis=1)
            matrix = jnp.concatenate([c[part] for _, c in adjoint for part in range(2)], axis=0)
            multiplier_out[b] = dot(fields, matrix, (1, 0))
    for o, ref in zip(early, received):
        valid = beyond(spot, sizes, o)

        def linked(k, x, y, d, valid=valid):
            return coupling[x * cols + y, d + 1] * (valid * joints[x, y, d].astype(F32)).astype(BF16)

        add_side(placed(cols, sides)[o], valid, ref, linked, residual_out, multiplier_out)
    i = 0
    for o in late:
        valid = beyond(spot, sizes, o)
        for x, y, d in sides[o]:
            later[i].wait()
            outer[i] = outer[i] * (valid * joints[x, y, d].astype(F32)).astype(BF16)
            i += 1
    for move in sent:
        move.wait()


def boundary_kernel(rows, cols, sizes, lift, late, map_ref, coupling, residual, multiplier, arrived, *refs):
    received, (residual_out, multiplier_out, full, leave) = refs[: len(late)], refs[len(late) :]
    blocks, unknowns, spot = rows * cols, residual.shape[2], here_on_mesh()
    panels = map_ref.shape[0] // blocks
    maps = jnp.concatenate(map_of_blocks(map_ref, blocks), axis=1)
    pressure = jnp.sum(arrived[:, :panels, :].astype(F32), axis=0).astype(BF16)
    forces = lift * dot(pressure, maps, (0, 0))
    for b in range(blocks):
        full[b] = residual[b] + forces[:, b * unknowns : (b + 1) * unknowns]
        multiplier_out[b] = multiplier[b]
    sides, first = placed(cols, edges(rows, cols, spot)), 0
    for o, ref in zip(late, received):
        at = first
        add_side(sides[o], beyond(spot, sizes, o), ref, lambda k, x, y, d: coupling[at + k], full, multiplier_out)
        first += len(sides[o])
    move = pltpu.make_async_copy(full, residual_out, leave)
    move.start()
    move.wait()


def final_kernel(rows, cols, lift, map_ref, multiplier, own, *refs):
    reactions, (multiplier_out, sensitivity_out, full, sensitivity, leave) = refs[:-5], refs[-5:]
    blocks = rows * cols
    unknowns = own.shape[2]
    maps = jnp.concatenate(map_of_blocks(map_ref, blocks), axis=1)
    reaction = sum(r[...].astype(F32) for r in reactions).astype(BF16)
    scale = 1.0 / math.sqrt(own.shape[1] // 2 * unknowns)
    forces = lift * dot(reaction, maps, (0, 0))
    sent, sums = [], []
    for b in range(blocks):
        value = multiplier[b] + forces[:, b * unknowns : (b + 1) * unknowns]
        full[b] = value
        sent.append(pltpu.make_async_copy(full.at[b], multiplier_out.at[b], leave.at[b]))
        sent[-1].start()
        sums.append(jnp.sum((value * own[b]).reshape(-1, 8, unknowns), axis=0))
    for b in range(blocks):
        sensitivity[b // cols, b % cols] = jnp.sum(sums[b]) * scale
    sent.append(pltpu.make_async_copy(sensitivity, sensitivity_out, leave.at[blocks]))
    sent[-1].start()
    for move in sent:
        move.wait()


def cost(flops, bytes_accessed):
    return pl.CostEstimate(flops=int(flops), bytes_accessed=int(bytes_accessed), transcendentals=0)


def shaped(dtype, *shape):
    return jax.ShapeDtypeStruct(shape, dtype)


def params(mebibytes):
    return pltpu.CompilerParams(vmem_limit_bytes=mebibytes * 1024 * 1024)


DMA = pltpu.SemaphoreType.DMA


def on_device(plate_motion, adjoint_load, excitation, coupling, joints, hydro, panel_map):
    rows, cols, cases, _, unknowns = plate_motion.shape
    panels = panel_map.shape[0]
    blocks, wide = rows * cols, 2 * cases
    n_gx, n_gy = lax.axis_size("gx"), lax.axis_size("gy")
    motion = plate_motion.reshape(blocks, wide, unknowns)
    load = adjoint_load.reshape(blocks, wide, unknowns)
    force = excitation.reshape(blocks, wide, unknowns)
    coupling = coupling.reshape(blocks, 5, 2, unknowns, unknowns)
    panel_map = panel_map.reshape(panels * blocks, unknowns)
    lift = math.sqrt(blocks * unknowns / panels)
    block_flops = 2 * wide * unknowns * unknowns * 2
    field = (blocks, wide, unknowns)

    counts = [cols, cols, rows, rows]
    early, late = (3,), (0, 1, 2)
    few, many = sum(counts[o] for o in early), sum(counts[o] for o in late)
    pair = (2, unknowns, unknowns)
    motion_panels, *payloads, near_motion, near_load, near_map, near_coupling = pl.pallas_call(
        functools.partial(panels_kernel, rows, cols, early, late),
        name="panels",
        out_shape=[pltpu.VMEM((panels, wide), BF16)]
        + [pltpu.VMEM((2 * counts[o] * wide, unknowns), BF16) for o in early]
        + [pltpu.VMEM(field, BF16)] * 2
        + [pltpu.VMEM(panel_map.shape, BF16), pltpu.VMEM((many,) + pair, BF16)],
        in_specs=[FAR] * 5,
        out_specs=[WHOLE] * (5 + len(early)),
        scratch_shapes=[
            pltpu.VMEM((few,) + pair, BF16),
            pltpu.SMEM(joints.shape, jnp.int32),
            DMA((4 + few + many,)),
        ],
        compiler_params=params(16),
        cost_estimate=cost(4 * blocks * wide * unknowns * panels, 4 * blocks * wide * unknowns),
    )(far(joints), far(motion), far(load), far(coupling), far(panel_map))
    pieces = [motion_panels] + [exchange(motion_panels, step) for step in range(1, n_gx)]
    fourth = exchange_sides(payloads[0], 1, 2)

    load_panels, *payloads = pl.pallas_call(
        functools.partial(edges_kernel, rows, cols, late),
        name="edges",
        out_shape=[pltpu.VMEM((panels, wide), BF16)]
        + [pltpu.VMEM((2 * counts[o] * wide, unknowns), BF16) for o in late],
        in_specs=[WHOLE] * 4,
        out_specs=[WHOLE] * (1 + len(late)),
        scratch_shapes=[pltpu.VMEM((blocks, wide, 2 * unknowns), BF16)],
        compiler_params=params(16),
        cost_estimate=cost(many * block_flops, 4 * blocks * wide * unknowns + 12 * blocks * unknowns**2),
    )(near_motion, near_load, near_map, near_coupling)
    (*payloads, load_panels) = lax.optimization_barrier((*payloads, load_panels))
    first, second = exchange_sides(payloads[0], 0, 1), exchange_sides(payloads[1], 0, 2)
    third = exchange_sides(payloads[2], 1, 1)

    parts = pl.pallas_call(
        functools.partial(pressure_kernel, n_gx),
        name="pressure",
        out_shape=pltpu.HBM((n_gy, 2 * panels, wide), BF16),
        in_specs=[WHOLE] * (2 + n_gx),
        out_specs=FAR,
        scratch_shapes=[pltpu.VMEM((2, n_gx * panels, wide), BF16), pltpu.VMEM((n_gy, 2 * panels, wide), BF16), DMA((2,))],
        compiler_params=params(16),
        cost_estimate=cost(2 * hydro.size * wide, 2 * hydro.size),
    )(hydro, load_panels, *pieces)
    parts, fourth = lax.optimization_barrier((parts, fourth))
    arrived = lax.all_to_all(parts, "gy", 0, 0, tiled=True)

    residual, multiplier, own, outer = pl.pallas_call(
        functools.partial(interior_kernel, rows, cols, (n_gx, n_gy), early, late),
        name="interior",
        out_shape=[pltpu.VMEM(field, F32)] * 2
        + [pltpu.HBM(field, F32), pltpu.VMEM((many,) + pair, BF16)],
        in_specs=[FAR] * 5 + [WHOLE] * len(early),
        out_specs=[WHOLE] * 2 + [FAR, WHOLE],
        scratch_shapes=[pltpu.VMEM(field, BF16)] * 3
        + [
            pltpu.VMEM(coupling.shape, BF16),
            pltpu.VMEM(field, F32),
            pltpu.SMEM(joints.shape, jnp.int32),
            DMA((4 + blocks + many,)),
            DMA((blocks,)),
        ],
        compiler_params=params(16),
        cost_estimate=cost(6 * blocks * block_flops, 20 * blocks * unknowns**2 + 18 * blocks * wide * unknowns),
    )(far(joints), far(motion), far(load), far(force), far(coupling), fourth)
    arrived, residual, multiplier, own, outer = lax.optimization_barrier((arrived, residual, multiplier, own, outer))

    reaction_parts = pl.pallas_call(
        functools.partial(reaction_kernel, n_gx),
        name="reaction",
        out_shape=[pltpu.VMEM((panels, wide), F32)] * n_gx,
        in_specs=[WHOLE] * 2,
        out_specs=[WHOLE] * n_gx,
        scratch_shapes=[pltpu.VMEM((n_gx * panels, wide), F32)],
        compiler_params=params(16),
        cost_estimate=cost(2 * hydro.size * wide, 2 * hydro.size),
    )(hydro, arrived)
    reactions = [reaction_parts[0]] + [exchange(reaction_parts[step], step) for step in range(1, n_gx)]

    residual, multiplier = pl.pallas_call(
        functools.partial(boundary_kernel, rows, cols, (n_gx, n_gy), lift, late),
        name="boundary",
        out_shape=[pltpu.HBM(field, F32), pltpu.VMEM(field, F32)],
        in_specs=[WHOLE] * (5 + len(late)),
        out_specs=[FAR, WHOLE],
        scratch_shapes=[pltpu.VMEM(field, F32), DMA],
        compiler_params=params(16),
        cost_estimate=cost(4 * blocks * block_flops, 10 * blocks * unknowns**2 + 18 * blocks * wide * unknowns),
    )(panel_map, outer, residual, multiplier, arrived, first, second, third)

    multiplier, sensitivity = pl.pallas_call(
        functools.partial(final_kernel, rows, cols, lift),
        name="final",
        out_shape=[pltpu.HBM(field, F32), pltpu.HBM((rows, cols), F32)],
        in_specs=[WHOLE] * (3 + n_gx),
        out_specs=[FAR, FAR],
        scratch_shapes=[pltpu.VMEM(field, F32), pltpu.SMEM((rows, cols), F32), DMA((blocks + 1,))],
        compiler_params=params(16),
        cost_estimate=cost(4 * blocks * wide * unknowns * panels, 20 * blocks * wide * unknowns),
    )(panel_map, multiplier, own, *reactions)
    shape = plate_motion.shape
    return residual.reshape(shape), multiplier.reshape(shape), sensitivity


def solution(mesh):
    field = P("gx", "gy", None, None, None)
    placed = (
        field,
        field,
        field,
        P("gx", "gy", None, None, None, None),
        P("gx", "gy", None),
        P(None, "gx", "gy"),
        P(("gx", "gy"), None, None, None),
    )
    return jax.shard_map(on_device, mesh=mesh, in_specs=placed, out_specs=(field, field, P("gx", "gy")), check_vma=False)
```

```python
import functools
import math

import jax
import jax.numpy as jnp
from jax import lax
from jax.experimental import pallas as pl
from jax.experimental.pallas import tpu as pltpu
from jax.sharding import PartitionSpec as P


F32 = jnp.float32
BF16 = jnp.bfloat16
OFFSETS = ((-1, 0), (1, 0), (0, -1), (0, 1))
WHOLE = pl.BlockSpec(memory_space=pltpu.VMEM)
FAR = pl.BlockSpec(memory_space=pltpu.HBM)


def dot(a, b, over):
    return lax.dot_general(a, b, ((over[:1], over[1:]), ((), ())), preferred_element_type=F32)


def times_i(field, axis):
    shape = field.shape
    if axis == 0:
        field, axis = field.reshape(-1, 8, shape[1]), 1
        place = lax.broadcasted_iota(jnp.int32, (1, 8, shape[1]), 1)
    else:
        place = lax.broadcasted_iota(jnp.int32, (1, shape[1]), 1)
    size = field.shape[axis]
    after = pltpu.roll(field, size - 1, axis)
    before = pltpu.roll(field, 1, axis)
    return jnp.where((place & 1) == 0, -after, before).reshape(shape)


def forward_parts(coupling, motion):
    return dot(motion, coupling.reshape(-1, coupling.shape[-1]), (1, 1))


def adjoint_parts(coupling, load):
    return dot(load, jnp.concatenate([coupling[0], coupling[1]], axis=1), (1, 0))


def beside_turned(field, sign):
    turned = times_i(field.astype(F32), 0)
    return jnp.concatenate([field, (turned if sign > 0 else -turned).astype(BF16)], axis=1)


def forward_product(coupling, both):
    return dot(both, jnp.concatenate([coupling[0], coupling[1]], axis=1), (1, 1))


def adjoint_product(coupling, both):
    return dot(both, coupling.reshape(-1, coupling.shape[-1]), (1, 0))


def joined(parts, sign):
    half = parts.shape[1] // 2
    turned = times_i(parts[:, half:], 0)
    return parts[:, :half] + turned if sign > 0 else parts[:, :half] - turned


def map_of_blocks(map_ref, blocks):
    rows = map_ref.shape[0]
    panels = rows // blocks
    row = lax.broadcasted_iota(jnp.int32, (panels, rows), 0)
    column = lax.broadcasted_iota(jnp.int32, (panels, rows), 1)
    whole = map_ref[...]
    out = []
    for b in range(blocks):
        pick = (column == row * blocks + b).astype(F32).astype(BF16)
        out.append(dot(pick, whole, (1, 0)).astype(BF16))
    return out


def target(i, step, n):
    if step == 0:
        return i
    if step == 1:
        return i ^ 1
    if step == 2:
        return (((i + 1) ^ 1) + n - 1) % n
    return (i + step - 1) % n


def source(i, step, n):
    return target(i, step, n) if step < 3 else (i + n + 1 - step) % n


def exchange(x, step):
    n = lax.axis_size("gx")
    return lax.ppermute(x, "gx", [(i, target(i, step, n)) for i in range(n)])


def exchange_sides(x, axis, step):
    sizes = lax.axis_size("gx"), lax.axis_size("gy")
    pairs = []
    for x_at in range(sizes[0]):
        for y_at in range(sizes[1]):
            there = [x_at, y_at]
            other = target(there[axis], step, sizes[axis])
            if axis == 0 or abs(other - there[axis]) == 1:
                there[axis] = other
            else:
                there[0] ^= 1
            pairs.append((x_at * sizes[1] + y_at, there[0] * sizes[1] + there[1]))
    return lax.ppermute(x, ("gx", "gy"), pairs)


def far(x):
    return pltpu.with_memory_space_constraint(x, pltpu.HBM)


def edges(rows, cols, spot):
    sides = []
    for axis in range(2):
        even = 1 - spot[axis] % 2
        for up in (even, 1 - even):
            if axis == 0:
                sides.append([(up * (rows - 1), y, up) for y in range(cols)])
            else:
                sides.append([(x, up * (cols - 1), 2 + up) for x in range(rows)])
    return sides


def here_on_mesh():
    return lax.axis_index("gx"), lax.axis_index("gy")


def fetch_edges(which, sides, cols, coupling_far, coupling, arrive, first):
    moves = []
    for o in which:
        for x, y, d in sides[o]:
            i = len(moves)
            moves.append(pltpu.make_async_copy(coupling_far.at[x * cols + y, d + 1], coupling.at[i], arrive.at[first + i]))
            moves[-1].start()
    return moves


def panels_kernel(rows, cols, early, late, joints_far, motion_far, load_far, coupling_far, map_far, *refs):
    motion_out, outs, refs = refs[0], refs[1 : 1 + len(early)], refs[1 + len(early) :]
    motion, load, maps, near_coupling, coupling, joints, arrive = refs
    moves = [
        pltpu.make_async_copy(map_far, maps, arrive.at[0]),
        pltpu.make_async_copy(motion_far, motion, arrive.at[1]),
        pltpu.make_async_copy(load_far, load, arrive.at[2]),
        pltpu.make_async_copy(joints_far, joints, arrive.at[3]),
    ]
    for move in moves:
        move.start()
    sides = edges(rows, cols, here_on_mesh())
    more = fetch_edges(early, sides, cols, coupling_far, coupling, arrive, 4)
    later = fetch_edges(late, sides, cols, coupling_far, near_coupling, arrive, 4 + len(more))
    blocks, wide = motion.shape[:2]
    moves[0].wait()
    split = map_of_blocks(maps, blocks)
    moves[1].wait()
    motion_out[...] = sum(dot(split[b], motion[b], (1, 1)) for b in range(blocks)).astype(BF16)
    moves[2].wait()
    moves[3].wait()
    i = 0
    for o, out in zip(early, outs):
        for k, (x, y, d) in enumerate(sides[o]):
            out[pl.ds(k * wide, wide), :] = motion[x * cols + y]
            more[i].wait()
            matrix = coupling[i] * joints[x, y, d].astype(BF16)
            term = joined(adjoint_parts(matrix, load[x * cols + y]), -1)
            out[pl.ds((len(sides[o]) + k) * wide, wide), :] = term.astype(BF16)
            i += 1
    i = 0
    for o in late:
        for x, y, d in sides[o]:
            later[i].wait()
            near_coupling[i] = near_coupling[i] * joints[x, y, d].astype(BF16)
            i += 1


def edges_kernel(rows, cols, late, motion, load, maps, coupling, *refs):
    load_out, outs, (both,) = refs[0], refs[1 : 1 + len(late)], refs[1 + len(late) :]
    blocks, wide = motion.shape[:2]
    sides = edges(rows, cols, here_on_mesh())
    split = map_of_blocks(maps, blocks)
    load_out[...] = sum(dot(split[b], load[b], (1, 1)) for b in range(blocks)).astype(BF16)
    for b in range(blocks):
        both[b] = beside_turned(load[b], -1)
    i = 0
    for o, out in zip(late, outs):
        for k, (x, y, d) in enumerate(sides[o]):
            out[pl.ds(k * wide, wide), :] = motion[x * cols + y]
            term = adjoint_product(coupling[i], both[x * cols + y])
            out[pl.ds((len(sides[o]) + k) * wide, wide), :] = term.astype(BF16)
            i += 1


def pressure_kernel(n_gx, hydro_ref, load_panels, *refs):
    pieces, (out_far, gathered, out, leave) = refs[:n_gx], refs[n_gx:]
    me = lax.axis_index("gx")
    panels, wide = load_panels.shape
    for step in range(n_gx):
        start = pl.multiple_of(source(me, step, n_gx) * panels, panels)
        gathered[0, pl.ds(start, panels), :] = pieces[step][...]
        gathered[1, pl.ds(start, panels), :] = times_i(pieces[step][...].astype(F32), 1).astype(BF16)
    fields = gathered[...].reshape(-1, wide)
    tiles = out.shape[0]
    moves = []
    for i in range(2):
        here = pl.ds(i * tiles // 2, tiles // 2)
        rows = pl.ds(i * tiles // 2 * panels, tiles // 2 * panels)
        hydro = jnp.concatenate([hydro_ref[0, rows, :], hydro_ref[1, rows, :]], axis=1)
        out[here, :panels, :] = dot(hydro, fields, (1, 0)).astype(BF16).reshape(-1, panels, wide)
        out[here, panels:, :] = jnp.broadcast_to(load_panels[...], (tiles // 2, panels, wide))
        moves.append(pltpu.make_async_copy(out.at[here], out_far.at[here], leave.at[i]))
        moves[-1].start()
    for move in moves:
        move.wait()


def reaction_kernel(n_gx, hydro_ref, arrived, *refs):
    outs, (reacted,) = refs[:n_gx], refs[n_gx:]
    me = lax.axis_index("gx")
    panels = outs[0].shape[0]
    hydro = hydro_ref[...]
    loads = arrived[:, panels:, :].reshape(hydro.shape[1], -1)
    real = dot(hydro[0], loads, (0, 0))
    imag = dot(hydro[1], loads, (0, 0))
    reacted[...] = real - times_i(imag, 1)
    for step in range(n_gx):
        start = pl.multiple_of(target(me, step, n_gx) * panels, panels)
        outs[step][...] = reacted[pl.ds(start, panels), :]


def add_side(side, valid, received, couplings, residual, multiplier):
    wide = residual.shape[1]
    for k, (b, x, y, d) in enumerate(side):
        motion = received[pl.ds(k * wide, wide), :]
        residual[b] += joined(forward_parts(couplings(k, x, y, d), motion), 1)
        terms = received[pl.ds((len(side) + k) * wide, wide), :]
        multiplier[b] += valid * terms.astype(F32)


def placed(cols, sides):
    return [[(x * cols + y, x, y, d) for x, y, d in side] for side in sides]


def beyond(spot, sizes, o):
    n, me = sizes[o // 2], spot[o // 2]
    other = target(me, 1 + o % 2, n)
    return (abs(me - other) <= 1).astype(F32) if n > 2 else F32(1 - o % 2)


def interior_kernel(rows, cols, sizes, early, late, joints_far, motion_far, load_far, excitation_far, *refs):
    coupling_far, received, refs = refs[0], refs[1 : 1 + len(early)], refs[1 + len(early) :]
    residual_out, multiplier_out, own_far, outer, motion, load, excitation, coupling, own, joints, arrive, leave = refs
    blocks, spot = rows * cols, here_on_mesh()
    moves = [
        pltpu.make_async_copy(motion_far, motion, arrive.at[0]),
        pltpu.make_async_copy(load_far, load, arrive.at[1]),
    ]
    for b in range(blocks):
        moves.append(pltpu.make_async_copy(coupling_far.at[b], coupling.at[b], arrive.at[2 + b]))
    moves.append(pltpu.make_async_copy(excitation_far, excitation, arrive.at[2 + blocks]))
    moves.append(pltpu.make_async_copy(joints_far, joints, arrive.at[3 + blocks]))
    for move in moves:
        move.start()
    sides = edges(rows, cols, spot)
    later = fetch_edges(late, sides, cols, coupling_far, outer, arrive, 4 + blocks)
    moves[0].wait()
    moving = [beside_turned(motion[b], 1) for b in range(blocks)]
    moves[1].wait()
    loads = [beside_turned(load[b], -1) for b in range(blocks)]
    sent = []
    for b in range(blocks):
        moves[2 + b].wait()
        own[b] = forward_product(coupling[b, 0], moving[b])
        sent.append(pltpu.make_async_copy(own.at[b], own_far.at[b], leave.at[b]))
        sent[-1].start()
    moves[2 + blocks].wait()
    moves[3 + blocks].wait()
    for x in range(rows):
        for y in range(cols):
            b = x * cols + y
            forward, adjoint = [], [(loads[b], coupling[b, 0])]
            for d in range(4):
                nx, ny = x + OFFSETS[d][0], y + OFFSETS[d][1]
                if 0 <= nx < rows and 0 <= ny < cols:
                    n = nx * cols + ny
                    forward.append((moving[n], coupling[b, d + 1] * joints[x, y, d].astype(BF16)))
                    adjoint.append((loads[n], coupling[n, (d ^ 1) + 1] * joints[nx, ny, d ^ 1].astype(BF16)))
            residual = own[b] - excitation[b].astype(F32)
            if forward:
                fields = jnp.concatenate([f for f, _ in forward], axis=1)
                matrix = jnp.concatenate([c[part] for _, c in forward for part in range(2)], axis=1)
                residual = residual + dot(fields, matrix, (1, 1))
            residual_out[b] = residual
            fields = jnp.concatenate([f for f, _ in adjoint], axis=1)
            matrix = jnp.concatenate([c[part] for _, c in adjoint for part in range(2)], axis=0)
            multiplier_out[b] = dot(fields, matrix, (1, 0))
    for o, ref in zip(early, received):
        valid = beyond(spot, sizes, o)

        def linked(k, x, y, d, valid=valid):
            return coupling[x * cols + y, d + 1] * (valid * joints[x, y, d].astype(F32)).astype(BF16)

        add_side(placed(cols, sides)[o], valid, ref, linked, residual_out, multiplier_out)
    i = 0
    for o in late:
        valid = beyond(spot, sizes, o)
        for x, y, d in sides[o]:
            later[i].wait()
            outer[i] = outer[i] * (valid * joints[x, y, d].astype(F32)).astype(BF16)
            i += 1
    for move in sent:
        move.wait()


def boundary_kernel(rows, cols, sizes, lift, which, map_ref, coupling, residual, multiplier, arrived, *refs):
    received, (residual_out, multiplier_out) = refs[: len(which)], refs[len(which) :]
    blocks, unknowns, spot = rows * cols, residual.shape[2], here_on_mesh()
    panels = map_ref.shape[0] // blocks
    maps = jnp.concatenate(map_of_blocks(map_ref, blocks), axis=1)
    pressure = jnp.sum(arrived[:, :panels, :].astype(F32), axis=0).astype(BF16)
    forces = lift * dot(pressure, maps, (0, 0))
    for b in range(blocks):
        residual_out[b] = residual[b] + forces[:, b * unknowns : (b + 1) * unknowns]
        multiplier_out[b] = multiplier[b]
    sides, first = placed(cols, edges(rows, cols, spot)), 0
    for o, ref in zip(which, received):
        at = first
        add_side(sides[o], beyond(spot, sizes, o), ref, lambda k, x, y, d: coupling[at + k], residual_out, multiplier_out)
        first += len(sides[o])


def final_kernel(rows, cols, sizes, lift, which, first, map_ref, coupling, residual, multiplier, own, *refs):
    received, refs = refs[: len(which)], refs[len(which) :]
    reactions, (residual_out, multiplier_out, sensitivity_out, full, sensitivity, leave) = refs[:-6], refs[-6:]
    blocks, spot = rows * cols, here_on_mesh()
    unknowns = own.shape[2]
    maps = jnp.concatenate(map_of_blocks(map_ref, blocks), axis=1)
    reaction = sum(r[...].astype(F32) for r in reactions).astype(BF16)
    scale = 1.0 / math.sqrt(own.shape[1] // 2 * unknowns)
    forces = lift * dot(reaction, maps, (0, 0))
    for b in range(blocks):
        full[0, b] = residual[b]
        full[1, b] = multiplier[b] + forces[:, b * unknowns : (b + 1) * unknowns]
    sides = placed(cols, edges(rows, cols, spot))
    for o, ref in zip(which, received):
        at = first
        add_side(sides[o], beyond(spot, sizes, o), ref, lambda k, x, y, d: coupling[at + k], full.at[0], full.at[1])
        first += len(sides[o])
    sent = [
        pltpu.make_async_copy(full.at[0], residual_out, leave.at[0]),
        pltpu.make_async_copy(full.at[1], multiplier_out, leave.at[1]),
    ]
    for move in sent:
        move.start()
    for b in range(blocks):
        total = jnp.sum((full[1, b] * own[b]).reshape(-1, 8, unknowns), axis=0)
        sensitivity[b // cols, b % cols] = jnp.sum(total) * scale
    sent.append(pltpu.make_async_copy(sensitivity, sensitivity_out, leave.at[2]))
    sent[-1].start()
    for move in sent:
        move.wait()


def cost(flops, bytes_accessed):
    return pl.CostEstimate(flops=int(flops), bytes_accessed=int(bytes_accessed), transcendentals=0)


def shaped(dtype, *shape):
    return jax.ShapeDtypeStruct(shape, dtype)


def params(mebibytes):
    return pltpu.CompilerParams(vmem_limit_bytes=mebibytes * 1024 * 1024)


DMA = pltpu.SemaphoreType.DMA


def on_device(plate_motion, adjoint_load, excitation, coupling, joints, hydro, panel_map):
    rows, cols, cases, _, unknowns = plate_motion.shape
    panels = panel_map.shape[0]
    blocks, wide = rows * cols, 2 * cases
    n_gx, n_gy = lax.axis_size("gx"), lax.axis_size("gy")
    motion = plate_motion.reshape(blocks, wide, unknowns)
    load = adjoint_load.reshape(blocks, wide, unknowns)
    force = excitation.reshape(blocks, wide, unknowns)
    coupling = coupling.reshape(blocks, 5, 2, unknowns, unknowns)
    panel_map = panel_map.reshape(panels * blocks, unknowns)
    lift = math.sqrt(blocks * unknowns / panels)
    block_flops = 2 * wide * unknowns * unknowns * 2
    field = (blocks, wide, unknowns)

    counts = [cols, cols, rows, rows]
    early, late = (3,), (0, 1, 2)
    few, many = sum(counts[o] for o in early), sum(counts[o] for o in late)
    pair = (2, unknowns, unknowns)
    motion_panels, *payloads, near_motion, near_load, near_map, near_coupling = pl.pallas_call(
        functools.partial(panels_kernel, rows, cols, early, late),
        name="panels",
        out_shape=[pltpu.VMEM((panels, wide), BF16)]
        + [pltpu.VMEM((2 * counts[o] * wide, unknowns), BF16) for o in early]
        + [pltpu.VMEM(field, BF16)] * 2
        + [pltpu.VMEM(panel_map.shape, BF16), pltpu.VMEM((many,) + pair, BF16)],
        in_specs=[FAR] * 5,
        out_specs=[WHOLE] * (5 + len(early)),
        scratch_shapes=[
            pltpu.VMEM((few,) + pair, BF16),
            pltpu.SMEM(joints.shape, jnp.int32),
            DMA((4 + few + many,)),
        ],
        compiler_params=params(16),
        cost_estimate=cost(4 * blocks * wide * unknowns * panels, 4 * blocks * wide * unknowns),
    )(far(joints), far(motion), far(load), far(coupling), far(panel_map))
    pieces = [motion_panels] + [exchange(motion_panels, step) for step in range(1, n_gx)]
    fourth = exchange_sides(payloads[0], 1, 2)

    load_panels, *payloads = pl.pallas_call(
        functools.partial(edges_kernel, rows, cols, late),
        name="edges",
        out_shape=[pltpu.VMEM((panels, wide), BF16)]
        + [pltpu.VMEM((2 * counts[o] * wide, unknowns), BF16) for o in late],
        in_specs=[WHOLE] * 4,
        out_specs=[WHOLE] * (1 + len(late)),
        scratch_shapes=[pltpu.VMEM((blocks, wide, 2 * unknowns), BF16)],
        compiler_params=params(16),
        cost_estimate=cost(many * block_flops, 4 * blocks * wide * unknowns + 12 * blocks * unknowns**2),
    )(near_motion, near_load, near_map, near_coupling)
    (*payloads, load_panels) = lax.optimization_barrier((*payloads, load_panels))
    parts = pl.pallas_call(
        functools.partial(pressure_kernel, n_gx),
        name="pressure",
        out_shape=pltpu.HBM((n_gy, 2 * panels, wide), BF16),
        in_specs=[WHOLE] * (2 + n_gx),
        out_specs=FAR,
        scratch_shapes=[pltpu.VMEM((2, n_gx * panels, wide), BF16), pltpu.VMEM((n_gy, 2 * panels, wide), BF16), DMA((2,))],
        compiler_params=params(16),
        cost_estimate=cost(2 * hydro.size * wide, 2 * hydro.size),
    )(hydro, load_panels, *pieces)
    arrived = lax.all_to_all(parts, "gy", 0, 0, tiled=True)
    (*payloads, fourth) = lax.optimization_barrier((*payloads, fourth))
    third = exchange_sides(payloads[2], 1, 1)
    second = exchange_sides(payloads[1], 0, 2)
    first = exchange_sides(payloads[0], 0, 1)

    residual, multiplier, own, outer = pl.pallas_call(
        functools.partial(interior_kernel, rows, cols, (n_gx, n_gy), early, late),
        name="interior",
        out_shape=[pltpu.VMEM(field, F32)] * 2
        + [pltpu.HBM(field, F32), pltpu.VMEM((many,) + pair, BF16)],
        in_specs=[FAR] * 5 + [WHOLE] * len(early),
        out_specs=[WHOLE] * 2 + [FAR, WHOLE],
        scratch_shapes=[pltpu.VMEM(field, BF16)] * 3
        + [
            pltpu.VMEM(coupling.shape, BF16),
            pltpu.VMEM(field, F32),
            pltpu.SMEM(joints.shape, jnp.int32),
            DMA((4 + blocks + many,)),
            DMA((blocks,)),
        ],
        compiler_params=params(16),
        cost_estimate=cost(6 * blocks * block_flops, 20 * blocks * unknowns**2 + 18 * blocks * wide * unknowns),
    )(far(joints), far(motion), far(load), far(force), far(coupling), fourth)
    arrived, residual, multiplier, own, outer = lax.optimization_barrier((arrived, residual, multiplier, own, outer))

    reaction_parts = pl.pallas_call(
        functools.partial(reaction_kernel, n_gx),
        name="reaction",
        out_shape=[pltpu.VMEM((panels, wide), F32)] * n_gx,
        in_specs=[WHOLE] * 2,
        out_specs=[WHOLE] * n_gx,
        scratch_shapes=[pltpu.VMEM((n_gx * panels, wide), F32)],
        compiler_params=params(16),
        cost_estimate=cost(2 * hydro.size * wide, 2 * hydro.size),
    )(hydro, arrived)
    reactions = [exchange(reaction_parts[step], step) for step in reversed(range(1, n_gx))] + [reaction_parts[0]]

    residual, multiplier = pl.pallas_call(
        functools.partial(boundary_kernel, rows, cols, (n_gx, n_gy), lift, late[:2]),
        name="boundary",
        out_shape=[pltpu.VMEM(field, F32)] * 2,
        in_specs=[WHOLE] * 7,
        out_specs=[WHOLE] * 2,
        compiler_params=params(16),
        cost_estimate=cost(4 * blocks * block_flops, 10 * blocks * unknowns**2 + 18 * blocks * wide * unknowns),
    )(panel_map, outer, residual, multiplier, arrived, first, second)

    done = counts[late[0]] + counts[late[1]]
    residual, multiplier, sensitivity = pl.pallas_call(
        functools.partial(final_kernel, rows, cols, (n_gx, n_gy), lift, late[2:], done),
        name="final",
        out_shape=[pltpu.HBM(field, F32), pltpu.HBM(field, F32), pltpu.HBM((rows, cols), F32)],
        in_specs=[WHOLE] * (6 + n_gx),
        out_specs=[FAR] * 3,
        scratch_shapes=[pltpu.VMEM((2,) + field, F32), pltpu.SMEM((rows, cols), F32), DMA((3,))],
        compiler_params=params(16),
        cost_estimate=cost(4 * blocks * wide * unknowns * panels, 20 * blocks * wide * unknowns),
    )(panel_map, outer, residual, multiplier, own, third, *reactions)
    shape = plate_motion.shape
    return residual.reshape(shape), multiplier.reshape(shape), sensitivity


def solution(mesh):
    field = P("gx", "gy", None, None, None)
    placed = (
        field,
        field,
        field,
        P("gx", "gy", None, None, None, None),
        P("gx", "gy", None),
        P(None, "gx", "gy"),
        P(("gx", "gy"), None, None, None),
    )
    return jax.shard_map(on_device, mesh=mesh, in_specs=placed, out_specs=(field, field, P("gx", "gy")), check_vma=False)
```

```python
import functools
import math

import jax
import jax.numpy as jnp
from jax import lax
from jax.experimental import pallas as pl
from jax.experimental.pallas import tpu as pltpu
from jax.sharding import PartitionSpec as P


F32 = jnp.float32
BF16 = jnp.bfloat16
OFFSETS = ((-1, 0), (1, 0), (0, -1), (0, 1))
WHOLE = pl.BlockSpec(memory_space=pltpu.VMEM)
FAR = pl.BlockSpec(memory_space=pltpu.HBM)


def dot(a, b, over):
    return lax.dot_general(a, b, ((over[:1], over[1:]), ((), ())), preferred_element_type=F32)


def times_i(field, axis):
    shape = field.shape
    if axis == 0:
        field, axis = field.reshape(-1, 8, shape[1]), 1
        place = lax.broadcasted_iota(jnp.int32, (1, 8, shape[1]), 1)
    else:
        place = lax.broadcasted_iota(jnp.int32, (1, shape[1]), 1)
    size = field.shape[axis]
    after = pltpu.roll(field, size - 1, axis)
    before = pltpu.roll(field, 1, axis)
    return jnp.where((place & 1) == 0, -after, before).reshape(shape)


def forward_parts(coupling, motion):
    return dot(motion, coupling.reshape(-1, coupling.shape[-1]), (1, 1))


def adjoint_parts(coupling, load):
    return dot(load, jnp.concatenate([coupling[0], coupling[1]], axis=1), (1, 0))


def beside_turned(field, sign):
    turned = times_i(field.astype(F32), 0)
    return jnp.concatenate([field, (turned if sign > 0 else -turned).astype(BF16)], axis=1)


def forward_product(coupling, both):
    return dot(both, jnp.concatenate([coupling[0], coupling[1]], axis=1), (1, 1))


def adjoint_product(coupling, both):
    return dot(both, coupling.reshape(-1, coupling.shape[-1]), (1, 0))


def joined(parts, sign):
    half = parts.shape[1] // 2
    turned = times_i(parts[:, half:], 0)
    return parts[:, :half] + turned if sign > 0 else parts[:, :half] - turned


def map_of_blocks(map_ref, blocks):
    rows = map_ref.shape[0]
    panels = rows // blocks
    row = lax.broadcasted_iota(jnp.int32, (panels, rows), 0)
    column = lax.broadcasted_iota(jnp.int32, (panels, rows), 1)
    whole = map_ref[...]
    out = []
    for b in range(blocks):
        pick = (column == row * blocks + b).astype(F32).astype(BF16)
        out.append(dot(pick, whole, (1, 0)).astype(BF16))
    return out


def target(i, step, n):
    if step == 0:
        return i
    if step == 1:
        return i ^ 1
    if step == 2:
        return (((i + 1) ^ 1) + n - 1) % n
    return (i + step - 1) % n


def source(i, step, n):
    return target(i, step, n) if step < 3 else (i + n + 1 - step) % n


def exchange(x, step):
    n = lax.axis_size("gx")
    return lax.ppermute(x, "gx", [(i, target(i, step, n)) for i in range(n)])


def exchange_sides(x, axis, step):
    sizes = lax.axis_size("gx"), lax.axis_size("gy")
    pairs = []
    for x_at in range(sizes[0]):
        for y_at in range(sizes[1]):
            there = [x_at, y_at]
            other = target(there[axis], step, sizes[axis])
            if axis == 0 or abs(other - there[axis]) == 1:
                there[axis] = other
            else:
                there[0] ^= 1
            pairs.append((x_at * sizes[1] + y_at, there[0] * sizes[1] + there[1]))
    return lax.ppermute(x, ("gx", "gy"), pairs)


def far(x):
    return pltpu.with_memory_space_constraint(x, pltpu.HBM)


def edges(rows, cols, spot):
    sides = []
    for axis in range(2):
        even = 1 - spot[axis] % 2
        for up in (even, 1 - even):
            if axis == 0:
                sides.append([(up * (rows - 1), y, up) for y in range(cols)])
            else:
                sides.append([(x, up * (cols - 1), 2 + up) for x in range(rows)])
    return sides


def here_on_mesh():
    return lax.axis_index("gx"), lax.axis_index("gy")


def fetch_edges(which, sides, cols, coupling_far, coupling, arrive, first):
    moves = []
    for o in which:
        for x, y, d in sides[o]:
            i = len(moves)
            moves.append(pltpu.make_async_copy(coupling_far.at[x * cols + y, d + 1], coupling.at[i], arrive.at[first + i]))
            moves[-1].start()
    return moves


def panels_kernel(rows, cols, early, late, joints_far, motion_far, load_far, coupling_far, map_far, *refs):
    motion_out, outs, refs = refs[0], refs[1 : 1 + len(early)], refs[1 + len(early) :]
    motion, load, spread, near_coupling, coupling, maps, joints, arrive = refs
    moves = [
        pltpu.make_async_copy(map_far, maps, arrive.at[0]),
        pltpu.make_async_copy(motion_far, motion, arrive.at[1]),
        pltpu.make_async_copy(load_far, load, arrive.at[2]),
        pltpu.make_async_copy(joints_far, joints, arrive.at[3]),
    ]
    for move in moves:
        move.start()
    sides = edges(rows, cols, here_on_mesh())
    more = fetch_edges(early, sides, cols, coupling_far, coupling, arrive, 4)
    later = fetch_edges(late, sides, cols, coupling_far, near_coupling, arrive, 4 + len(more))
    blocks, wide = motion.shape[:2]
    moves[0].wait()
    split = map_of_blocks(maps, blocks)
    spread[...] = jnp.concatenate(split, axis=1)
    moves[1].wait()
    motion_out[...] = sum(dot(split[b], motion[b], (1, 1)) for b in range(blocks)).astype(BF16)
    moves[2].wait()
    moves[3].wait()
    i = 0
    for o, out in zip(early, outs):
        for k, (x, y, d) in enumerate(sides[o]):
            out[pl.ds(k * wide, wide), :] = motion[x * cols + y]
            more[i].wait()
            matrix = coupling[i] * joints[x, y, d].astype(BF16)
            term = joined(adjoint_parts(matrix, load[x * cols + y]), -1)
            out[pl.ds((len(sides[o]) + k) * wide, wide), :] = term.astype(BF16)
            i += 1
    i = 0
    for o in late:
        for x, y, d in sides[o]:
            later[i].wait()
            near_coupling[i] = near_coupling[i] * joints[x, y, d].astype(BF16)
            i += 1


def edges_kernel(rows, cols, late, motion, load, maps, coupling, *refs):
    load_out, outs, (both,) = refs[0], refs[1 : 1 + len(late)], refs[1 + len(late) :]
    blocks, wide = motion.shape[:2]
    sides = edges(rows, cols, here_on_mesh())
    width = load.shape[2]
    split = [maps[:, b * width : (b + 1) * width] for b in range(blocks)]
    load_out[...] = sum(dot(split[b], load[b], (1, 1)) for b in range(blocks)).astype(BF16)
    for b in range(blocks):
        both[b] = beside_turned(load[b], -1)
    i = 0
    for o, out in zip(late, outs):
        for k, (x, y, d) in enumerate(sides[o]):
            out[pl.ds(k * wide, wide), :] = motion[x * cols + y]
            term = adjoint_product(coupling[i], both[x * cols + y])
            out[pl.ds((len(sides[o]) + k) * wide, wide), :] = term.astype(BF16)
            i += 1


def pressure_kernel(n_gx, hydro_ref, load_panels, *refs):
    pieces, (out_far, gathered, out, leave) = refs[:n_gx], refs[n_gx:]
    me = lax.axis_index("gx")
    panels, wide = load_panels.shape
    for step in range(n_gx):
        start = pl.multiple_of(source(me, step, n_gx) * panels, panels)
        gathered[0, pl.ds(start, panels), :] = pieces[step][...]
        gathered[1, pl.ds(start, panels), :] = times_i(pieces[step][...].astype(F32), 1).astype(BF16)
    fields = gathered[...].reshape(-1, wide)
    tiles = out.shape[0]
    moves = []
    for i in range(2):
        here = pl.ds(i * tiles // 2, tiles // 2)
        rows = pl.ds(i * tiles // 2 * panels, tiles // 2 * panels)
        hydro = jnp.concatenate([hydro_ref[0, rows, :], hydro_ref[1, rows, :]], axis=1)
        out[here, :panels, :] = dot(hydro, fields, (1, 0)).astype(BF16).reshape(-1, panels, wide)
        out[here, panels:, :] = jnp.broadcast_to(load_panels[...], (tiles // 2, panels, wide))
        moves.append(pltpu.make_async_copy(out.at[here], out_far.at[here], leave.at[i]))
        moves[-1].start()
    for move in moves:
        move.wait()


def reaction_kernel(n_gx, hydro_ref, arrived, *refs):
    outs, (reacted,) = refs[:n_gx], refs[n_gx:]
    me = lax.axis_index("gx")
    panels = outs[0].shape[0]
    hydro = hydro_ref[...]
    loads = arrived[:, panels:, :].reshape(hydro.shape[1], -1)
    real = dot(hydro[0], loads, (0, 0))
    imag = dot(hydro[1], loads, (0, 0))
    reacted[...] = real - times_i(imag, 1)
    for step in range(n_gx):
        start = pl.multiple_of(target(me, step, n_gx) * panels, panels)
        outs[step][...] = reacted[pl.ds(start, panels), :]


def add_side(side, valid, received, couplings, residual, multiplier):
    wide = residual.shape[1]
    for k, (b, x, y, d) in enumerate(side):
        motion = received[pl.ds(k * wide, wide), :]
        residual[b] += joined(forward_parts(couplings(k, x, y, d), motion), 1)
        terms = received[pl.ds((len(side) + k) * wide, wide), :]
        multiplier[b] += valid * terms.astype(F32)


def placed(cols, sides):
    return [[(x * cols + y, x, y, d) for x, y, d in side] for side in sides]


def beyond(spot, sizes, o):
    n, me = sizes[o // 2], spot[o // 2]
    other = target(me, 1 + o % 2, n)
    return (abs(me - other) <= 1).astype(F32) if n > 2 else F32(1 - o % 2)


def interior_kernel(rows, cols, sizes, early, late, joints_far, motion_far, load_far, excitation_far, *refs):
    coupling_far, received, refs = refs[0], refs[1 : 1 + len(early)], refs[1 + len(early) :]
    residual_out, multiplier_out, own_far, outer, motion, load, excitation, coupling, own, joints, arrive, leave = refs
    blocks, spot = rows * cols, here_on_mesh()
    moves = [
        pltpu.make_async_copy(motion_far, motion, arrive.at[0]),
        pltpu.make_async_copy(load_far, load, arrive.at[1]),
    ]
    for b in range(blocks):
        moves.append(pltpu.make_async_copy(coupling_far.at[b], coupling.at[b], arrive.at[2 + b]))
    moves.append(pltpu.make_async_copy(excitation_far, excitation, arrive.at[2 + blocks]))
    moves.append(pltpu.make_async_copy(joints_far, joints, arrive.at[3 + blocks]))
    for move in moves:
        move.start()
    sides = edges(rows, cols, spot)
    later = fetch_edges(late, sides, cols, coupling_far, outer, arrive, 4 + blocks)
    moves[0].wait()
    moving = [beside_turned(motion[b], 1) for b in range(blocks)]
    moves[1].wait()
    loads = [beside_turned(load[b], -1) for b in range(blocks)]
    sent = []
    for b in range(blocks):
        moves[2 + b].wait()
        own[b] = forward_product(coupling[b, 0], moving[b])
        sent.append(pltpu.make_async_copy(own.at[b], own_far.at[b], leave.at[b]))
        sent[-1].start()
    moves[2 + blocks].wait()
    moves[3 + blocks].wait()
    for x in range(rows):
        for y in range(cols):
            b = x * cols + y
            forward, adjoint = [], [(loads[b], coupling[b, 0])]
            for d in range(4):
                nx, ny = x + OFFSETS[d][0], y + OFFSETS[d][1]
                if 0 <= nx < rows and 0 <= ny < cols:
                    n = nx * cols + ny
                    forward.append((moving[n], coupling[b, d + 1] * joints[x, y, d].astype(BF16)))
                    adjoint.append((loads[n], coupling[n, (d ^ 1) + 1] * joints[nx, ny, d ^ 1].astype(BF16)))
            residual = own[b] - excitation[b].astype(F32)
            if forward:
                fields = jnp.concatenate([f for f, _ in forward], axis=1)
                matrix = jnp.concatenate([c[part] for _, c in forward for part in range(2)], axis=1)
                residual = residual + dot(fields, matrix, (1, 1))
            residual_out[b] = residual
            fields = jnp.concatenate([f for f, _ in adjoint], axis=1)
            matrix = jnp.concatenate([c[part] for _, c in adjoint for part in range(2)], axis=0)
            multiplier_out[b] = dot(fields, matrix, (1, 0))
    for o, ref in zip(early, received):
        valid = beyond(spot, sizes, o)

        def linked(k, x, y, d, valid=valid):
            return coupling[x * cols + y, d + 1] * (valid * joints[x, y, d].astype(F32)).astype(BF16)

        add_side(placed(cols, sides)[o], valid, ref, linked, residual_out, multiplier_out)
    i = 0
    for o in late:
        valid = beyond(spot, sizes, o)
        for x, y, d in sides[o]:
            later[i].wait()
            outer[i] = outer[i] * (valid * joints[x, y, d].astype(F32)).astype(BF16)
            i += 1
    for move in sent:
        move.wait()


def boundary_kernel(rows, cols, sizes, lift, which, maps, coupling, residual, multiplier, arrived, *refs):
    received, (residual_out, multiplier_out) = refs[: len(which)], refs[len(which) :]
    blocks, unknowns, spot = rows * cols, residual.shape[2], here_on_mesh()
    panels = maps.shape[0]
    pressure = jnp.sum(arrived[:, :panels, :].astype(F32), axis=0).astype(BF16)
    forces = lift * dot(pressure, maps[...], (0, 0))
    for b in range(blocks):
        residual_out[b] = residual[b] + forces[:, b * unknowns : (b + 1) * unknowns]
        multiplier_out[b] = multiplier[b]
    sides, first = placed(cols, edges(rows, cols, spot)), 0
    for o, ref in zip(which, received):
        at = first
        add_side(sides[o], beyond(spot, sizes, o), ref, lambda k, x, y, d: coupling[at + k], residual_out, multiplier_out)
        first += len(sides[o])


def final_kernel(rows, cols, lift, maps, residual, multiplier, own, *refs):
    reactions, (residual_out, multiplier_out, sensitivity_out, full, sensitivity, leave) = refs[:-6], refs[-6:]
    blocks = rows * cols
    unknowns = own.shape[2]
    sent = [pltpu.make_async_copy(residual, residual_out, leave.at[blocks + 1])]
    sent[0].start()
    reaction = sum(r[...].astype(F32) for r in reactions).astype(BF16)
    scale = 1.0 / math.sqrt(own.shape[1] // 2 * unknowns)
    forces = lift * dot(reaction, maps[...], (0, 0))
    sums = []
    for b in range(blocks):
        value = multiplier[b] + forces[:, b * unknowns : (b + 1) * unknowns]
        full[b] = value
        sent.append(pltpu.make_async_copy(full.at[b], multiplier_out.at[b], leave.at[b]))
        sent[-1].start()
        sums.append(jnp.sum((value * own[b]).reshape(-1, 8, unknowns), axis=0))
    for b in range(blocks):
        sensitivity[b // cols, b % cols] = jnp.sum(sums[b]) * scale
    sent.append(pltpu.make_async_copy(sensitivity, sensitivity_out, leave.at[blocks]))
    sent[-1].start()
    for move in sent:
        move.wait()


def cost(flops, bytes_accessed):
    return pl.CostEstimate(flops=int(flops), bytes_accessed=int(bytes_accessed), transcendentals=0)


def shaped(dtype, *shape):
    return jax.ShapeDtypeStruct(shape, dtype)


def params(mebibytes):
    return pltpu.CompilerParams(vmem_limit_bytes=mebibytes * 1024 * 1024)


DMA = pltpu.SemaphoreType.DMA


def on_device(plate_motion, adjoint_load, excitation, coupling, joints, hydro, panel_map):
    rows, cols, cases, _, unknowns = plate_motion.shape
    panels = panel_map.shape[0]
    blocks, wide = rows * cols, 2 * cases
    n_gx, n_gy = lax.axis_size("gx"), lax.axis_size("gy")
    motion = plate_motion.reshape(blocks, wide, unknowns)
    load = adjoint_load.reshape(blocks, wide, unknowns)
    force = excitation.reshape(blocks, wide, unknowns)
    coupling = coupling.reshape(blocks, 5, 2, unknowns, unknowns)
    panel_map = panel_map.reshape(panels * blocks, unknowns)
    lift = math.sqrt(blocks * unknowns / panels)
    block_flops = 2 * wide * unknowns * unknowns * 2
    field = (blocks, wide, unknowns)

    counts = [cols, cols, rows, rows]
    early, late = (3,), (0, 1, 2)
    few, many = sum(counts[o] for o in early), sum(counts[o] for o in late)
    pair = (2, unknowns, unknowns)
    motion_panels, *payloads, near_motion, near_load, maps, near_coupling = pl.pallas_call(
        functools.partial(panels_kernel, rows, cols, early, late),
        name="panels",
        out_shape=[pltpu.VMEM((panels, wide), BF16)]
        + [pltpu.VMEM((2 * counts[o] * wide, unknowns), BF16) for o in early]
        + [pltpu.VMEM(field, BF16)] * 2
        + [pltpu.VMEM((panels, blocks * unknowns), BF16), pltpu.VMEM((many,) + pair, BF16)],
        in_specs=[FAR] * 5,
        out_specs=[WHOLE] * (5 + len(early)),
        scratch_shapes=[
            pltpu.VMEM((few,) + pair, BF16),
            pltpu.VMEM(panel_map.shape, BF16),
            pltpu.SMEM(joints.shape, jnp.int32),
            DMA((4 + few + many,)),
        ],
        compiler_params=params(16),
        cost_estimate=cost(4 * blocks * wide * unknowns * panels, 4 * blocks * wide * unknowns),
    )(far(joints), far(motion), far(load), far(coupling), far(panel_map))
    pieces = [motion_panels] + [exchange(motion_panels, step) for step in range(1, n_gx)]
    fourth = exchange_sides(payloads[0], 1, 2)

    load_panels, *payloads = pl.pallas_call(
        functools.partial(edges_kernel, rows, cols, late),
        name="edges",
        out_shape=[pltpu.VMEM((panels, wide), BF16)]
        + [pltpu.VMEM((2 * counts[o] * wide, unknowns), BF16) for o in late],
        in_specs=[WHOLE] * 4,
        out_specs=[WHOLE] * (1 + len(late)),
        scratch_shapes=[pltpu.VMEM((blocks, wide, 2 * unknowns), BF16)],
        compiler_params=params(16),
        cost_estimate=cost(many * block_flops, 4 * blocks * wide * unknowns + 12 * blocks * unknowns**2),
    )(near_motion, near_load, maps, near_coupling)
    (*payloads, load_panels) = lax.optimization_barrier((*payloads, load_panels))
    parts = pl.pallas_call(
        functools.partial(pressure_kernel, n_gx),
        name="pressure",
        out_shape=pltpu.HBM((n_gy, 2 * panels, wide), BF16),
        in_specs=[WHOLE] * (2 + n_gx),
        out_specs=FAR,
        scratch_shapes=[pltpu.VMEM((2, n_gx * panels, wide), BF16), pltpu.VMEM((n_gy, 2 * panels, wide), BF16), DMA((2,))],
        compiler_params=params(16),
        cost_estimate=cost(2 * hydro.size * wide, 2 * hydro.size),
    )(hydro, load_panels, *pieces)
    arrived = lax.all_to_all(parts, "gy", 0, 0, tiled=True)
    (*payloads, fourth) = lax.optimization_barrier((*payloads, fourth))
    third = exchange_sides(payloads[2], 1, 1)
    second = exchange_sides(payloads[1], 0, 2)
    first = exchange_sides(payloads[0], 0, 1)

    residual, multiplier, own, outer = pl.pallas_call(
        functools.partial(interior_kernel, rows, cols, (n_gx, n_gy), early, late),
        name="interior",
        out_shape=[pltpu.VMEM(field, F32)] * 2
        + [pltpu.HBM(field, F32), pltpu.VMEM((many,) + pair, BF16)],
        in_specs=[FAR] * 5 + [WHOLE] * len(early),
        out_specs=[WHOLE] * 2 + [FAR, WHOLE],
        scratch_shapes=[pltpu.VMEM(field, BF16)] * 3
        + [
            pltpu.VMEM(coupling.shape, BF16),
            pltpu.VMEM(field, F32),
            pltpu.SMEM(joints.shape, jnp.int32),
            DMA((4 + blocks + many,)),
            DMA((blocks,)),
        ],
        compiler_params=params(16),
        cost_estimate=cost(6 * blocks * block_flops, 20 * blocks * unknowns**2 + 18 * blocks * wide * unknowns),
    )(far(joints), far(motion), far(load), far(force), far(coupling), fourth)
    arrived, residual, multiplier, own, outer = lax.optimization_barrier((arrived, residual, multiplier, own, outer))

    reaction_parts = pl.pallas_call(
        functools.partial(reaction_kernel, n_gx),
        name="reaction",
        out_shape=[pltpu.VMEM((panels, wide), F32)] * n_gx,
        in_specs=[WHOLE] * 2,
        out_specs=[WHOLE] * n_gx,
        scratch_shapes=[pltpu.VMEM((n_gx * panels, wide), F32)],
        compiler_params=params(16),
        cost_estimate=cost(2 * hydro.size * wide, 2 * hydro.size),
    )(hydro, arrived)
    reactions = [exchange(reaction_parts[step], step) for step in reversed(range(1, n_gx))] + [reaction_parts[0]]

    residual, multiplier = pl.pallas_call(
        functools.partial(boundary_kernel, rows, cols, (n_gx, n_gy), lift, late),
        name="boundary",
        out_shape=[pltpu.VMEM(field, F32)] * 2,
        in_specs=[WHOLE] * (5 + len(late)),
        out_specs=[WHOLE] * 2,
        compiler_params=params(16),
        cost_estimate=cost(4 * blocks * block_flops, 10 * blocks * unknowns**2 + 18 * blocks * wide * unknowns),
    )(maps, outer, residual, multiplier, arrived, first, second, third)

    residual, multiplier, sensitivity = pl.pallas_call(
        functools.partial(final_kernel, rows, cols, lift),
        name="final",
        out_shape=[pltpu.HBM(field, F32), pltpu.HBM(field, F32), pltpu.HBM((rows, cols), F32)],
        in_specs=[WHOLE] * (4 + n_gx),
        out_specs=[FAR] * 3,
        scratch_shapes=[pltpu.VMEM(field, F32), pltpu.SMEM((rows, cols), F32), DMA((blocks + 2,))],
        compiler_params=params(16),
        cost_estimate=cost(4 * blocks * wide * unknowns * panels, 20 * blocks * wide * unknowns),
    )(maps, residual, multiplier, own, *reactions)
    shape = plate_motion.shape
    return residual.reshape(shape), multiplier.reshape(shape), sensitivity


def solution(mesh):
    field = P("gx", "gy", None, None, None)
    placed = (
        field,
        field,
        field,
        P("gx", "gy", None, None, None, None),
        P("gx", "gy", None),
        P(None, "gx", "gy"),
        P(("gx", "gy"), None, None, None),
    )
    return jax.shard_map(on_device, mesh=mesh, in_specs=placed, out_specs=(field, field, P("gx", "gy")), check_vma=False)
```

```python
import functools
import math

import jax
import jax.numpy as jnp
from jax import lax
from jax.experimental import pallas as pl
from jax.experimental.pallas import tpu as pltpu
from jax.sharding import PartitionSpec as P


F32 = jnp.float32
BF16 = jnp.bfloat16
OFFSETS = ((-1, 0), (1, 0), (0, -1), (0, 1))
WHOLE = pl.BlockSpec(memory_space=pltpu.VMEM)
FAR = pl.BlockSpec(memory_space=pltpu.HBM)


def dot(a, b, over):
    return lax.dot_general(a, b, ((over[:1], over[1:]), ((), ())), preferred_element_type=F32)


def times_i(field, axis):
    shape = field.shape
    if axis == 0:
        field, axis = field.reshape(-1, 8, shape[1]), 1
        place = lax.broadcasted_iota(jnp.int32, (1, 8, shape[1]), 1)
    else:
        place = lax.broadcasted_iota(jnp.int32, (1, shape[1]), 1)
    size = field.shape[axis]
    after = pltpu.roll(field, size - 1, axis)
    before = pltpu.roll(field, 1, axis)
    return jnp.where((place & 1) == 0, -after, before).reshape(shape)


def forward_parts(coupling, motion):
    return dot(motion, coupling.reshape(-1, coupling.shape[-1]), (1, 1))


def adjoint_parts(coupling, load):
    return dot(load, jnp.concatenate([coupling[0], coupling[1]], axis=1), (1, 0))


def beside_turned(field, sign):
    turned = times_i(field.astype(F32), 0)
    return jnp.concatenate([field, (turned if sign > 0 else -turned).astype(BF16)], axis=1)


def forward_product(coupling, both):
    return dot(both, jnp.concatenate([coupling[0], coupling[1]], axis=1), (1, 1))


def adjoint_product(coupling, both):
    return dot(both, coupling.reshape(-1, coupling.shape[-1]), (1, 0))


def joined(parts, sign):
    half = parts.shape[1] // 2
    turned = times_i(parts[:, half:], 0)
    return parts[:, :half] + turned if sign > 0 else parts[:, :half] - turned


def map_of_blocks(map_ref, blocks):
    rows = map_ref.shape[0]
    panels = rows // blocks
    row = lax.broadcasted_iota(jnp.int32, (panels, rows), 0)
    column = lax.broadcasted_iota(jnp.int32, (panels, rows), 1)
    whole = map_ref[...]
    out = []
    for b in range(blocks):
        pick = (column == row * blocks + b).astype(F32).astype(BF16)
        out.append(dot(pick, whole, (1, 0)).astype(BF16))
    return out


def target(i, step, n):
    if step == 0:
        return i
    if step == 1:
        return i ^ 1
    if step == 2:
        return (((i + 1) ^ 1) + n - 1) % n
    return (i + step - 1) % n


def source(i, step, n):
    return target(i, step, n) if step < 3 else (i + n + 1 - step) % n


def places_along_gy(n):
    return list(range(n // 2, n)) + list(range(n // 2))


def all_steps(n):
    return [0, 1] + list(range(3, n)) + [2] if n > 2 else list(range(n))


def exchange(x, step):
    n = lax.axis_size("gx")
    return lax.ppermute(x, "gx", [(i, target(i, step, n)) for i in range(n)])


def exchange_sides(x, axis, step):
    sizes = lax.axis_size("gx"), lax.axis_size("gy")
    pairs = []
    for x_at in range(sizes[0]):
        for y_at in range(sizes[1]):
            there = [x_at, y_at]
            other = target(there[axis], step, sizes[axis])
            if axis == 0 or abs(other - there[axis]) == 1:
                there[axis] = other
            else:
                there[0] ^= 1
            pairs.append((x_at * sizes[1] + y_at, there[0] * sizes[1] + there[1]))
    return lax.ppermute(x, ("gx", "gy"), pairs)


def far(x):
    return pltpu.with_memory_space_constraint(x, pltpu.HBM)


def edges(rows, cols, spot):
    sides = []
    for axis in range(2):
        even = 1 - spot[axis] % 2
        for up in (even, 1 - even):
            if axis == 0:
                sides.append([(up * (rows - 1), y, up) for y in range(cols)])
            else:
                sides.append([(x, up * (cols - 1), 2 + up) for x in range(rows)])
    return sides


def here_on_mesh():
    return lax.axis_index("gx"), lax.axis_index("gy")


def fetch_edges(which, sides, cols, coupling_far, coupling, arrive, first):
    moves = []
    for o in which:
        for x, y, d in sides[o]:
            i = len(moves)
            moves.append(pltpu.make_async_copy(coupling_far.at[x * cols + y, d + 1], coupling.at[i], arrive.at[first + i]))
            moves[-1].start()
    return moves


def panels_kernel(rows, cols, early, late, joints_far, motion_far, load_far, coupling_far, map_far, *refs):
    motion_out, outs, refs = refs[0], refs[1 : 1 + len(early)], refs[1 + len(early) :]
    motion, load, spread, near_coupling, coupling, maps, joints, arrive = refs
    moves = [
        pltpu.make_async_copy(map_far, maps, arrive.at[0]),
        pltpu.make_async_copy(motion_far, motion, arrive.at[1]),
        pltpu.make_async_copy(load_far, load, arrive.at[2]),
        pltpu.make_async_copy(joints_far, joints, arrive.at[3]),
    ]
    for move in moves:
        move.start()
    sides = edges(rows, cols, here_on_mesh())
    more = fetch_edges(early, sides, cols, coupling_far, coupling, arrive, 4)
    later = fetch_edges(late, sides, cols, coupling_far, near_coupling, arrive, 4 + len(more))
    blocks, wide = motion.shape[:2]
    moves[0].wait()
    split = map_of_blocks(maps, blocks)
    spread[...] = jnp.concatenate(split, axis=1)
    moves[1].wait()
    motion_out[...] = sum(dot(split[b], motion[b], (1, 1)) for b in range(blocks)).astype(BF16)
    moves[2].wait()
    moves[3].wait()
    i = 0
    for o, out in zip(early, outs):
        for k, (x, y, d) in enumerate(sides[o]):
            out[pl.ds(k * wide, wide), :] = motion[x * cols + y]
            more[i].wait()
            matrix = coupling[i] * joints[x, y, d].astype(BF16)
            term = joined(adjoint_parts(matrix, load[x * cols + y]), -1)
            out[pl.ds((len(sides[o]) + k) * wide, wide), :] = term.astype(BF16)
            i += 1
    i = 0
    for o in late:
        for x, y, d in sides[o]:
            later[i].wait()
            near_coupling[i] = near_coupling[i] * joints[x, y, d].astype(BF16)
            i += 1


def edges_kernel(rows, cols, late, motion, load, maps, coupling, *refs):
    load_out, outs, (both,) = refs[0], refs[1 : 1 + len(late)], refs[1 + len(late) :]
    blocks, wide = motion.shape[:2]
    sides = edges(rows, cols, here_on_mesh())
    width = load.shape[2]
    split = [maps[:, b * width : (b + 1) * width] for b in range(blocks)]
    load_out[...] = sum(dot(split[b], load[b], (1, 1)) for b in range(blocks)).astype(BF16)
    for b in range(blocks):
        both[b] = beside_turned(load[b], -1)
    i = 0
    for o, out in zip(late, outs):
        for k, (x, y, d) in enumerate(sides[o]):
            out[pl.ds(k * wide, wide), :] = motion[x * cols + y]
            term = adjoint_product(coupling[i], both[x * cols + y])
            out[pl.ds((len(sides[o]) + k) * wide, wide), :] = term.astype(BF16)
            i += 1


def pressure_kernel(n_gx, hydro_ref, load_panels, *refs):
    pieces, (out_far, gathered, out, leave) = refs[:n_gx], refs[n_gx:]
    me = lax.axis_index("gx")
    panels, wide = load_panels.shape
    for step, piece in zip(all_steps(n_gx), pieces):
        start = pl.multiple_of(source(me, step, n_gx) * panels, panels)
        gathered[0, pl.ds(start, panels), :] = piece[...]
        gathered[1, pl.ds(start, panels), :] = times_i(piece[...].astype(F32), 1).astype(BF16)
    fields = gathered[...].reshape(-1, wide)
    tiles = out.shape[0]
    places, half = places_along_gy(tiles), tiles // 2
    moves = []
    for i in range(2):
        here = pl.ds(i * half, half)
        tops = [places[k] * panels for k in range(i * half, (i + 1) * half)]
        hydro = jnp.concatenate(
            [jnp.concatenate([hydro_ref[part, pl.ds(top, panels), :] for part in range(2)], axis=1) for top in tops], axis=0
        )
        out[here, :panels, :] = dot(hydro, fields, (1, 0)).astype(BF16).reshape(-1, panels, wide)
        out[here, panels:, :] = jnp.broadcast_to(load_panels[...], (half, panels, wide))
        moves.append(pltpu.make_async_copy(out.at[here], out_far.at[here], leave.at[i]))
        moves[-1].start()
    for move in moves:
        move.wait()


def reaction_kernel(n_gx, hydro_ref, arrived, *refs):
    outs, (reacted,) = refs[:n_gx], refs[n_gx:]
    me = lax.axis_index("gx")
    panels = outs[0].shape[0]
    hydro = hydro_ref[...]
    places = places_along_gy(arrived.shape[0])
    loads = jnp.concatenate([arrived[places.index(j), panels:, :] for j in range(len(places))], axis=0)
    real = dot(hydro[0], loads, (0, 0))
    imag = dot(hydro[1], loads, (0, 0))
    reacted[...] = real - times_i(imag, 1)
    for step in range(n_gx):
        start = pl.multiple_of(target(me, step, n_gx) * panels, panels)
        outs[step][...] = reacted[pl.ds(start, panels), :]


def add_side(side, valid, received, couplings, residual, multiplier):
    wide = residual.shape[1]
    for k, (b, x, y, d) in enumerate(side):
        motion = received[pl.ds(k * wide, wide), :]
        residual[b] += joined(forward_parts(couplings(k, x, y, d), motion), 1)
        terms = received[pl.ds((len(side) + k) * wide, wide), :]
        multiplier[b] += valid * terms.astype(F32)


def placed(cols, sides):
    return [[(x * cols + y, x, y, d) for x, y, d in side] for side in sides]


def beyond(spot, sizes, o):
    n, me = sizes[o // 2], spot[o // 2]
    other = target(me, 1 + o % 2, n)
    return (abs(me - other) <= 1).astype(F32) if n > 2 else F32(1 - o % 2)


def interior_kernel(rows, cols, sizes, early, late, joints_far, motion_far, load_far, excitation_far, *refs):
    coupling_far, received, refs = refs[0], refs[1 : 1 + len(early)], refs[1 + len(early) :]
    residual_out, multiplier_out, own_far, outer, motion, load, excitation, coupling, own, joints, arrive, leave = refs
    blocks, spot = rows * cols, here_on_mesh()
    moves = [
        pltpu.make_async_copy(motion_far, motion, arrive.at[0]),
        pltpu.make_async_copy(load_far, load, arrive.at[1]),
    ]
    for b in range(blocks):
        moves.append(pltpu.make_async_copy(coupling_far.at[b], coupling.at[b], arrive.at[2 + b]))
    moves.append(pltpu.make_async_copy(excitation_far, excitation, arrive.at[2 + blocks]))
    moves.append(pltpu.make_async_copy(joints_far, joints, arrive.at[3 + blocks]))
    for move in moves:
        move.start()
    sides = edges(rows, cols, spot)
    later = fetch_edges(late, sides, cols, coupling_far, outer, arrive, 4 + blocks)
    moves[0].wait()
    moving = [beside_turned(motion[b], 1) for b in range(blocks)]
    moves[1].wait()
    loads = [beside_turned(load[b], -1) for b in range(blocks)]
    sent = []
    for b in range(blocks):
        moves[2 + b].wait()
        own[b] = forward_product(coupling[b, 0], moving[b])
        sent.append(pltpu.make_async_copy(own.at[b], own_far.at[b], leave.at[b]))
        sent[-1].start()
    moves[2 + blocks].wait()
    moves[3 + blocks].wait()
    for x in range(rows):
        for y in range(cols):
            b = x * cols + y
            forward, adjoint = [], [(loads[b], coupling[b, 0])]
            for d in range(4):
                nx, ny = x + OFFSETS[d][0], y + OFFSETS[d][1]
                if 0 <= nx < rows and 0 <= ny < cols:
                    n = nx * cols + ny
                    forward.append((moving[n], coupling[b, d + 1] * joints[x, y, d].astype(BF16)))
                    adjoint.append((loads[n], coupling[n, (d ^ 1) + 1] * joints[nx, ny, d ^ 1].astype(BF16)))
            residual = own[b] - excitation[b].astype(F32)
            if forward:
                fields = jnp.concatenate([f for f, _ in forward], axis=1)
                matrix = jnp.concatenate([c[part] for _, c in forward for part in range(2)], axis=1)
                residual = residual + dot(fields, matrix, (1, 1))
            residual_out[b] = residual
            fields = jnp.concatenate([f for f, _ in adjoint], axis=1)
            matrix = jnp.concatenate([c[part] for _, c in adjoint for part in range(2)], axis=0)
            multiplier_out[b] = dot(fields, matrix, (1, 0))
    for o, ref in zip(early, received):
        valid = beyond(spot, sizes, o)

        def linked(k, x, y, d, valid=valid):
            return coupling[x * cols + y, d + 1] * (valid * joints[x, y, d].astype(F32)).astype(BF16)

        add_side(placed(cols, sides)[o], valid, ref, linked, residual_out, multiplier_out)
    i = 0
    for o in late:
        valid = beyond(spot, sizes, o)
        for x, y, d in sides[o]:
            later[i].wait()
            outer[i] = outer[i] * (valid * joints[x, y, d].astype(F32)).astype(BF16)
            i += 1
    for move in sent:
        move.wait()


def boundary_kernel(rows, cols, sizes, lift, which, maps, coupling, residual, multiplier, arrived, *refs):
    received, (residual_out, multiplier_out) = refs[: len(which)], refs[len(which) :]
    blocks, unknowns, spot = rows * cols, residual.shape[2], here_on_mesh()
    panels = maps.shape[0]
    pressure = jnp.sum(arrived[:, :panels, :].astype(F32), axis=0).astype(BF16)
    forces = lift * dot(pressure, maps[...], (0, 0))
    for b in range(blocks):
        residual_out[b] = residual[b] + forces[:, b * unknowns : (b + 1) * unknowns]
        multiplier_out[b] = multiplier[b]
    sides, first = placed(cols, edges(rows, cols, spot)), 0
    for o, ref in zip(which, received):
        at = first
        add_side(sides[o], beyond(spot, sizes, o), ref, lambda k, x, y, d: coupling[at + k], residual_out, multiplier_out)
        first += len(sides[o])


def final_kernel(rows, cols, lift, maps, residual, multiplier, own, *refs):
    reactions, (residual_out, multiplier_out, sensitivity_out, full, sensitivity, leave) = refs[:-6], refs[-6:]
    blocks = rows * cols
    unknowns = own.shape[2]
    sent = [pltpu.make_async_copy(residual, residual_out, leave.at[blocks + 1])]
    sent[0].start()
    reaction = sum(r[...].astype(F32) for r in reactions).astype(BF16)
    scale = 1.0 / math.sqrt(own.shape[1] // 2 * unknowns)
    forces = lift * dot(reaction, maps[...], (0, 0))
    sums = []
    for b in range(blocks):
        value = multiplier[b] + forces[:, b * unknowns : (b + 1) * unknowns]
        full[b] = value
        sent.append(pltpu.make_async_copy(full.at[b], multiplier_out.at[b], leave.at[b]))
        sent[-1].start()
        sums.append(jnp.sum((value * own[b]).reshape(-1, 8, unknowns), axis=0))
    for b in range(blocks):
        sensitivity[b // cols, b % cols] = jnp.sum(sums[b]) * scale
    sent.append(pltpu.make_async_copy(sensitivity, sensitivity_out, leave.at[blocks]))
    sent[-1].start()
    for move in sent:
        move.wait()


def cost(flops, bytes_accessed):
    return pl.CostEstimate(flops=int(flops), bytes_accessed=int(bytes_accessed), transcendentals=0)


def shaped(dtype, *shape):
    return jax.ShapeDtypeStruct(shape, dtype)


def params(mebibytes):
    return pltpu.CompilerParams(vmem_limit_bytes=mebibytes * 1024 * 1024)


DMA = pltpu.SemaphoreType.DMA


def on_device(plate_motion, adjoint_load, excitation, coupling, joints, hydro, panel_map):
    rows, cols, cases, _, unknowns = plate_motion.shape
    panels = panel_map.shape[0]
    blocks, wide = rows * cols, 2 * cases
    n_gx, n_gy = lax.axis_size("gx"), lax.axis_size("gy")
    motion = plate_motion.reshape(blocks, wide, unknowns)
    load = adjoint_load.reshape(blocks, wide, unknowns)
    force = excitation.reshape(blocks, wide, unknowns)
    coupling = coupling.reshape(blocks, 5, 2, unknowns, unknowns)
    panel_map = panel_map.reshape(panels * blocks, unknowns)
    lift = math.sqrt(blocks * unknowns / panels)
    block_flops = 2 * wide * unknowns * unknowns * 2
    field = (blocks, wide, unknowns)

    counts = [cols, cols, rows, rows]
    early, late = (3,), (0, 1, 2)
    few, many = sum(counts[o] for o in early), sum(counts[o] for o in late)
    pair = (2, unknowns, unknowns)
    motion_panels, *payloads, near_motion, near_load, maps, near_coupling = pl.pallas_call(
        functools.partial(panels_kernel, rows, cols, early, late),
        name="panels",
        out_shape=[pltpu.VMEM((panels, wide), BF16)]
        + [pltpu.VMEM((2 * counts[o] * wide, unknowns), BF16) for o in early]
        + [pltpu.VMEM(field, BF16)] * 2
        + [pltpu.VMEM((panels, blocks * unknowns), BF16), pltpu.VMEM((many,) + pair, BF16)],
        in_specs=[FAR] * 5,
        out_specs=[WHOLE] * (5 + len(early)),
        scratch_shapes=[
            pltpu.VMEM((few,) + pair, BF16),
            pltpu.VMEM(panel_map.shape, BF16),
            pltpu.SMEM(joints.shape, jnp.int32),
            DMA((4 + few + many,)),
        ],
        compiler_params=params(16),
        cost_estimate=cost(4 * blocks * wide * unknowns * panels, 4 * blocks * wide * unknowns),
    )(far(joints), far(motion), far(load), far(coupling), far(panel_map))
    pieces = [motion_panels] + [exchange(motion_panels, step) for step in all_steps(n_gx)[1:]]
    fourth = exchange_sides(payloads[0], 1, 2)

    load_panels, *payloads = pl.pallas_call(
        functools.partial(edges_kernel, rows, cols, late),
        name="edges",
        out_shape=[pltpu.VMEM((panels, wide), BF16)]
        + [pltpu.VMEM((2 * counts[o] * wide, unknowns), BF16) for o in late],
        in_specs=[WHOLE] * 4,
        out_specs=[WHOLE] * (1 + len(late)),
        scratch_shapes=[pltpu.VMEM((blocks, wide, 2 * unknowns), BF16)],
        compiler_params=params(16),
        cost_estimate=cost(many * block_flops, 4 * blocks * wide * unknowns + 12 * blocks * unknowns**2),
    )(near_motion, near_load, maps, near_coupling)
    (*payloads, load_panels) = lax.optimization_barrier((*payloads, load_panels))
    parts = pl.pallas_call(
        functools.partial(pressure_kernel, n_gx),
        name="pressure",
        out_shape=pltpu.HBM((n_gy, 2 * panels, wide), BF16),
        in_specs=[WHOLE] * (2 + n_gx),
        out_specs=FAR,
        scratch_shapes=[pltpu.VMEM((2, n_gx * panels, wide), BF16), pltpu.VMEM((n_gy, 2 * panels, wide), BF16), DMA((2,))],
        compiler_params=params(16),
        cost_estimate=cost(2 * hydro.size * wide, 2 * hydro.size),
    )(hydro, load_panels, *pieces)
    arrived = lax.all_to_all(parts, "gy", 0, 0, axis_index_groups=[places_along_gy(n_gy)], tiled=True)
    (*payloads, fourth) = lax.optimization_barrier((*payloads, fourth))
    third = exchange_sides(payloads[2], 1, 1)
    second = exchange_sides(payloads[1], 0, 2)
    first = exchange_sides(payloads[0], 0, 1)

    residual, multiplier, own, outer = pl.pallas_call(
        functools.partial(interior_kernel, rows, cols, (n_gx, n_gy), early, late),
        name="interior",
        out_shape=[pltpu.VMEM(field, F32)] * 2
        + [pltpu.HBM(field, F32), pltpu.VMEM((many,) + pair, BF16)],
        in_specs=[FAR] * 5 + [WHOLE] * len(early),
        out_specs=[WHOLE] * 2 + [FAR, WHOLE],
        scratch_shapes=[pltpu.VMEM(field, BF16)] * 3
        + [
            pltpu.VMEM(coupling.shape, BF16),
            pltpu.VMEM(field, F32),
            pltpu.SMEM(joints.shape, jnp.int32),
            DMA((4 + blocks + many,)),
            DMA((blocks,)),
        ],
        compiler_params=params(16),
        cost_estimate=cost(6 * blocks * block_flops, 20 * blocks * unknowns**2 + 18 * blocks * wide * unknowns),
    )(far(joints), far(motion), far(load), far(force), far(coupling), fourth)
    arrived, residual, multiplier, own, outer = lax.optimization_barrier((arrived, residual, multiplier, own, outer))

    reaction_parts = pl.pallas_call(
        functools.partial(reaction_kernel, n_gx),
        name="reaction",
        out_shape=[pltpu.VMEM((panels, wide), F32)] * n_gx,
        in_specs=[WHOLE] * 2,
        out_specs=[WHOLE] * n_gx,
        scratch_shapes=[pltpu.VMEM((n_gx * panels, wide), F32)],
        compiler_params=params(16),
        cost_estimate=cost(2 * hydro.size * wide, 2 * hydro.size),
    )(hydro, arrived)
    reactions = [exchange(reaction_parts[step], step) for step in reversed(range(1, n_gx))] + [reaction_parts[0]]

    residual, multiplier = pl.pallas_call(
        functools.partial(boundary_kernel, rows, cols, (n_gx, n_gy), lift, late),
        name="boundary",
        out_shape=[pltpu.VMEM(field, F32)] * 2,
        in_specs=[WHOLE] * (5 + len(late)),
        out_specs=[WHOLE] * 2,
        compiler_params=params(16),
        cost_estimate=cost(4 * blocks * block_flops, 10 * blocks * unknowns**2 + 18 * blocks * wide * unknowns),
    )(maps, outer, residual, multiplier, arrived, first, second, third)

    residual, multiplier, sensitivity = pl.pallas_call(
        functools.partial(final_kernel, rows, cols, lift),
        name="final",
        out_shape=[pltpu.HBM(field, F32), pltpu.HBM(field, F32), pltpu.HBM((rows, cols), F32)],
        in_specs=[WHOLE] * (4 + n_gx),
        out_specs=[FAR] * 3,
        scratch_shapes=[pltpu.VMEM(field, F32), pltpu.SMEM((rows, cols), F32), DMA((blocks + 2,))],
        compiler_params=params(16),
        cost_estimate=cost(4 * blocks * wide * unknowns * panels, 20 * blocks * wide * unknowns),
    )(maps, residual, multiplier, own, *reactions)
    shape = plate_motion.shape
    return residual.reshape(shape), multiplier.reshape(shape), sensitivity


def solution(mesh):
    field = P("gx", "gy", None, None, None)
    placed = (
        field,
        field,
        field,
        P("gx", "gy", None, None, None, None),
        P("gx", "gy", None),
        P(None, "gx", "gy"),
        P(("gx", "gy"), None, None, None),
    )
    return jax.shard_map(on_device, mesh=mesh, in_specs=placed, out_specs=(field, field, P("gx", "gy")), check_vma=False)
```

```python
import functools
import math

import jax
import jax.numpy as jnp
from jax import lax
from jax.experimental import pallas as pl
from jax.experimental.pallas import tpu as pltpu
from jax.sharding import PartitionSpec as P


F32 = jnp.float32
BF16 = jnp.bfloat16
OFFSETS = ((-1, 0), (1, 0), (0, -1), (0, 1))
WHOLE = pl.BlockSpec(memory_space=pltpu.VMEM)
FAR = pl.BlockSpec(memory_space=pltpu.HBM)


def dot(a, b, over):
    return lax.dot_general(a, b, ((over[:1], over[1:]), ((), ())), preferred_element_type=F32)


def times_i(field, axis):
    shape = field.shape
    if axis == 0:
        field, axis = field.reshape(-1, 8, shape[1]), 1
        place = lax.broadcasted_iota(jnp.int32, (1, 8, shape[1]), 1)
    else:
        place = lax.broadcasted_iota(jnp.int32, (1, shape[1]), 1)
    size = field.shape[axis]
    after = pltpu.roll(field, size - 1, axis)
    before = pltpu.roll(field, 1, axis)
    return jnp.where((place & 1) == 0, -after, before).reshape(shape)


def forward_parts(coupling, motion):
    return dot(motion, coupling.reshape(-1, coupling.shape[-1]), (1, 1))


def adjoint_parts(coupling, load):
    return dot(load, jnp.concatenate([coupling[0], coupling[1]], axis=1), (1, 0))


def beside_turned(field, sign):
    turned = times_i(field.astype(F32), 0)
    return jnp.concatenate([field, (turned if sign > 0 else -turned).astype(BF16)], axis=1)


def forward_product(coupling, both):
    return dot(both, jnp.concatenate([coupling[0], coupling[1]], axis=1), (1, 1))


def adjoint_product(coupling, both):
    return dot(both, coupling.reshape(-1, coupling.shape[-1]), (1, 0))


def joined(parts, sign):
    half = parts.shape[1] // 2
    turned = times_i(parts[:, half:], 0)
    return parts[:, :half] + turned if sign > 0 else parts[:, :half] - turned


def map_of_blocks(map_ref, blocks):
    rows = map_ref.shape[0]
    panels = rows // blocks
    row = lax.broadcasted_iota(jnp.int32, (panels, rows), 0)
    column = lax.broadcasted_iota(jnp.int32, (panels, rows), 1)
    whole = map_ref[...]
    out = []
    for b in range(blocks):
        pick = (column == row * blocks + b).astype(F32).astype(BF16)
        out.append(dot(pick, whole, (1, 0)).astype(BF16))
    return out


def target(i, step, n):
    if step == 0:
        return i
    if step == 1:
        return i ^ 1
    if step == 2:
        return (((i + 1) ^ 1) + n - 1) % n
    return (i + step - 1) % n


def source(i, step, n):
    return target(i, step, n) if step < 3 else (i + n + 1 - step) % n


def places_along_gy(n):
    return list(range(n // 2, n)) + list(range(n // 2))


def all_steps(n):
    return [0, 1] + list(range(3, n)) + [2] if n > 2 else list(range(n))


def exchange(x, step):
    n = lax.axis_size("gx")
    return lax.ppermute(x, "gx", [(i, target(i, step, n)) for i in range(n)])


def exchange_sides(x, axis, step):
    sizes = lax.axis_size("gx"), lax.axis_size("gy")
    pairs = []
    for x_at in range(sizes[0]):
        for y_at in range(sizes[1]):
            there = [x_at, y_at]
            other = target(there[axis], step, sizes[axis])
            if axis == 0 or abs(other - there[axis]) == 1:
                there[axis] = other
            else:
                there[0] ^= 1
            pairs.append((x_at * sizes[1] + y_at, there[0] * sizes[1] + there[1]))
    return lax.ppermute(x, ("gx", "gy"), pairs)


def far(x):
    return pltpu.with_memory_space_constraint(x, pltpu.HBM)


def edges(rows, cols, spot):
    sides = []
    for axis in range(2):
        even = 1 - spot[axis] % 2
        for up in (even, 1 - even):
            if axis == 0:
                sides.append([(up * (rows - 1), y, up) for y in range(cols)])
            else:
                sides.append([(x, up * (cols - 1), 2 + up) for x in range(rows)])
    return sides


def here_on_mesh():
    return lax.axis_index("gx"), lax.axis_index("gy")


def fetch_edges(which, sides, cols, coupling_far, coupling, arrive, first):
    moves = []
    for o in which:
        for x, y, d in sides[o]:
            i = len(moves)
            moves.append(pltpu.make_async_copy(coupling_far.at[x * cols + y, d + 1], coupling.at[i], arrive.at[first + i]))
            moves[-1].start()
    return moves


def panels_kernel(rows, cols, early, late, joints_far, motion_far, load_far, coupling_far, map_far, *refs):
    motion_out, outs, refs = refs[0], refs[1 : 1 + len(early)], refs[1 + len(early) :]
    motion, load, spread, near_coupling, coupling, maps, joints, arrive = refs
    moves = [
        pltpu.make_async_copy(map_far, maps, arrive.at[0]),
        pltpu.make_async_copy(motion_far, motion, arrive.at[1]),
        pltpu.make_async_copy(load_far, load, arrive.at[2]),
        pltpu.make_async_copy(joints_far, joints, arrive.at[3]),
    ]
    for move in moves:
        move.start()
    sides = edges(rows, cols, here_on_mesh())
    more = fetch_edges(early, sides, cols, coupling_far, coupling, arrive, 4)
    later = fetch_edges(late, sides, cols, coupling_far, near_coupling, arrive, 4 + len(more))
    blocks, wide = motion.shape[:2]
    moves[0].wait()
    split = map_of_blocks(maps, blocks)
    spread[...] = jnp.concatenate(split, axis=1)
    moves[1].wait()
    motion_out[...] = sum(dot(split[b], motion[b], (1, 1)) for b in range(blocks)).astype(BF16)
    moves[2].wait()
    moves[3].wait()
    i = 0
    for o, out in zip(early, outs):
        for k, (x, y, d) in enumerate(sides[o]):
            out[pl.ds(k * wide, wide), :] = motion[x * cols + y]
            more[i].wait()
            matrix = coupling[i] * joints[x, y, d].astype(BF16)
            term = joined(adjoint_parts(matrix, load[x * cols + y]), -1)
            out[pl.ds((len(sides[o]) + k) * wide, wide), :] = term.astype(BF16)
            i += 1
    i = 0
    for o in late:
        for x, y, d in sides[o]:
            later[i].wait()
            near_coupling[i] = near_coupling[i] * joints[x, y, d].astype(BF16)
            i += 1


def edges_kernel(rows, cols, late, motion, load, maps, coupling, *refs):
    load_out, outs, (both,) = refs[0], refs[1 : 1 + len(late)], refs[1 + len(late) :]
    blocks, wide = motion.shape[:2]
    sides = edges(rows, cols, here_on_mesh())
    width = load.shape[2]
    split = [maps[:, b * width : (b + 1) * width] for b in range(blocks)]
    load_out[...] = sum(dot(split[b], load[b], (1, 1)) for b in range(blocks)).astype(BF16)
    for b in range(blocks):
        both[b] = beside_turned(load[b], -1)
    i = 0
    for o, out in zip(late, outs):
        for k, (x, y, d) in enumerate(sides[o]):
            out[pl.ds(k * wide, wide), :] = motion[x * cols + y]
            term = adjoint_product(coupling[i], both[x * cols + y])
            out[pl.ds((len(sides[o]) + k) * wide, wide), :] = term.astype(BF16)
            i += 1


def pressure_kernel(n_gx, hydro_ref, load_panels, *refs):
    pieces, (out_far, gathered, out, leave) = refs[:n_gx], refs[n_gx:]
    me = lax.axis_index("gx")
    panels, wide = load_panels.shape
    for step, piece in zip(all_steps(n_gx), pieces):
        start = pl.multiple_of(source(me, step, n_gx) * panels, panels)
        gathered[0, pl.ds(start, panels), :] = piece[...]
        gathered[1, pl.ds(start, panels), :] = times_i(piece[...].astype(F32), 1).astype(BF16)
    fields = gathered[...].reshape(-1, wide)
    tiles = out.shape[0]
    places, half = places_along_gy(tiles), tiles // 2
    moves = []
    for i in range(2):
        here = pl.ds(i * half, half)
        tops = [places[k] * panels for k in range(i * half, (i + 1) * half)]
        hydro = jnp.concatenate(
            [jnp.concatenate([hydro_ref[part, pl.ds(top, panels), :] for part in range(2)], axis=1) for top in tops], axis=0
        )
        out[here, :panels, :] = dot(hydro, fields, (1, 0)).astype(BF16).reshape(-1, panels, wide)
        out[here, panels:, :] = jnp.broadcast_to(load_panels[...], (half, panels, wide))
        moves.append(pltpu.make_async_copy(out.at[here], out_far.at[here], leave.at[i]))
        moves[-1].start()
    for move in moves:
        move.wait()


def reaction_kernel(n_gx, hydro_ref, arrived, *refs):
    outs, (reacted,) = refs[:n_gx], refs[n_gx:]
    me = lax.axis_index("gx")
    panels = outs[0].shape[0]
    hydro = hydro_ref[...]
    places = places_along_gy(arrived.shape[0])
    loads = jnp.concatenate([arrived[places.index(j), panels:, :] for j in range(len(places))], axis=0)
    real = dot(hydro[0], loads, (0, 0))
    imag = dot(hydro[1], loads, (0, 0))
    reacted[...] = real - times_i(imag, 1)
    for step in range(n_gx):
        start = pl.multiple_of(target(me, step, n_gx) * panels, panels)
        outs[step][...] = reacted[pl.ds(start, panels), :]


def add_side(side, valid, received, couplings, residual, multiplier):
    wide = residual.shape[1]
    for k, (b, x, y, d) in enumerate(side):
        motion = received[pl.ds(k * wide, wide), :]
        residual[b] += joined(forward_parts(couplings(k, x, y, d), motion), 1)
        terms = received[pl.ds((len(side) + k) * wide, wide), :]
        multiplier[b] += valid * terms.astype(F32)


def placed(cols, sides):
    return [[(x * cols + y, x, y, d) for x, y, d in side] for side in sides]


def beyond(spot, sizes, o):
    n, me = sizes[o // 2], spot[o // 2]
    other = target(me, 1 + o % 2, n)
    return (abs(me - other) <= 1).astype(F32) if n > 2 else F32(1 - o % 2)


def interior_kernel(rows, cols, sizes, early, late, joints_far, motion_far, load_far, excitation_far, *refs):
    coupling_far, received, refs = refs[0], refs[1 : 1 + len(early)], refs[1 + len(early) :]
    residual_out, multiplier_out, own_far, outer, motion, load, excitation, coupling, own, joints, arrive, leave = refs
    blocks, spot = rows * cols, here_on_mesh()
    moves = [
        pltpu.make_async_copy(motion_far, motion, arrive.at[0]),
        pltpu.make_async_copy(load_far, load, arrive.at[1]),
    ]
    for b in range(blocks):
        moves.append(pltpu.make_async_copy(coupling_far.at[b], coupling.at[b], arrive.at[2 + b]))
    moves.append(pltpu.make_async_copy(excitation_far, excitation, arrive.at[2 + blocks]))
    moves.append(pltpu.make_async_copy(joints_far, joints, arrive.at[3 + blocks]))
    for move in moves:
        move.start()
    sides = edges(rows, cols, spot)
    later = fetch_edges(late, sides, cols, coupling_far, outer, arrive, 4 + blocks)
    moves[0].wait()
    moving = [beside_turned(motion[b], 1) for b in range(blocks)]
    moves[1].wait()
    loads = [beside_turned(load[b], -1) for b in range(blocks)]
    sent = []
    for b in range(blocks):
        moves[2 + b].wait()
        own[b] = forward_product(coupling[b, 0], moving[b])
        sent.append(pltpu.make_async_copy(own.at[b], own_far.at[b], leave.at[b]))
        sent[-1].start()
    moves[2 + blocks].wait()
    moves[3 + blocks].wait()
    for x in range(rows):
        for y in range(cols):
            b = x * cols + y
            forward, adjoint = [], [(loads[b], coupling[b, 0])]
            for d in range(4):
                nx, ny = x + OFFSETS[d][0], y + OFFSETS[d][1]
                if 0 <= nx < rows and 0 <= ny < cols:
                    n = nx * cols + ny
                    forward.append((moving[n], coupling[b, d + 1] * joints[x, y, d].astype(BF16)))
                    adjoint.append((loads[n], coupling[n, (d ^ 1) + 1] * joints[nx, ny, d ^ 1].astype(BF16)))
            residual = own[b] - excitation[b].astype(F32)
            if forward:
                fields = jnp.concatenate([f for f, _ in forward], axis=1)
                matrix = jnp.concatenate([c[part] for _, c in forward for part in range(2)], axis=1)
                residual = residual + dot(fields, matrix, (1, 1))
            residual_out[b] = residual
            fields = jnp.concatenate([f for f, _ in adjoint], axis=1)
            matrix = jnp.concatenate([c[part] for _, c in adjoint for part in range(2)], axis=0)
            multiplier_out[b] = dot(fields, matrix, (1, 0))
    for o, ref in zip(early, received):
        valid = beyond(spot, sizes, o)

        def linked(k, x, y, d, valid=valid):
            return coupling[x * cols + y, d + 1] * (valid * joints[x, y, d].astype(F32)).astype(BF16)

        add_side(placed(cols, sides)[o], valid, ref, linked, residual_out, multiplier_out)
    i = 0
    for o in late:
        valid = beyond(spot, sizes, o)
        for x, y, d in sides[o]:
            later[i].wait()
            outer[i] = outer[i] * (valid * joints[x, y, d].astype(F32)).astype(BF16)
            i += 1
    for move in sent:
        move.wait()


def boundary_kernel(rows, cols, sizes, lift, which, maps, coupling, residual, multiplier, arrived, *refs):
    received, (residual_out, multiplier_out) = refs[: len(which)], refs[len(which) :]
    blocks, unknowns, spot = rows * cols, residual.shape[2], here_on_mesh()
    panels = maps.shape[0]
    pressure = jnp.sum(arrived[:, :panels, :].astype(F32), axis=0).astype(BF16)
    forces = lift * dot(pressure, maps[...], (0, 0))
    for b in range(blocks):
        residual_out[b] = residual[b] + forces[:, b * unknowns : (b + 1) * unknowns]
        multiplier_out[b] = multiplier[b]
    sides, first = placed(cols, edges(rows, cols, spot)), 0
    for o, ref in zip(which, received):
        at = first
        add_side(sides[o], beyond(spot, sizes, o), ref, lambda k, x, y, d: coupling[at + k], residual_out, multiplier_out)
        first += len(sides[o])


def final_kernel(rows, cols, lift, maps, residual, multiplier, own, *refs):
    reactions, (residual_out, multiplier_out, sensitivity_out, full, sensitivity, leave) = refs[:-6], refs[-6:]
    blocks = rows * cols
    unknowns = own.shape[2]
    sent = [pltpu.make_async_copy(residual, residual_out, leave.at[blocks + 1])]
    sent[0].start()
    reaction = sum(r[...].astype(F32) for r in reactions).astype(BF16)
    scale = 1.0 / math.sqrt(own.shape[1] // 2 * unknowns)
    forces = lift * dot(reaction, maps[...], (0, 0))
    sums = []
    for b in range(blocks):
        value = multiplier[b] + forces[:, b * unknowns : (b + 1) * unknowns]
        full[b] = value
        sent.append(pltpu.make_async_copy(full.at[b], multiplier_out.at[b], leave.at[b]))
        sent[-1].start()
        sums.append(jnp.sum((value * own[b]).reshape(-1, 8, unknowns), axis=0))
    for b in range(blocks):
        sensitivity[b // cols, b % cols] = jnp.sum(sums[b]) * scale
    sent.append(pltpu.make_async_copy(sensitivity, sensitivity_out, leave.at[blocks]))
    sent[-1].start()
    for move in sent:
        move.wait()


def cost(flops, bytes_accessed):
    return pl.CostEstimate(flops=int(flops), bytes_accessed=int(bytes_accessed), transcendentals=0)


def shaped(dtype, *shape):
    return jax.ShapeDtypeStruct(shape, dtype)


def params(mebibytes):
    return pltpu.CompilerParams(vmem_limit_bytes=mebibytes * 1024 * 1024)


DMA = pltpu.SemaphoreType.DMA


def on_device(plate_motion, adjoint_load, excitation, coupling, joints, hydro, panel_map):
    rows, cols, cases, _, unknowns = plate_motion.shape
    panels = panel_map.shape[0]
    blocks, wide = rows * cols, 2 * cases
    n_gx, n_gy = lax.axis_size("gx"), lax.axis_size("gy")
    motion = plate_motion.reshape(blocks, wide, unknowns)
    load = adjoint_load.reshape(blocks, wide, unknowns)
    force = excitation.reshape(blocks, wide, unknowns)
    coupling = coupling.reshape(blocks, 5, 2, unknowns, unknowns)
    panel_map = panel_map.reshape(panels * blocks, unknowns)
    lift = math.sqrt(blocks * unknowns / panels)
    block_flops = 2 * wide * unknowns * unknowns * 2
    field = (blocks, wide, unknowns)

    counts = [cols, cols, rows, rows]
    early, late = (3,), (0, 1, 2)
    few, many = sum(counts[o] for o in early), sum(counts[o] for o in late)
    pair = (2, unknowns, unknowns)
    motion_panels, *payloads, near_motion, near_load, maps, near_coupling = pl.pallas_call(
        functools.partial(panels_kernel, rows, cols, early, late),
        name="panels",
        out_shape=[pltpu.VMEM((panels, wide), BF16)]
        + [pltpu.VMEM((2 * counts[o] * wide, unknowns), BF16) for o in early]
        + [pltpu.VMEM(field, BF16)] * 2
        + [pltpu.VMEM((panels, blocks * unknowns), BF16), pltpu.VMEM((many,) + pair, BF16)],
        in_specs=[FAR] * 5,
        out_specs=[WHOLE] * (5 + len(early)),
        scratch_shapes=[
            pltpu.VMEM((few,) + pair, BF16),
            pltpu.VMEM(panel_map.shape, BF16),
            pltpu.SMEM(joints.shape, jnp.int32),
            DMA((4 + few + many,)),
        ],
        compiler_params=params(16),
        cost_estimate=cost(4 * blocks * wide * unknowns * panels, 4 * blocks * wide * unknowns),
    )(far(joints), far(motion), far(load), far(coupling), far(panel_map))
    pieces = [motion_panels] + [exchange(motion_panels, step) for step in all_steps(n_gx)[1:]]
    fourth = exchange_sides(payloads[0], 1, 2)

    load_panels, *payloads = pl.pallas_call(
        functools.partial(edges_kernel, rows, cols, late),
        name="edges",
        out_shape=[pltpu.VMEM((panels, wide), BF16)]
        + [pltpu.VMEM((2 * counts[o] * wide, unknowns), BF16) for o in late],
        in_specs=[WHOLE] * 4,
        out_specs=[WHOLE] * (1 + len(late)),
        scratch_shapes=[pltpu.VMEM((blocks, wide, 2 * unknowns), BF16)],
        compiler_params=params(16),
        cost_estimate=cost(30 * many * block_flops, 4 * blocks * wide * unknowns + 12 * blocks * unknowns**2),
    )(near_motion, near_load, maps, near_coupling)
    (*payloads, load_panels) = lax.optimization_barrier((*payloads, load_panels))
    parts = pl.pallas_call(
        functools.partial(pressure_kernel, n_gx),
        name="pressure",
        out_shape=pltpu.HBM((n_gy, 2 * panels, wide), BF16),
        in_specs=[WHOLE] * (2 + n_gx),
        out_specs=FAR,
        scratch_shapes=[pltpu.VMEM((2, n_gx * panels, wide), BF16), pltpu.VMEM((n_gy, 2 * panels, wide), BF16), DMA((2,))],
        compiler_params=params(16),
        cost_estimate=cost(60 * hydro.size * wide, 2 * hydro.size),
    )(hydro, load_panels, *pieces)
    arrived = lax.all_to_all(parts, "gy", 0, 0, axis_index_groups=[places_along_gy(n_gy)], tiled=True)
    (*payloads, fourth) = lax.optimization_barrier((*payloads, fourth))
    third = exchange_sides(payloads[2], 1, 1)
    second = exchange_sides(payloads[1], 0, 2)
    first = exchange_sides(payloads[0], 0, 1)

    residual, multiplier, own, outer = pl.pallas_call(
        functools.partial(interior_kernel, rows, cols, (n_gx, n_gy), early, late),
        name="interior",
        out_shape=[pltpu.VMEM(field, F32)] * 2
        + [pltpu.HBM(field, F32), pltpu.VMEM((many,) + pair, BF16)],
        in_specs=[FAR] * 5 + [WHOLE] * len(early),
        out_specs=[WHOLE] * 2 + [FAR, WHOLE],
        scratch_shapes=[pltpu.VMEM(field, BF16)] * 3
        + [
            pltpu.VMEM(coupling.shape, BF16),
            pltpu.VMEM(field, F32),
            pltpu.SMEM(joints.shape, jnp.int32),
            DMA((4 + blocks + many,)),
            DMA((blocks,)),
        ],
        compiler_params=params(16),
        cost_estimate=cost(6 * blocks * block_flops, 20 * blocks * unknowns**2 + 18 * blocks * wide * unknowns),
    )(far(joints), far(motion), far(load), far(force), far(coupling), fourth)
    arrived, residual, multiplier, own, outer = lax.optimization_barrier((arrived, residual, multiplier, own, outer))

    reaction_parts = pl.pallas_call(
        functools.partial(reaction_kernel, n_gx),
        name="reaction",
        out_shape=[pltpu.VMEM((panels, wide), F32)] * n_gx,
        in_specs=[WHOLE] * 2,
        out_specs=[WHOLE] * n_gx,
        scratch_shapes=[pltpu.VMEM((n_gx * panels, wide), F32)],
        compiler_params=params(16),
        cost_estimate=cost(2 * hydro.size * wide, 2 * hydro.size),
    )(hydro, arrived)
    reactions = [exchange(reaction_parts[step], step) for step in reversed(range(1, n_gx))] + [reaction_parts[0]]

    residual, multiplier = pl.pallas_call(
        functools.partial(boundary_kernel, rows, cols, (n_gx, n_gy), lift, late),
        name="boundary",
        out_shape=[pltpu.VMEM(field, F32)] * 2,
        in_specs=[WHOLE] * (5 + len(late)),
        out_specs=[WHOLE] * 2,
        compiler_params=params(16),
        cost_estimate=cost(4 * blocks * block_flops, 10 * blocks * unknowns**2 + 18 * blocks * wide * unknowns),
    )(maps, outer, residual, multiplier, arrived, first, second, third)

    residual, multiplier, sensitivity = pl.pallas_call(
        functools.partial(final_kernel, rows, cols, lift),
        name="final",
        out_shape=[pltpu.HBM(field, F32), pltpu.HBM(field, F32), pltpu.HBM((rows, cols), F32)],
        in_specs=[WHOLE] * (4 + n_gx),
        out_specs=[FAR] * 3,
        scratch_shapes=[pltpu.VMEM(field, F32), pltpu.SMEM((rows, cols), F32), DMA((blocks + 2,))],
        compiler_params=params(16),
        cost_estimate=cost(4 * blocks * wide * unknowns * panels, 20 * blocks * wide * unknowns),
    )(maps, residual, multiplier, own, *reactions)
    shape = plate_motion.shape
    return residual.reshape(shape), multiplier.reshape(shape), sensitivity


def solution(mesh):
    field = P("gx", "gy", None, None, None)
    placed = (
        field,
        field,
        field,
        P("gx", "gy", None, None, None, None),
        P("gx", "gy", None),
        P(None, "gx", "gy"),
        P(("gx", "gy"), None, None, None),
    )
    return jax.shard_map(on_device, mesh=mesh, in_specs=placed, out_specs=(field, field, P("gx", "gy")), check_vma=False)
```

```python
import functools
import math

import jax
import jax.numpy as jnp
from jax import lax
from jax.experimental import pallas as pl
from jax.experimental.pallas import tpu as pltpu
from jax.sharding import PartitionSpec as P


F32 = jnp.float32
BF16 = jnp.bfloat16
OFFSETS = ((-1, 0), (1, 0), (0, -1), (0, 1))
WHOLE = pl.BlockSpec(memory_space=pltpu.VMEM)
FAR = pl.BlockSpec(memory_space=pltpu.HBM)


def dot(a, b, over):
    return lax.dot_general(a, b, ((over[:1], over[1:]), ((), ())), preferred_element_type=F32)


def times_i(field, axis):
    shape = field.shape
    if axis == 0:
        field, axis = field.reshape(-1, 8, shape[1]), 1
        place = lax.broadcasted_iota(jnp.int32, (1, 8, shape[1]), 1)
    else:
        place = lax.broadcasted_iota(jnp.int32, (1, shape[1]), 1)
    size = field.shape[axis]
    after = pltpu.roll(field, size - 1, axis)
    before = pltpu.roll(field, 1, axis)
    return jnp.where((place & 1) == 0, -after, before).reshape(shape)


def forward_parts(coupling, motion):
    return dot(motion, coupling.reshape(-1, coupling.shape[-1]), (1, 1))


def adjoint_parts(coupling, load):
    return dot(load, jnp.concatenate([coupling[0], coupling[1]], axis=1), (1, 0))


def beside_turned(field, sign):
    turned = times_i(field.astype(F32), 0)
    return jnp.concatenate([field, (turned if sign > 0 else -turned).astype(BF16)], axis=1)


def forward_product(coupling, both):
    return dot(both, jnp.concatenate([coupling[0], coupling[1]], axis=1), (1, 1))


def adjoint_product(coupling, both):
    return dot(both, coupling.reshape(-1, coupling.shape[-1]), (1, 0))


def joined(parts, sign):
    half = parts.shape[1] // 2
    turned = times_i(parts[:, half:], 0)
    return parts[:, :half] + turned if sign > 0 else parts[:, :half] - turned


def map_of_blocks(map_ref, blocks):
    rows = map_ref.shape[0]
    panels = rows // blocks
    row = lax.broadcasted_iota(jnp.int32, (panels, rows), 0)
    column = lax.broadcasted_iota(jnp.int32, (panels, rows), 1)
    whole = map_ref[...]
    out = []
    for b in range(blocks):
        pick = (column == row * blocks + b).astype(F32).astype(BF16)
        out.append(dot(pick, whole, (1, 0)).astype(BF16))
    return out


def target(i, step, n):
    if step == 0:
        return i
    if step == 1:
        return i ^ 1
    if step == 2:
        return (((i + 1) ^ 1) + n - 1) % n
    return (i + step - 1) % n


def source(i, step, n):
    return target(i, step, n) if step < 3 else (i + n + 1 - step) % n


def places_along_gy(n):
    return list(range(n // 2, n)) + list(range(n // 2))


def all_steps(n):
    return [0, 1] + list(range(3, n)) + [2] if n > 2 else list(range(n))


def exchange(x, step):
    n = lax.axis_size("gx")
    return lax.ppermute(x, "gx", [(i, target(i, step, n)) for i in range(n)])


def exchange_sides(x, axis, step):
    sizes = lax.axis_size("gx"), lax.axis_size("gy")
    pairs = []
    for x_at in range(sizes[0]):
        for y_at in range(sizes[1]):
            there = [x_at, y_at]
            other = target(there[axis], step, sizes[axis])
            if axis == 0 or abs(other - there[axis]) == 1:
                there[axis] = other
            else:
                there[0] ^= 1
            pairs.append((x_at * sizes[1] + y_at, there[0] * sizes[1] + there[1]))
    return lax.ppermute(x, ("gx", "gy"), pairs)


def far(x):
    return pltpu.with_memory_space_constraint(x, pltpu.HBM)


def edges(rows, cols, spot):
    sides = []
    for axis in range(2):
        even = 1 - spot[axis] % 2
        for up in (even, 1 - even):
            if axis == 0:
                sides.append([(up * (rows - 1), y, up) for y in range(cols)])
            else:
                sides.append([(x, up * (cols - 1), 2 + up) for x in range(rows)])
    return sides


def here_on_mesh():
    return lax.axis_index("gx"), lax.axis_index("gy")


def fetch_edges(which, sides, cols, coupling_far, coupling, arrive, first):
    moves = []
    for o in which:
        for x, y, d in sides[o]:
            i = len(moves)
            moves.append(pltpu.make_async_copy(coupling_far.at[x * cols + y, d + 1], coupling.at[i], arrive.at[first + i]))
            moves[-1].start()
    return moves


def panels_kernel(rows, cols, early, late, joints_far, motion_far, load_far, coupling_far, map_far, *refs):
    motion_out, outs, refs = refs[0], refs[1 : 1 + len(early)], refs[1 + len(early) :]
    motion, load, spread, near_coupling, coupling, maps, joints, arrive = refs
    moves = [
        pltpu.make_async_copy(map_far, maps, arrive.at[0]),
        pltpu.make_async_copy(motion_far, motion, arrive.at[1]),
        pltpu.make_async_copy(load_far, load, arrive.at[2]),
        pltpu.make_async_copy(joints_far, joints, arrive.at[3]),
    ]
    for move in moves:
        move.start()
    sides = edges(rows, cols, here_on_mesh())
    more = fetch_edges(early, sides, cols, coupling_far, coupling, arrive, 4)
    later = fetch_edges(late, sides, cols, coupling_far, near_coupling, arrive, 4 + len(more))
    blocks, wide = motion.shape[:2]
    moves[0].wait()
    split = map_of_blocks(maps, blocks)
    spread[...] = jnp.concatenate(split, axis=1)
    moves[1].wait()
    motion_out[...] = sum(dot(split[b], motion[b], (1, 1)) for b in range(blocks)).astype(BF16)
    moves[2].wait()
    moves[3].wait()
    i = 0
    for o, out in zip(early, outs):
        for k, (x, y, d) in enumerate(sides[o]):
            out[pl.ds(k * wide, wide), :] = motion[x * cols + y]
            more[i].wait()
            matrix = coupling[i] * joints[x, y, d].astype(BF16)
            term = joined(adjoint_parts(matrix, load[x * cols + y]), -1)
            out[pl.ds((len(sides[o]) + k) * wide, wide), :] = term.astype(BF16)
            i += 1
    i = 0
    for o in late:
        for x, y, d in sides[o]:
            later[i].wait()
            near_coupling[i] = near_coupling[i] * joints[x, y, d].astype(BF16)
            i += 1


def edges_kernel(rows, cols, late, motion, load, maps, coupling, *refs):
    load_out, outs, (both,) = refs[0], refs[1 : 1 + len(late)], refs[1 + len(late) :]
    blocks, wide = motion.shape[:2]
    sides = edges(rows, cols, here_on_mesh())
    width = load.shape[2]
    split = [maps[:, b * width : (b + 1) * width] for b in range(blocks)]
    load_out[...] = sum(dot(split[b], load[b], (1, 1)) for b in range(blocks)).astype(BF16)
    for b in range(blocks):
        both[b] = beside_turned(load[b], -1)
    i = 0
    for o, out in zip(late, outs):
        for k, (x, y, d) in enumerate(sides[o]):
            out[pl.ds(k * wide, wide), :] = motion[x * cols + y]
            term = adjoint_product(coupling[i], both[x * cols + y])
            out[pl.ds((len(sides[o]) + k) * wide, wide), :] = term.astype(BF16)
            i += 1


def pressure_kernel(n_gx, hydro_ref, load_panels, *refs):
    pieces, (out_far, gathered, out, leave) = refs[:n_gx], refs[n_gx:]
    me = lax.axis_index("gx")
    panels, wide = load_panels.shape
    for step, piece in zip(all_steps(n_gx), pieces):
        start = pl.multiple_of(source(me, step, n_gx) * panels, panels)
        gathered[0, pl.ds(start, panels), :] = piece[...]
        gathered[1, pl.ds(start, panels), :] = times_i(piece[...].astype(F32), 1).astype(BF16)
    fields = gathered[...].reshape(-1, wide)
    tiles = out.shape[0]
    places, half = places_along_gy(tiles), tiles // 2
    moves = []
    for i in range(2):
        here = pl.ds(i * half, half)
        tops = [places[k] * panels for k in range(i * half, (i + 1) * half)]
        hydro = jnp.concatenate(
            [jnp.concatenate([hydro_ref[part, pl.ds(top, panels), :] for part in range(2)], axis=1) for top in tops], axis=0
        )
        out[here, :panels, :] = dot(hydro, fields, (1, 0)).astype(BF16).reshape(-1, panels, wide)
        out[here, panels:, :] = jnp.broadcast_to(load_panels[...], (half, panels, wide))
        moves.append(pltpu.make_async_copy(out.at[here], out_far.at[here], leave.at[i]))
        moves[-1].start()
    for move in moves:
        move.wait()


def reaction_kernel(n_gx, hydro_ref, arrived, *refs):
    outs, (reacted,) = refs[:n_gx], refs[n_gx:]
    me = lax.axis_index("gx")
    panels = outs[0].shape[0]
    hydro = hydro_ref[...]
    places = places_along_gy(arrived.shape[0])
    loads = jnp.concatenate([arrived[places.index(j), panels:, :] for j in range(len(places))], axis=0)
    real = dot(hydro[0], loads, (0, 0))
    imag = dot(hydro[1], loads, (0, 0))
    reacted[...] = real - times_i(imag, 1)
    for step in range(n_gx):
        start = pl.multiple_of(target(me, step, n_gx) * panels, panels)
        outs[step][...] = reacted[pl.ds(start, panels), :]


def add_side(side, valid, received, couplings, residual, multiplier):
    wide = residual.shape[1]
    for k, (b, x, y, d) in enumerate(side):
        motion = received[pl.ds(k * wide, wide), :]
        residual[b] += joined(forward_parts(couplings(k, x, y, d), motion), 1)
        terms = received[pl.ds((len(side) + k) * wide, wide), :]
        multiplier[b] += valid * terms.astype(F32)


def placed(cols, sides):
    return [[(x * cols + y, x, y, d) for x, y, d in side] for side in sides]


def beyond(spot, sizes, o):
    n, me = sizes[o // 2], spot[o // 2]
    other = target(me, 1 + o % 2, n)
    return (abs(me - other) <= 1).astype(F32) if n > 2 else F32(1 - o % 2)


def interior_kernel(rows, cols, sizes, early, late, joints_far, motion_far, load_far, excitation_far, *refs):
    coupling_far, received, refs = refs[0], refs[1 : 1 + len(early)], refs[1 + len(early) :]
    residual_out, multiplier_out, own_far, outer, motion, load, excitation, coupling, own, joints, arrive, leave = refs
    blocks, spot = rows * cols, here_on_mesh()
    moves = [
        pltpu.make_async_copy(motion_far, motion, arrive.at[0]),
        pltpu.make_async_copy(load_far, load, arrive.at[1]),
    ]
    for b in range(blocks):
        moves.append(pltpu.make_async_copy(coupling_far.at[b], coupling.at[b], arrive.at[2 + b]))
    moves.append(pltpu.make_async_copy(excitation_far, excitation, arrive.at[2 + blocks]))
    moves.append(pltpu.make_async_copy(joints_far, joints, arrive.at[3 + blocks]))
    for move in moves:
        move.start()
    sides = edges(rows, cols, spot)
    later = fetch_edges(late, sides, cols, coupling_far, outer, arrive, 4 + blocks)
    moves[0].wait()
    moving = [beside_turned(motion[b], 1) for b in range(blocks)]
    moves[1].wait()
    loads = [beside_turned(load[b], -1) for b in range(blocks)]
    sent = []
    for b in range(blocks):
        moves[2 + b].wait()
        own[b] = forward_product(coupling[b, 0], moving[b])
        sent.append(pltpu.make_async_copy(own.at[b], own_far.at[b], leave.at[b]))
        sent[-1].start()
    moves[2 + blocks].wait()
    moves[3 + blocks].wait()
    for x in range(rows):
        for y in range(cols):
            b = x * cols + y
            forward, adjoint = [], [(loads[b], coupling[b, 0])]
            for d in range(4):
                nx, ny = x + OFFSETS[d][0], y + OFFSETS[d][1]
                if 0 <= nx < rows and 0 <= ny < cols:
                    n = nx * cols + ny
                    forward.append((moving[n], coupling[b, d + 1] * joints[x, y, d].astype(BF16)))
                    adjoint.append((loads[n], coupling[n, (d ^ 1) + 1] * joints[nx, ny, d ^ 1].astype(BF16)))
            residual = own[b] - excitation[b].astype(F32)
            if forward:
                fields = jnp.concatenate([f for f, _ in forward], axis=1)
                matrix = jnp.concatenate([c[part] for _, c in forward for part in range(2)], axis=1)
                residual = residual + dot(fields, matrix, (1, 1))
            residual_out[b] = residual
            fields = jnp.concatenate([f for f, _ in adjoint], axis=1)
            matrix = jnp.concatenate([c[part] for _, c in adjoint for part in range(2)], axis=0)
            multiplier_out[b] = dot(fields, matrix, (1, 0))
    for o, ref in zip(early, received):
        valid = beyond(spot, sizes, o)

        def linked(k, x, y, d, valid=valid):
            return coupling[x * cols + y, d + 1] * (valid * joints[x, y, d].astype(F32)).astype(BF16)

        add_side(placed(cols, sides)[o], valid, ref, linked, residual_out, multiplier_out)
    i = 0
    for o in late:
        valid = beyond(spot, sizes, o)
        for x, y, d in sides[o]:
            later[i].wait()
            outer[i] = outer[i] * (valid * joints[x, y, d].astype(F32)).astype(BF16)
            i += 1
    for move in sent:
        move.wait()


def boundary_kernel(rows, cols, sizes, lift, which, maps, coupling, residual, multiplier, arrived, *refs):
    received, (residual_out, multiplier_out) = refs[: len(which)], refs[len(which) :]
    blocks, unknowns, spot = rows * cols, residual.shape[2], here_on_mesh()
    panels = maps.shape[0]
    pressure = jnp.sum(arrived[:, :panels, :].astype(F32), axis=0).astype(BF16)
    forces = lift * dot(pressure, maps[...], (0, 0))
    for b in range(blocks):
        residual_out[b] = residual[b] + forces[:, b * unknowns : (b + 1) * unknowns]
        multiplier_out[b] = multiplier[b]
    sides, first = placed(cols, edges(rows, cols, spot)), 0
    for o, ref in zip(which, received):
        at = first
        add_side(sides[o], beyond(spot, sizes, o), ref, lambda k, x, y, d: coupling[at + k], residual_out, multiplier_out)
        first += len(sides[o])


def final_kernel(rows, cols, lift, maps, residual, multiplier, own, *refs):
    reactions, (residual_out, multiplier_out, sensitivity_out, full, sensitivity, leave) = refs[:-6], refs[-6:]
    blocks = rows * cols
    unknowns = own.shape[2]
    sent = [pltpu.make_async_copy(residual, residual_out, leave.at[blocks + 1])]
    sent[0].start()
    reaction = sum(r[...].astype(F32) for r in reactions).astype(BF16)
    scale = 1.0 / math.sqrt(own.shape[1] // 2 * unknowns)
    forces = lift * dot(reaction, maps[...], (0, 0))
    sums = []
    for b in range(blocks):
        value = multiplier[b] + forces[:, b * unknowns : (b + 1) * unknowns]
        full[b] = value
        sent.append(pltpu.make_async_copy(full.at[b], multiplier_out.at[b], leave.at[b]))
        sent[-1].start()
        sums.append(jnp.sum((value * own[b]).reshape(-1, 8, unknowns), axis=0))
    for b in range(blocks):
        sensitivity[b // cols, b % cols] = jnp.sum(sums[b]) * scale
    sent.append(pltpu.make_async_copy(sensitivity, sensitivity_out, leave.at[blocks]))
    sent[-1].start()
    for move in sent:
        move.wait()


def cost(flops, bytes_accessed):
    return pl.CostEstimate(flops=int(flops), bytes_accessed=int(bytes_accessed), transcendentals=0)


def shaped(dtype, *shape):
    return jax.ShapeDtypeStruct(shape, dtype)


def params(mebibytes):
    return pltpu.CompilerParams(vmem_limit_bytes=mebibytes * 1024 * 1024)


DMA = pltpu.SemaphoreType.DMA


def on_device(plate_motion, adjoint_load, excitation, coupling, joints, hydro, panel_map):
    rows, cols, cases, _, unknowns = plate_motion.shape
    panels = panel_map.shape[0]
    blocks, wide = rows * cols, 2 * cases
    n_gx, n_gy = lax.axis_size("gx"), lax.axis_size("gy")
    motion = plate_motion.reshape(blocks, wide, unknowns)
    load = adjoint_load.reshape(blocks, wide, unknowns)
    force = excitation.reshape(blocks, wide, unknowns)
    coupling = coupling.reshape(blocks, 5, 2, unknowns, unknowns)
    panel_map = panel_map.reshape(panels * blocks, unknowns)
    lift = math.sqrt(blocks * unknowns / panels)
    block_flops = 2 * wide * unknowns * unknowns * 2
    field = (blocks, wide, unknowns)

    counts = [cols, cols, rows, rows]
    early, late = (3,), (0, 1, 2)
    few, many = sum(counts[o] for o in early), sum(counts[o] for o in late)
    pair = (2, unknowns, unknowns)
    motion_panels, *payloads, near_motion, near_load, maps, near_coupling = pl.pallas_call(
        functools.partial(panels_kernel, rows, cols, early, late),
        name="panels",
        out_shape=[pltpu.VMEM((panels, wide), BF16)]
        + [pltpu.VMEM((2 * counts[o] * wide, unknowns), BF16) for o in early]
        + [pltpu.VMEM(field, BF16)] * 2
        + [pltpu.VMEM((panels, blocks * unknowns), BF16), pltpu.VMEM((many,) + pair, BF16)],
        in_specs=[FAR] * 5,
        out_specs=[WHOLE] * (5 + len(early)),
        scratch_shapes=[
            pltpu.VMEM((few,) + pair, BF16),
            pltpu.VMEM(panel_map.shape, BF16),
            pltpu.SMEM(joints.shape, jnp.int32),
            DMA((4 + few + many,)),
        ],
        compiler_params=params(16),
        cost_estimate=cost(4 * blocks * wide * unknowns * panels, 4 * blocks * wide * unknowns),
    )(far(joints), far(motion), far(load), far(coupling), far(panel_map))
    pieces = [motion_panels] + [exchange(motion_panels, step) for step in all_steps(n_gx)[1:]]
    fourth = exchange_sides(payloads[0], 1, 2)

    load_panels, *payloads = pl.pallas_call(
        functools.partial(edges_kernel, rows, cols, late),
        name="edges",
        out_shape=[pltpu.VMEM((panels, wide), BF16)]
        + [pltpu.VMEM((2 * counts[o] * wide, unknowns), BF16) for o in late],
        in_specs=[WHOLE] * 4,
        out_specs=[WHOLE] * (1 + len(late)),
        scratch_shapes=[pltpu.VMEM((blocks, wide, 2 * unknowns), BF16)],
        compiler_params=params(16),
        cost_estimate=cost(30 * many * block_flops, 4 * blocks * wide * unknowns + 12 * blocks * unknowns**2),
    )(near_motion, near_load, maps, near_coupling)
    (*payloads, load_panels) = lax.optimization_barrier((*payloads, load_panels))
    parts = pl.pallas_call(
        functools.partial(pressure_kernel, n_gx),
        name="pressure",
        out_shape=pltpu.HBM((n_gy, 2 * panels, wide), BF16),
        in_specs=[WHOLE] * (2 + n_gx),
        out_specs=FAR,
        scratch_shapes=[pltpu.VMEM((2, n_gx * panels, wide), BF16), pltpu.VMEM((n_gy, 2 * panels, wide), BF16), DMA((2,))],
        compiler_params=params(16),
        cost_estimate=cost(60 * hydro.size * wide, 2 * hydro.size),
    )(hydro, load_panels, *pieces)
    arrived = lax.all_to_all(parts, "gy", 0, 0, axis_index_groups=[places_along_gy(n_gy)], tiled=True)
    (*payloads, fourth) = lax.optimization_barrier((*payloads, fourth))
    third = exchange_sides(payloads[2], 1, 1)
    second = exchange_sides(payloads[1], 0, 2)
    first = exchange_sides(payloads[0], 0, 1)

    residual, multiplier, own, outer = pl.pallas_call(
        functools.partial(interior_kernel, rows, cols, (n_gx, n_gy), early, late),
        name="interior",
        out_shape=[pltpu.VMEM(field, F32)] * 2
        + [pltpu.HBM(field, F32), pltpu.VMEM((many,) + pair, BF16)],
        in_specs=[FAR] * 5 + [WHOLE] * len(early),
        out_specs=[WHOLE] * 2 + [FAR, WHOLE],
        scratch_shapes=[pltpu.VMEM(field, BF16)] * 3
        + [
            pltpu.VMEM(coupling.shape, BF16),
            pltpu.VMEM(field, F32),
            pltpu.SMEM(joints.shape, jnp.int32),
            DMA((4 + blocks + many,)),
            DMA((blocks,)),
        ],
        compiler_params=params(16),
        cost_estimate=cost(6 * blocks * block_flops, 20 * blocks * unknowns**2 + 18 * blocks * wide * unknowns),
    )(far(joints), far(motion), far(load), far(force), far(coupling), fourth)
    arrived, residual, multiplier, own, outer = lax.optimization_barrier((arrived, residual, multiplier, own, outer))

    reaction_parts = pl.pallas_call(
        functools.partial(reaction_kernel, n_gx),
        name="reaction",
        out_shape=[pltpu.VMEM((panels, wide), F32)] * n_gx,
        in_specs=[WHOLE] * 2,
        out_specs=[WHOLE] * n_gx,
        scratch_shapes=[pltpu.VMEM((n_gx * panels, wide), F32)],
        compiler_params=params(16),
        cost_estimate=cost(2 * hydro.size * wide, 2 * hydro.size),
    )(hydro, arrived)
    reactions = [exchange(reaction_parts[step], step) for step in [*range(2, n_gx), 1]] + [reaction_parts[0]]

    residual, multiplier = pl.pallas_call(
        functools.partial(boundary_kernel, rows, cols, (n_gx, n_gy), lift, late),
        name="boundary",
        out_shape=[pltpu.VMEM(field, F32)] * 2,
        in_specs=[WHOLE] * (5 + len(late)),
        out_specs=[WHOLE] * 2,
        compiler_params=params(16),
        cost_estimate=cost(4 * blocks * block_flops, 10 * blocks * unknowns**2 + 18 * blocks * wide * unknowns),
    )(maps, outer, residual, multiplier, arrived, first, second, third)

    residual, multiplier, sensitivity = pl.pallas_call(
        functools.partial(final_kernel, rows, cols, lift),
        name="final",
        out_shape=[pltpu.HBM(field, F32), pltpu.HBM(field, F32), pltpu.HBM((rows, cols), F32)],
        in_specs=[WHOLE] * (4 + n_gx),
        out_specs=[FAR] * 3,
        scratch_shapes=[pltpu.VMEM(field, F32), pltpu.SMEM((rows, cols), F32), DMA((blocks + 2,))],
        compiler_params=params(16),
        cost_estimate=cost(4 * blocks * wide * unknowns * panels, 20 * blocks * wide * unknowns),
    )(maps, residual, multiplier, own, *reactions)
    shape = plate_motion.shape
    return residual.reshape(shape), multiplier.reshape(shape), sensitivity


def solution(mesh):
    field = P("gx", "gy", None, None, None)
    placed = (
        field,
        field,
        field,
        P("gx", "gy", None, None, None, None),
        P("gx", "gy", None),
        P(None, "gx", "gy"),
        P(("gx", "gy"), None, None, None),
    )
    return jax.shard_map(on_device, mesh=mesh, in_specs=placed, out_specs=(field, field, P("gx", "gy")), check_vma=False)
```

```python
import functools
import math

import jax
import jax.numpy as jnp
from jax import lax
from jax.experimental import pallas as pl
from jax.experimental.pallas import tpu as pltpu
from jax.sharding import PartitionSpec as P


F32 = jnp.float32
BF16 = jnp.bfloat16
OFFSETS = ((-1, 0), (1, 0), (0, -1), (0, 1))
WHOLE = pl.BlockSpec(memory_space=pltpu.VMEM)
FAR = pl.BlockSpec(memory_space=pltpu.HBM)


def dot(a, b, over):
    return lax.dot_general(a, b, ((over[:1], over[1:]), ((), ())), preferred_element_type=F32)


def times_i(field, axis):
    shape = field.shape
    if axis == 0:
        field, axis = field.reshape(-1, 8, shape[1]), 1
        place = lax.broadcasted_iota(jnp.int32, (1, 8, shape[1]), 1)
    else:
        place = lax.broadcasted_iota(jnp.int32, (1, shape[1]), 1)
    size = field.shape[axis]
    after = pltpu.roll(field, size - 1, axis)
    before = pltpu.roll(field, 1, axis)
    return jnp.where((place & 1) == 0, -after, before).reshape(shape)


def forward_parts(coupling, motion):
    return dot(motion, coupling.reshape(-1, coupling.shape[-1]), (1, 1))


def adjoint_parts(coupling, load):
    return dot(load, jnp.concatenate([coupling[0], coupling[1]], axis=1), (1, 0))


def beside_turned(field, sign):
    turned = times_i(field.astype(F32), 0)
    return jnp.concatenate([field, (turned if sign > 0 else -turned).astype(BF16)], axis=1)


def forward_product(coupling, both):
    return dot(both, jnp.concatenate([coupling[0], coupling[1]], axis=1), (1, 1))


def adjoint_product(coupling, both):
    return dot(both, coupling.reshape(-1, coupling.shape[-1]), (1, 0))


def joined(parts, sign):
    half = parts.shape[1] // 2
    turned = times_i(parts[:, half:], 0)
    return parts[:, :half] + turned if sign > 0 else parts[:, :half] - turned


def map_of_blocks(map_ref, blocks):
    rows = map_ref.shape[0]
    panels = rows // blocks
    row = lax.broadcasted_iota(jnp.int32, (panels, rows), 0)
    column = lax.broadcasted_iota(jnp.int32, (panels, rows), 1)
    whole = map_ref[...]
    out = []
    for b in range(blocks):
        pick = (column == row * blocks + b).astype(F32).astype(BF16)
        out.append(dot(pick, whole, (1, 0)).astype(BF16))
    return out


def target(i, step, n):
    if step == 0:
        return i
    if step == 1:
        return i ^ 1
    if step == 2:
        return (((i + 1) ^ 1) + n - 1) % n
    return (i + step - 1) % n


def source(i, step, n):
    return target(i, step, n) if step < 3 else (i + n + 1 - step) % n


def places_along_gy(n):
    return list(range(n // 2, n)) + list(range(n // 2))


def all_steps(n):
    return [0, 1] + list(range(3, n)) + [2] if n > 2 else list(range(n))


def exchange(x, step):
    n = lax.axis_size("gx")
    return lax.ppermute(x, "gx", [(i, target(i, step, n)) for i in range(n)])


def exchange_sides(x, axis, step):
    sizes = lax.axis_size("gx"), lax.axis_size("gy")
    pairs = []
    for x_at in range(sizes[0]):
        for y_at in range(sizes[1]):
            there = [x_at, y_at]
            other = target(there[axis], step, sizes[axis])
            if axis == 0 or abs(other - there[axis]) == 1:
                there[axis] = other
            else:
                there[0] ^= 1
            pairs.append((x_at * sizes[1] + y_at, there[0] * sizes[1] + there[1]))
    return lax.ppermute(x, ("gx", "gy"), pairs)


def far(x):
    return pltpu.with_memory_space_constraint(x, pltpu.HBM)


def edges(rows, cols, spot):
    sides = []
    for axis in range(2):
        even = 1 - spot[axis] % 2
        for up in (even, 1 - even):
            if axis == 0:
                sides.append([(up * (rows - 1), y, up) for y in range(cols)])
            else:
                sides.append([(x, up * (cols - 1), 2 + up) for x in range(rows)])
    return sides


def here_on_mesh():
    return lax.axis_index("gx"), lax.axis_index("gy")


def fetch_edges(which, sides, cols, coupling_far, coupling, arrive, first):
    moves = []
    for o in which:
        for x, y, d in sides[o]:
            i = len(moves)
            moves.append(pltpu.make_async_copy(coupling_far.at[x * cols + y, d + 1], coupling.at[i], arrive.at[first + i]))
            moves[-1].start()
    return moves


def panels_kernel(rows, cols, early, late, joints_far, motion_far, load_far, coupling_far, map_far, *refs):
    motion_out, outs, refs = refs[0], refs[1 : 1 + len(early)], refs[1 + len(early) :]
    motion, load, spread, near_coupling, coupling, maps, joints, arrive = refs
    moves = [
        pltpu.make_async_copy(map_far, maps, arrive.at[0]),
        pltpu.make_async_copy(motion_far, motion, arrive.at[1]),
        pltpu.make_async_copy(load_far, load, arrive.at[2]),
        pltpu.make_async_copy(joints_far, joints, arrive.at[3]),
    ]
    for move in moves:
        move.start()
    sides = edges(rows, cols, here_on_mesh())
    more = fetch_edges(early, sides, cols, coupling_far, coupling, arrive, 4)
    later = fetch_edges(late, sides, cols, coupling_far, near_coupling, arrive, 4 + len(more))
    blocks, wide = motion.shape[:2]
    moves[0].wait()
    split = map_of_blocks(maps, blocks)
    spread[...] = jnp.concatenate(split, axis=1)
    moves[1].wait()
    motion_out[...] = sum(dot(split[b], motion[b], (1, 1)) for b in range(blocks)).astype(BF16)
    moves[2].wait()
    moves[3].wait()
    i = 0
    for o, out in zip(early, outs):
        for k, (x, y, d) in enumerate(sides[o]):
            out[pl.ds(k * wide, wide), :] = motion[x * cols + y]
            more[i].wait()
            matrix = coupling[i] * joints[x, y, d].astype(BF16)
            term = joined(adjoint_parts(matrix, load[x * cols + y]), -1)
            out[pl.ds((len(sides[o]) + k) * wide, wide), :] = term.astype(BF16)
            i += 1
    i = 0
    for o in late:
        for x, y, d in sides[o]:
            later[i].wait()
            near_coupling[i] = near_coupling[i] * joints[x, y, d].astype(BF16)
            i += 1


def edges_kernel(rows, cols, late, motion, load, maps, coupling, *refs):
    load_out, outs, (both,) = refs[0], refs[1 : 1 + len(late)], refs[1 + len(late) :]
    blocks, wide = motion.shape[:2]
    sides = edges(rows, cols, here_on_mesh())
    width = load.shape[2]
    split = [maps[:, b * width : (b + 1) * width] for b in range(blocks)]
    load_out[...] = sum(dot(split[b], load[b], (1, 1)) for b in range(blocks)).astype(BF16)
    for b in range(blocks):
        both[b] = beside_turned(load[b], -1)
    i = 0
    for o, out in zip(late, outs):
        for k, (x, y, d) in enumerate(sides[o]):
            out[pl.ds(k * wide, wide), :] = motion[x * cols + y]
            term = adjoint_product(coupling[i], both[x * cols + y])
            out[pl.ds((len(sides[o]) + k) * wide, wide), :] = term.astype(BF16)
            i += 1


def pressure_kernel(n_gx, hydro_ref, load_panels, *refs):
    pieces, (out_far, gathered, out, leave) = refs[:n_gx], refs[n_gx:]
    me = lax.axis_index("gx")
    panels, wide = load_panels.shape
    for step, piece in zip(all_steps(n_gx), pieces):
        start = pl.multiple_of(source(me, step, n_gx) * panels, panels)
        gathered[0, pl.ds(start, panels), :] = piece[...]
        gathered[1, pl.ds(start, panels), :] = times_i(piece[...].astype(F32), 1).astype(BF16)
    fields = gathered[...].reshape(-1, wide)
    tiles = out.shape[0]
    places, half = places_along_gy(tiles), tiles // 2
    moves = []
    for i in range(2):
        here = pl.ds(i * half, half)
        tops = [places[k] * panels for k in range(i * half, (i + 1) * half)]
        hydro = jnp.concatenate(
            [jnp.concatenate([hydro_ref[part, pl.ds(top, panels), :] for part in range(2)], axis=1) for top in tops], axis=0
        )
        out[here, :panels, :] = dot(hydro, fields, (1, 0)).astype(BF16).reshape(-1, panels, wide)
        out[here, panels:, :] = jnp.broadcast_to(load_panels[...], (half, panels, wide))
        moves.append(pltpu.make_async_copy(out.at[here], out_far.at[here], leave.at[i]))
        moves[-1].start()
    for move in moves:
        move.wait()


def reaction_kernel(n_gx, hydro_ref, arrived, *refs):
    outs, (reacted,) = refs[:n_gx], refs[n_gx:]
    me = lax.axis_index("gx")
    panels = outs[0].shape[0]
    hydro = hydro_ref[...]
    places = places_along_gy(arrived.shape[0])
    loads = jnp.concatenate([arrived[places.index(j), panels:, :] for j in range(len(places))], axis=0)
    real = dot(hydro[0], loads, (0, 0))
    imag = dot(hydro[1], loads, (0, 0))
    reacted[...] = real - times_i(imag, 1)
    for step in range(n_gx):
        start = pl.multiple_of(target(me, step, n_gx) * panels, panels)
        outs[step][...] = reacted[pl.ds(start, panels), :]


def add_side(side, valid, received, couplings, residual, multiplier):
    wide = residual.shape[1]
    for k, (b, x, y, d) in enumerate(side):
        motion = received[pl.ds(k * wide, wide), :]
        residual[b] += joined(forward_parts(couplings(k, x, y, d), motion), 1)
        terms = received[pl.ds((len(side) + k) * wide, wide), :]
        multiplier[b] += valid * terms.astype(F32)


def placed(cols, sides):
    return [[(x * cols + y, x, y, d) for x, y, d in side] for side in sides]


def beyond(spot, sizes, o):
    n, me = sizes[o // 2], spot[o // 2]
    other = target(me, 1 + o % 2, n)
    return (abs(me - other) <= 1).astype(F32) if n > 2 else F32(1 - o % 2)


def interior_kernel(rows, cols, sizes, early, late, joints_far, motion_far, load_far, excitation_far, *refs):
    coupling_far, received, refs = refs[0], refs[1 : 1 + len(early)], refs[1 + len(early) :]
    residual_out, multiplier_out, own_far, outer, motion, load, excitation, coupling, own, joints, arrive, leave = refs
    blocks, spot = rows * cols, here_on_mesh()
    moves = [
        pltpu.make_async_copy(motion_far, motion, arrive.at[0]),
        pltpu.make_async_copy(load_far, load, arrive.at[1]),
    ]
    for b in range(blocks):
        moves.append(pltpu.make_async_copy(coupling_far.at[b], coupling.at[b], arrive.at[2 + b]))
    moves.append(pltpu.make_async_copy(excitation_far, excitation, arrive.at[2 + blocks]))
    moves.append(pltpu.make_async_copy(joints_far, joints, arrive.at[3 + blocks]))
    for move in moves:
        move.start()
    sides = edges(rows, cols, spot)
    later = fetch_edges(late, sides, cols, coupling_far, outer, arrive, 4 + blocks)
    moves[0].wait()
    moving = [beside_turned(motion[b], 1) for b in range(blocks)]
    moves[1].wait()
    loads = [beside_turned(load[b], -1) for b in range(blocks)]
    sent = []
    for b in range(blocks):
        moves[2 + b].wait()
        own[b] = forward_product(coupling[b, 0], moving[b])
        sent.append(pltpu.make_async_copy(own.at[b], own_far.at[b], leave.at[b]))
        sent[-1].start()
    moves[2 + blocks].wait()
    moves[3 + blocks].wait()
    for x in range(rows):
        for y in range(cols):
            b = x * cols + y
            forward, adjoint = [], [(loads[b], coupling[b, 0])]
            for d in range(4):
                nx, ny = x + OFFSETS[d][0], y + OFFSETS[d][1]
                if 0 <= nx < rows and 0 <= ny < cols:
                    n = nx * cols + ny
                    forward.append((moving[n], coupling[b, d + 1] * joints[x, y, d].astype(BF16)))
                    adjoint.append((loads[n], coupling[n, (d ^ 1) + 1] * joints[nx, ny, d ^ 1].astype(BF16)))
            residual = own[b] - excitation[b].astype(F32)
            if forward:
                fields = jnp.concatenate([f for f, _ in forward], axis=1)
                matrix = jnp.concatenate([c[part] for _, c in forward for part in range(2)], axis=1)
                residual = residual + dot(fields, matrix, (1, 1))
            residual_out[b] = residual
            fields = jnp.concatenate([f for f, _ in adjoint], axis=1)
            matrix = jnp.concatenate([c[part] for _, c in adjoint for part in range(2)], axis=0)
            multiplier_out[b] = dot(fields, matrix, (1, 0))
    for o, ref in zip(early, received):
        valid = beyond(spot, sizes, o)

        def linked(k, x, y, d, valid=valid):
            return coupling[x * cols + y, d + 1] * (valid * joints[x, y, d].astype(F32)).astype(BF16)

        add_side(placed(cols, sides)[o], valid, ref, linked, residual_out, multiplier_out)
    i = 0
    for o in late:
        valid = beyond(spot, sizes, o)
        for x, y, d in sides[o]:
            later[i].wait()
            outer[i] = outer[i] * (valid * joints[x, y, d].astype(F32)).astype(BF16)
            i += 1
    for move in sent:
        move.wait()


def boundary_kernel(rows, cols, sizes, lift, which, maps, coupling, residual, multiplier, arrived, *refs):
    received, (residual_out, multiplier_out) = refs[: len(which)], refs[len(which) :]
    blocks, unknowns, spot = rows * cols, residual.shape[2], here_on_mesh()
    panels = maps.shape[0]
    pressure = jnp.sum(arrived[:, :panels, :].astype(F32), axis=0).astype(BF16)
    forces = lift * dot(pressure, maps[...], (0, 0))
    for b in range(blocks):
        residual_out[b] = residual[b] + forces[:, b * unknowns : (b + 1) * unknowns]
        multiplier_out[b] = multiplier[b]
    sides, first = placed(cols, edges(rows, cols, spot)), 0
    for o, ref in zip(which, received):
        at = first
        add_side(sides[o], beyond(spot, sizes, o), ref, lambda k, x, y, d: coupling[at + k], residual_out, multiplier_out)
        first += len(sides[o])


def final_kernel(rows, cols, lift, maps, residual, multiplier, own, *refs):
    reactions, (residual_out, multiplier_out, sensitivity_out, full, sensitivity, leave) = refs[:-6], refs[-6:]
    blocks = rows * cols
    unknowns = own.shape[2]
    sent = [pltpu.make_async_copy(residual, residual_out, leave.at[blocks + 1])]
    sent[0].start()
    reaction = sum(r[...].astype(F32) for r in reactions).astype(BF16)
    scale = 1.0 / math.sqrt(own.shape[1] // 2 * unknowns)
    forces = lift * dot(reaction, maps[...], (0, 0))
    sums = []
    for b in range(blocks):
        value = multiplier[b] + forces[:, b * unknowns : (b + 1) * unknowns]
        full[b] = value
        sent.append(pltpu.make_async_copy(full.at[b], multiplier_out.at[b], leave.at[b]))
        sent[-1].start()
        sums.append(jnp.sum((value * own[b]).reshape(-1, 8, unknowns), axis=0))
    for b in range(blocks):
        sensitivity[b // cols, b % cols] = jnp.sum(sums[b]) * scale
    sent.append(pltpu.make_async_copy(sensitivity, sensitivity_out, leave.at[blocks]))
    sent[-1].start()
    for move in sent:
        move.wait()


def cost(flops, bytes_accessed):
    return pl.CostEstimate(flops=int(flops), bytes_accessed=int(bytes_accessed), transcendentals=0)


def shaped(dtype, *shape):
    return jax.ShapeDtypeStruct(shape, dtype)


def params(mebibytes):
    return pltpu.CompilerParams(vmem_limit_bytes=mebibytes * 1024 * 1024)


DMA = pltpu.SemaphoreType.DMA


def on_device(plate_motion, adjoint_load, excitation, coupling, joints, hydro, panel_map):
    rows, cols, cases, _, unknowns = plate_motion.shape
    panels = panel_map.shape[0]
    blocks, wide = rows * cols, 2 * cases
    n_gx, n_gy = lax.axis_size("gx"), lax.axis_size("gy")
    motion = plate_motion.reshape(blocks, wide, unknowns)
    load = adjoint_load.reshape(blocks, wide, unknowns)
    force = excitation.reshape(blocks, wide, unknowns)
    coupling = coupling.reshape(blocks, 5, 2, unknowns, unknowns)
    panel_map = panel_map.reshape(panels * blocks, unknowns)
    lift = math.sqrt(blocks * unknowns / panels)
    block_flops = 2 * wide * unknowns * unknowns * 2
    field = (blocks, wide, unknowns)

    counts = [cols, cols, rows, rows]
    early, late = (3,), (0, 1, 2)
    few, many = sum(counts[o] for o in early), sum(counts[o] for o in late)
    pair = (2, unknowns, unknowns)
    motion_panels, *payloads, near_motion, near_load, maps, near_coupling = pl.pallas_call(
        functools.partial(panels_kernel, rows, cols, early, late),
        name="panels",
        out_shape=[pltpu.VMEM((panels, wide), BF16)]
        + [pltpu.VMEM((2 * counts[o] * wide, unknowns), BF16) for o in early]
        + [pltpu.VMEM(field, BF16)] * 2
        + [pltpu.VMEM((panels, blocks * unknowns), BF16), pltpu.VMEM((many,) + pair, BF16)],
        in_specs=[FAR] * 5,
        out_specs=[WHOLE] * (5 + len(early)),
        scratch_shapes=[
            pltpu.VMEM((few,) + pair, BF16),
            pltpu.VMEM(panel_map.shape, BF16),
            pltpu.SMEM(joints.shape, jnp.int32),
            DMA((4 + few + many,)),
        ],
        compiler_params=params(16),
        cost_estimate=cost(4 * blocks * wide * unknowns * panels, 4 * blocks * wide * unknowns),
    )(far(joints), far(motion), far(load), far(coupling), far(panel_map))
    pieces = [motion_panels] + [exchange(motion_panels, step) for step in all_steps(n_gx)[1:]]
    fourth = exchange_sides(payloads[0], 1, 2)

    load_panels, *payloads = pl.pallas_call(
        functools.partial(edges_kernel, rows, cols, late),
        name="edges",
        out_shape=[pltpu.VMEM((panels, wide), BF16)]
        + [pltpu.VMEM((2 * counts[o] * wide, unknowns), BF16) for o in late],
        in_specs=[WHOLE] * 4,
        out_specs=[WHOLE] * (1 + len(late)),
        scratch_shapes=[pltpu.VMEM((blocks, wide, 2 * unknowns), BF16)],
        compiler_params=params(16),
        cost_estimate=cost(30 * many * block_flops, 4 * blocks * wide * unknowns + 12 * blocks * unknowns**2),
    )(near_motion, near_load, maps, near_coupling)
    (*payloads, load_panels) = lax.optimization_barrier((*payloads, load_panels))
    parts = pl.pallas_call(
        functools.partial(pressure_kernel, n_gx),
        name="pressure",
        out_shape=pltpu.HBM((n_gy, 2 * panels, wide), BF16),
        in_specs=[WHOLE] * (2 + n_gx),
        out_specs=FAR,
        scratch_shapes=[pltpu.VMEM((2, n_gx * panels, wide), BF16), pltpu.VMEM((n_gy, 2 * panels, wide), BF16), DMA((2,))],
        compiler_params=params(16),
        cost_estimate=cost(60 * hydro.size * wide, 2 * hydro.size),
    )(hydro, load_panels, *pieces)
    arrived = lax.all_to_all(parts, "gy", 0, 0, axis_index_groups=[places_along_gy(n_gy)], tiled=True)
    payloads = list(payloads)
    payloads[0], fourth = lax.optimization_barrier((payloads[0], fourth))
    third = exchange_sides(payloads[2], 1, 1)
    second = exchange_sides(payloads[1], 0, 2)
    first = exchange_sides(payloads[0], 0, 1)

    residual, multiplier, own, outer = pl.pallas_call(
        functools.partial(interior_kernel, rows, cols, (n_gx, n_gy), early, late),
        name="interior",
        out_shape=[pltpu.VMEM(field, F32)] * 2
        + [pltpu.HBM(field, F32), pltpu.VMEM((many,) + pair, BF16)],
        in_specs=[FAR] * 5 + [WHOLE] * len(early),
        out_specs=[WHOLE] * 2 + [FAR, WHOLE],
        scratch_shapes=[pltpu.VMEM(field, BF16)] * 3
        + [
            pltpu.VMEM(coupling.shape, BF16),
            pltpu.VMEM(field, F32),
            pltpu.SMEM(joints.shape, jnp.int32),
            DMA((4 + blocks + many,)),
            DMA((blocks,)),
        ],
        compiler_params=params(16),
        cost_estimate=cost(6 * blocks * block_flops, 20 * blocks * unknowns**2 + 18 * blocks * wide * unknowns),
    )(far(joints), far(motion), far(load), far(force), far(coupling), fourth)
    arrived, residual, multiplier, own, outer = lax.optimization_barrier((arrived, residual, multiplier, own, outer))

    reaction_parts = pl.pallas_call(
        functools.partial(reaction_kernel, n_gx),
        name="reaction",
        out_shape=[pltpu.VMEM((panels, wide), F32)] * n_gx,
        in_specs=[WHOLE] * 2,
        out_specs=[WHOLE] * n_gx,
        scratch_shapes=[pltpu.VMEM((n_gx * panels, wide), F32)],
        compiler_params=params(16),
        cost_estimate=cost(2 * hydro.size * wide, 2 * hydro.size),
    )(hydro, arrived)
    reactions = [exchange(reaction_parts[step], step) for step in [*range(2, n_gx), 1]] + [reaction_parts[0]]

    residual, multiplier = pl.pallas_call(
        functools.partial(boundary_kernel, rows, cols, (n_gx, n_gy), lift, late),
        name="boundary",
        out_shape=[pltpu.VMEM(field, F32)] * 2,
        in_specs=[WHOLE] * (5 + len(late)),
        out_specs=[WHOLE] * 2,
        compiler_params=params(16),
        cost_estimate=cost(4 * blocks * block_flops, 10 * blocks * unknowns**2 + 18 * blocks * wide * unknowns),
    )(maps, outer, residual, multiplier, arrived, first, second, third)

    residual, multiplier, sensitivity = pl.pallas_call(
        functools.partial(final_kernel, rows, cols, lift),
        name="final",
        out_shape=[pltpu.HBM(field, F32), pltpu.HBM(field, F32), pltpu.HBM((rows, cols), F32)],
        in_specs=[WHOLE] * (4 + n_gx),
        out_specs=[FAR] * 3,
        scratch_shapes=[pltpu.VMEM(field, F32), pltpu.SMEM((rows, cols), F32), DMA((blocks + 2,))],
        compiler_params=params(16),
        cost_estimate=cost(4 * blocks * wide * unknowns * panels, 20 * blocks * wide * unknowns),
    )(maps, residual, multiplier, own, *reactions)
    shape = plate_motion.shape
    return residual.reshape(shape), multiplier.reshape(shape), sensitivity


def solution(mesh):
    field = P("gx", "gy", None, None, None)
    placed = (
        field,
        field,
        field,
        P("gx", "gy", None, None, None, None),
        P("gx", "gy", None),
        P(None, "gx", "gy"),
        P(("gx", "gy"), None, None, None),
    )
    return jax.shard_map(on_device, mesh=mesh, in_specs=placed, out_specs=(field, field, P("gx", "gy")), check_vma=False)
```
